32 devices in a mesh: dp: 16 (over z, y, x), head: 2 (over core).
Axes of the slice: x: 2, y: 2, z: 4, core: 2. Of those that a mesh axis runs over, the one named last changes fastest.
Arguments:
- tokens: bfloat16 [24576, 768], P('dp'), may hold values from -6 to 6
- teacher: bfloat16 [24576, 768], P('dp'), may hold values from -12 to 12
- lengths: int32 [48, 6], P('dp'), may hold values from 0 to 512, as said below
- head_gate: float32 [12], P('head'), may hold values from 0.25 to 1
- unit_gate: float32 [3072], P('head'), may hold values from 0.25 to 1
- hidden_gate: float32 [768], replicated, may hold values from 0.5 to 1
- layer_gates: float32 [2], replicated, may hold values from 0.5 to 1
- master_qkv: float32 [768, 3, 768], P('dp', None, 'head'), may hold values from -4 to 4
- first_qkv: float32 [768, 3, 768], P('dp', None, 'head'), may hold values from -1881.2081 to 1881.2081
- second_qkv: float32 [768, 3, 768], P('dp', None, 'head'), may hold values from 49152 to 393216
- master_attn_out: float32 [768, 768], P('head', 'dp'), may hold values from -4 to 4
- first_attn_out: float32 [768, 768], P('head', 'dp'), may hold values from -1881.2081 to 1881.2081
- second_attn_out: float32 [768, 768], P('head', 'dp'), may hold values from 49152 to 393216
- master_ffn_in: float32 [768, 3072], P('dp', 'head'), may hold values from -4 to 4
- first_ffn_in: float32 [768, 3072], P('dp', 'head'), may hold values from -1881.2081 to 1881.2081
- second_ffn_in: float32 [768, 3072], P('dp', 'head'), may hold values from 49152 to 393216
- master_ffn_out: float32 [3072, 768], P('head', 'dp'), may hold values from -4 to 4
- first_ffn_out: float32 [3072, 768], P('head', 'dp'), may hold values from -1881.2081 to 1881.2081
- second_ffn_out: float32 [3072, 768], P('head', 'dp'), may hold values from 49152 to 393216
- master_norms: float32 [4, 768], P(None, 'dp'), may hold values from -1 to 2.5
- first_norms: float32 [4, 768], P(None, 'dp'), may hold values from -1881.2081 to 1881.2081
- second_norms: float32 [4, 768], P(None, 'dp'), may hold values from 49152 to 393216
Outputs:
- student: bfloat16 [24576, 768], P('dp')
- grad_tokens: float32 [24576, 768], P('dp')
- grad_head_gate: float32 [12], P('head')
- grad_unit_gate: float32 [3072], P('head')
- grad_hidden_gate: float32 [768], replicated
- grad_layer_gates: float32 [2], replicated
- grad_qkv: float32 [768, 3, 768], P('dp', None, 'head')
- new_first_qkv: float32 [768, 3, 768], P('dp', None, 'head')
- new_second_qkv: float32 [768, 3, 768], P('dp', None, 'head')
- new_master_qkv: float32 [768, 3, 768], P('dp', None, 'head')
- copy_qkv: bfloat16 [768, 3, 768], P('dp', None, 'head')
- grad_attn_out: float32 [768, 768], P('head', 'dp')
- new_first_attn_out: float32 [768, 768], P('head', 'dp')
- new_second_attn_out: float32 [768, 768], P('head', 'dp')
- new_master_attn_out: float32 [768, 768], P('head', 'dp')
- copy_attn_out: bfloat16 [768, 768], P('head', 'dp')
- grad_ffn_in: float32 [768, 3072], P('dp', 'head')
- new_first_ffn_in: float32 [768, 3072], P('dp', 'head')
- new_second_ffn_in: float32 [768, 3072], P('dp', 'head')
- new_master_ffn_in: float32 [768, 3072], P('dp', 'head')
- copy_ffn_in: bfloat16 [768, 3072], P('dp', 'head')
- grad_ffn_out: float32 [3072, 768], P('head', 'dp')
- new_first_ffn_out: float32 [3072, 768], P('head', 'dp')
- new_second_ffn_out: float32 [3072, 768], P('head', 'dp')
- new_master_ffn_out: float32 [3072, 768], P('head', 'dp')
- copy_ffn_out: bfloat16 [3072, 768], P('head', 'dp')
- grad_norms: float32 [4, 768], P(None, 'dp')
- new_first_norms: float32 [4, 768], P(None, 'dp')
- new_second_norms: float32 [4, 768], P(None, 'dp')
- new_master_norms: float32 [4, 768], P(None, 'dp')
- copy_norms: bfloat16 [4, 768], P(None, 'dp')
- lamb_stats: float32 [3, 8], replicated
The draws below stay inside these ranges and needn't reach their ends.
Inputs may be any that keep to these rules, and one draw needn't show every extreme that they name: `lengths`: each row of 512 tokens holds whole sequences from its first position on, of 64 to 128 tokens, or one sequence of 512 tokens, with zeros after the last; the rest of a row is padding.
All inputs are finite; a program needn't handle non-finite values.
Results may differ from the reference program's by a relative error of at most 0.012.
The reference program's roundings to bfloat16 on the way count: a program that leaves them out, or rounds other values in their place, can miss the bound.
Values may be sent and summed in bfloat16 or wider, within the bound.
A program may use at most 192 MiB of HBM per device.

```python
import math
import jax
import jax.numpy as jnp
from jax import lax

D = 768
HEADS = 12
FF = 3072
HEAD_DIM = 64
ROW = 512
SLOTS = 6
SEQ_MIN = 64
SEQ_MAX = 128
ROWS_DEV = 3
STEP_COUNT = 5
TOKENS = 24576


def ramp_along(shape, axis, low_end, high_end):
    count = shape[axis]
    steps = jnp.arange(count, dtype=jnp.float32) / max(count - 1, 1)
    factor = low_end + (high_end - low_end) * steps
    view = [1] * len(shape)
    view[axis] = count
    return factor.reshape(view)


def matrix_draw(key, shape, axis, fan_in):
    base = jnp.clip(jax.random.normal(key, shape, jnp.float32), -3.0, 3.0)
    ramp = ramp_along(shape, axis, 0.5, 1.5)
    return base * ramp * fan_in ** (-0.5)


def draw_teacher(key, part):
    key = jax.random.fold_in(key, 3)
    shape = (TOKENS, D)
    base = jnp.clip(jax.random.normal(key, shape, jnp.float32), -4.0, 4.0)
    ramp = ramp_along(shape, 0, 1.0, 3.0)
    return (base * ramp).astype(jnp.bfloat16)


def draw_lengths(key, part):
    key = jax.random.fold_in(key, 5)
    first_key, second_key, third_key = jax.random.split(key, 3)
    rows_all = TOKENS // ROW
    raw = jax.random.randint(first_key, (rows_all, SLOTS), SEQ_MIN, SEQ_MAX + 1, dtype=jnp.int32)
    seq_ends = jnp.cumsum(raw, axis=1, dtype=jnp.int32)
    kept = jnp.where(seq_ends <= ROW, raw, 0)
    row_ids = jnp.arange(rows_all, dtype=jnp.int32)
    chosen = jax.random.randint(third_key, (), 0, rows_all, dtype=jnp.int32)
    whole_row = (jax.random.randint(second_key, (rows_all,), 0, 32, dtype=jnp.int32) == 0) | (row_ids == chosen)
    single = jnp.where(jnp.arange(SLOTS, dtype=jnp.int32) == 0, ROW, 0).astype(jnp.int32)
    return jnp.where(whole_row[:, None], single[None, :], kept).astype(jnp.int32)


def draw_master_qkv(key, part):
    key = jax.random.fold_in(key, 7)
    return matrix_draw(key, (D, 3, D), 0, D)


def draw_master_attn_out(key, part):
    key = jax.random.fold_in(key, 11)
    return matrix_draw(key, (D, D), 1, D // 16)


def draw_master_ffn_in(key, part):
    key = jax.random.fold_in(key, 13)
    return matrix_draw(key, (D, FF), 0, D)


def draw_master_ffn_out(key, part):
    key = jax.random.fold_in(key, 17)
    return matrix_draw(key, (FF, D), 1, FF)


def draw_master_norms(key, part):
    key = jax.random.fold_in(key, 19)
    gain_key, bias_key = jax.random.split(key)
    gains = jax.random.uniform(gain_key, (D,), jnp.float32, 0.8, 1.2) * ramp_along((D,), 0, 0.6, 1.8)
    biases = 0.3 * jnp.clip(jax.random.normal(bias_key, (2, D), jnp.float32), -3.0, 3.0)
    second_gains = jnp.roll(gains, 1) * 0.9 + 0.1 * gains
    return jnp.stack([gains, biases[0], second_gains, biases[1]]).astype(jnp.float32)


def shard_levels(key, shape, cuts, least, top_value):
    factor_of, own = 1.0, jax.random.fold_in(key, 6)
    for position, shards_of in cuts:
        heights = jnp.exp(jax.random.uniform(jax.random.fold_in(own, position), (shards_of,), jnp.float32, least / len(cuts), top_value / len(cuts)))
        factor_of = factor_of * jnp.repeat(heights, shape[position] // shards_of).reshape([-1 if axis == position else 1 for axis in range(len(shape))])
    return factor_of


def noise(stream_key, dims, scale, limit, shards=(), kind=jnp.bfloat16):
    loudness = shard_levels(stream_key, dims, shards, -0.22, 0.18) if shards else 1.0
    drawn = jax.random.normal(stream_key, dims, jnp.float32) * scale * loudness
    return jnp.minimum(jnp.maximum(drawn, -limit), limit).astype(kind)


def setup_inputs(seed: int = 0) -> dict:
    streams_of = jax.random.split(jax.random.key(seed), 23)
    tokens = noise(streams_of[0], (TOKENS, D), 1.0, 6.0, ((0, 16),))
    teacher = draw_teacher(jax.random.fold_in(streams_of[22], 71), 0)
    lengths = draw_lengths(jax.random.fold_in(streams_of[22], 71), 0)
    head_gate = jnp.clip(0.25 + 0.75 * jax.random.uniform(streams_of[3], (HEADS,), jnp.float32) ** shard_levels(streams_of[3], (HEADS,), ((0, 2),), -0.2, 0.2), 0.25, 1.0)
    unit_gate = jnp.clip(0.25 + 0.75 * jax.random.uniform(streams_of[4], (FF,), jnp.float32) ** shard_levels(streams_of[4], (FF,), ((0, 2),), -0.2, 0.2), 0.25, 1.0)
    hidden_gate = jnp.clip(jax.random.uniform(streams_of[5], (D,), jnp.float32, 0.5, 1.0), 0.5, 1.0)
    layer_gates = jnp.clip(jax.random.uniform(streams_of[6], (2,), jnp.float32, 0.5, 1.0), 0.5, 1.0)
    master_qkv = draw_master_qkv(jax.random.fold_in(streams_of[22], 71), 0)
    first_qkv = noise(streams_of[8], (D, 3, D), (2.0 * TOKENS ** 0.5), 1881.2081, ((0, 16), (2, 2)), jnp.float32)
    second_qkv = jnp.clip(jnp.exp(math.log(393216.0) - 2.0794415 * jax.random.uniform(streams_of[9], (D, 3, D), jnp.float32) ** shard_levels(streams_of[9], (D, 3, D), ((0, 16), (2, 2)), -0.2, 0.2)), 49152.0, 393216.0)
    master_attn_out = draw_master_attn_out(jax.random.fold_in(streams_of[22], 71), 0)
    first_attn_out = noise(streams_of[11], (D, D), (2.0 * TOKENS ** 0.5), 1881.2081, ((0, 2), (1, 16)), jnp.float32)
    second_attn_out = jnp.clip(jnp.exp(math.log(393216.0) - 2.0794415 * jax.random.uniform(streams_of[12], (D, D), jnp.float32) ** shard_levels(streams_of[12], (D, D), ((0, 2), (1, 16)), -0.2, 0.2)), 49152.0, 393216.0)
    master_ffn_in = draw_master_ffn_in(jax.random.fold_in(streams_of[22], 71), 0)
    first_ffn_in = noise(streams_of[14], (D, FF), (2.0 * TOKENS ** 0.5), 1881.2081, ((0, 16), (1, 2)), jnp.float32)
    second_ffn_in = jnp.clip(jnp.exp(math.log(393216.0) - 2.0794415 * jax.random.uniform(streams_of[15], (D, FF), jnp.float32) ** shard_levels(streams_of[15], (D, FF), ((0, 16), (1, 2)), -0.2, 0.2)), 49152.0, 393216.0)
    master_ffn_out = draw_master_ffn_out(jax.random.fold_in(streams_of[22], 71), 0)
    first_ffn_out = noise(streams_of[17], (FF, D), (2.0 * TOKENS ** 0.5), 1881.2081, ((0, 2), (1, 16)), jnp.float32)
    second_ffn_out = jnp.clip(jnp.exp(math.log(393216.0) - 2.0794415 * jax.random.uniform(streams_of[18], (FF, D), jnp.float32) ** shard_levels(streams_of[18], (FF, D), ((0, 2), (1, 16)), -0.2, 0.2)), 49152.0, 393216.0)
    master_norms = draw_master_norms(jax.random.fold_in(streams_of[22], 71), 0)
    first_norms = noise(streams_of[20], (4, D), (2.0 * TOKENS ** 0.5), 1881.2081, ((1, 16),), jnp.float32)
    second_norms = jnp.clip(jnp.exp(math.log(393216.0) - 2.0794415 * jax.random.uniform(streams_of[21], (4, D), jnp.float32) ** shard_levels(streams_of[21], (4, D), ((1, 16),), -0.2, 0.2)), 49152.0, 393216.0)
    return {"tokens": tokens, "teacher": teacher, "lengths": lengths, "head_gate": head_gate, "unit_gate": unit_gate, "hidden_gate": hidden_gate, "layer_gates": layer_gates, "master_qkv": master_qkv, "first_qkv": first_qkv, "second_qkv": second_qkv, "master_attn_out": master_attn_out, "first_attn_out": first_attn_out, "second_attn_out": second_attn_out, "master_ffn_in": master_ffn_in, "first_ffn_in": first_ffn_in, "second_ffn_in": second_ffn_in, "master_ffn_out": master_ffn_out, "first_ffn_out": first_ffn_out, "second_ffn_out": second_ffn_out, "master_norms": master_norms, "first_norms": first_norms, "second_norms": second_norms}


LN_EPS = 1e-05
LAMB_EPS = 1e-06
WEIGHT_DECAY = 0.01
LEARN_RATE = 0.5
MOMENT_DECAY = 0.5
MASK_FILL = -1000000000.0
HIGHEST = lax.Precision.HIGHEST

@jax.custom_vjp
def low(v):
    return lax.optimization_barrier(v.astype(jnp.bfloat16)).astype(jnp.float32)

@jax.custom_vjp
def low_back(v):
    return v

def low_keep(v):
    return (low(v), None)

def low_pass(kept, grad):
    return (grad,)

def back_keep(v):
    return (v, None)

def back_low(kept, grad):
    return (low(grad),)
low.defvjp(low_keep, low_pass)
low_back.defvjp(back_keep, back_low)

def layer_norm(rows_in, norm_gain, norm_bias):
    center = rows_in - lax.optimization_barrier(jnp.mean(rows_in, axis=-1, keepdims=True))
    spread = lax.optimization_barrier(jnp.mean(center * center, axis=-1, keepdims=True))
    return center * lax.rsqrt(spread + LN_EPS) * norm_gain + norm_bias

def lamb_moments(master, first, second, grad, decay):
    new_first = MOMENT_DECAY * first + (1.0 - MOMENT_DECAY) * grad
    new_second = MOMENT_DECAY * second + (1.0 - MOMENT_DECAY) * grad * grad
    correction = 1.0 - MOMENT_DECAY ** STEP_COUNT
    update = new_first / correction / (jnp.sqrt(new_second / correction) + LAMB_EPS) + decay * master
    return (new_first, new_second, update)

def block_forward(x_rows, teach_rows, row_lengths, w_qkv, w_out, w_in, w_fo, norm_p, head_gate, unit_gate, hidden_gate, layer_gates):
    rows_here = x_rows.shape[0]
    seq_ends = jnp.cumsum(row_lengths, axis=1, dtype=jnp.int32)
    positions = jnp.arange(ROW, dtype=jnp.int32)
    seg_index = lax.optimization_barrier(jnp.sum((positions[None, :, None] >= seq_ends[:, None, :]).astype(jnp.int32), axis=2, dtype=jnp.int32))
    valid_mask = (positions[None, :] < seq_ends[:, -1:]).astype(jnp.float32).reshape(-1, 1)
    same_seq = seg_index[:, :, None] == seg_index[:, None, :]
    flat_in = x_rows.reshape(-1, D)
    qkv_all = jnp.dot(flat_in, w_qkv.reshape(D, 3 * D), precision=HIGHEST)
    qkv_all = low_back(low(qkv_all)).reshape(rows_here, ROW, 3, HEADS, HEAD_DIM)
    queries = qkv_all[:, :, 0]
    key_rows = qkv_all[:, :, 1]
    value_rows = qkv_all[:, :, 2]
    scores = jnp.einsum('rihd,rjhd->rhij', queries, key_rows, precision=HIGHEST) * HEAD_DIM ** (-0.5)
    scores = jnp.where(same_seq[:, None], low_back(scores), MASK_FILL)
    attn_probs = jax.nn.softmax(scores, axis=-1)
    head_mix = jnp.einsum('rhij,rjhd->rihd', low(attn_probs), value_rows, precision=HIGHEST)
    head_mix = low_back(head_mix)
    context = low(head_mix * head_gate[None, None, :, None]).reshape(-1, D)
    attn_part = jnp.dot(context, w_out, precision=HIGHEST)
    attention = low_back(attn_part) * layer_gates[0] * hidden_gate
    hidden = layer_norm(flat_in + attention, norm_p[0], norm_p[1])
    up_proj = low_back(jnp.dot(low(hidden), w_in, precision=HIGHEST))
    gated = low(jax.nn.gelu(up_proj, approximate=False) * unit_gate)
    ffn_part = jnp.dot(gated, w_fo, precision=HIGHEST)
    ffn_out = low_back(ffn_part) * layer_gates[1] * hidden_gate
    student = layer_norm(hidden + ffn_out, norm_p[2], norm_p[3])
    distance = student - teach_rows.reshape(-1, D)
    loss_part = 0.5 * jnp.sum(valid_mask * distance * distance)
    return (student, loss_part)

def reference(tokens, teacher, lengths, head_gate, unit_gate, hidden_gate, layer_gates, master_qkv, first_qkv, second_qkv, master_attn_out, first_attn_out, second_attn_out, master_ffn_in, first_ffn_in, second_ffn_in, master_ffn_out, first_ffn_out, second_ffn_out, master_norms, first_norms, second_norms):
    groups = TOKENS // (ROWS_DEV * ROW)
    copies_f = [w.astype(jnp.bfloat16).astype(jnp.float32) for w in (master_qkv, master_attn_out, master_ffn_in, master_ffn_out, master_norms)]
    x_float = tokens.astype(jnp.float32)
    teach_rows = teacher.astype(jnp.float32).reshape(groups, ROWS_DEV, ROW, D)
    row_lengths = lengths.reshape(groups, ROWS_DEV, SLOTS)

    def objective(x_in, w_qkv, w_out, w_in, w_fo, norm_p, gate_heads, gate_units, gate_hidden, gate_layers):

        def group_step(loss_total, pieces):
            x_rows, teach_part, length_part = pieces
            student, loss_part = block_forward(x_rows, teach_part, length_part, w_qkv, w_out, w_in, w_fo, norm_p, gate_heads, gate_units, gate_hidden, gate_layers)
            return (loss_total + loss_part, student)
        loss_total, students = lax.scan(jax.checkpoint(group_step), jnp.zeros((), jnp.float32), (x_in.reshape(groups, ROWS_DEV, ROW, D), teach_rows, row_lengths))
        return (loss_total, students.reshape(TOKENS, D))
    loss_total, pullback, student = jax.vjp(objective, x_float, *copies_f, head_gate, unit_gate, hidden_gate, layer_gates, has_aux=True)
    gradients = pullback(jnp.ones((), jnp.float32))
    grad_x, grad_qkv, grad_out, grad_in, grad_fo, grad_norm, grad_heads, grad_units, grad_hidden, grad_layers = gradients
    mats = [(master_qkv, first_qkv, second_qkv, grad_qkv), (master_attn_out, first_attn_out, second_attn_out, grad_out), (master_ffn_in, first_ffn_in, second_ffn_in, grad_in), (master_ffn_out, first_ffn_out, second_ffn_out, grad_fo)]
    results = []
    weight_norms = []
    update_norms = []
    for master, first, second, grad in mats:
        new_first, new_second, update = lamb_moments(master, first, second, grad, WEIGHT_DECAY)
        weight_norm = jnp.sqrt(jnp.sum(master * master))
        update_norm = jnp.sqrt(jnp.sum(update * update))
        new_master = master - LEARN_RATE * (weight_norm / update_norm) * update
        results.append((grad, new_first, new_second, new_master, new_master.astype(jnp.bfloat16)))
        weight_norms.append(weight_norm)
        update_norms.append(update_norm)
    nf_norms, ns_norms, upd_norms = lamb_moments(master_norms, first_norms, second_norms, grad_norm, 0.0)
    row_wnorm = jnp.sqrt(lax.optimization_barrier(jnp.sum(master_norms * master_norms, axis=1)))
    row_unorm = jnp.sqrt(lax.optimization_barrier(jnp.sum(upd_norms * upd_norms, axis=1)))
    new_norms = master_norms - LEARN_RATE * (row_wnorm / row_unorm)[:, None] * upd_norms
    all_wnorm = jnp.concatenate([jnp.stack(weight_norms), row_wnorm])
    all_unorm = jnp.concatenate([jnp.stack(update_norms), row_unorm])
    lamb_stats = jnp.stack([all_wnorm, all_unorm, all_wnorm / all_unorm])
    return (student.astype(jnp.bfloat16), grad_x, grad_heads, grad_units, grad_hidden, grad_layers, results[0][0], results[0][1], results[0][2], results[0][3], results[0][4], results[1][0], results[1][1], results[1][2], results[1][3], results[1][4], results[2][0], results[2][1], results[2][2], results[2][3], results[2][4], results[3][0], results[3][1], results[3][2], results[3][3], results[3][4], grad_norm, nf_norms, ns_norms, new_norms, new_norms.astype(jnp.bfloat16), lamb_stats)
```

```python
import functools

import jax
import jax.numpy as jnp
from jax import lax
from jax.experimental import pallas as pl
from jax.experimental.pallas import tpu as pltpu
from jax.sharding import PartitionSpec as P

D = 768
HEAD_DIM = 64
ROW = 512
STEP_COUNT = 5

LN_EPS = 1e-05
LAMB_EPS = 1e-06
WEIGHT_DECAY = 0.01
LEARN_RATE = 0.5
MOMENT_DECAY = 0.5
MASK_FILL = -1000000000.0


MESH = pl.DeviceIdType.MESH
NZ, NY, NX = 4, 2, 2
GRID = NZ * NY * NX
CHUNKS = (
    (0, 0, 640, 0),
    (0, 640, 512, 1),
    (1, 0, 128, 0),
    (1, 128, 256, 1),
    (2, 0, 768, 0),
    (2, 768, 768, 1),
    (3, 0, 768, 0),
    (3, 768, 768, 1),
)
NORM_CHUNK = (4, 0, 128, 0)


def place(me):
    return me // (NY * NX), (me // NX) % NY, me % NX


def index(z, y, x):
    return (z * NY + y) * NX + x


def relative(z, y, x, rz, ra, rb, order):
    zz = lax.rem(z + rz, NZ)
    flip_x, flip_y = (ra, rb) if order == 0 else (rb, ra)
    return index(zz, 1 - y if flip_y else y, 1 - x if flip_x else x)


def slot(rz, ra, rb):
    return rz + NZ * (ra + 2 * rb)


def greet(peers):
    barrier = pltpu.get_barrier_semaphore()
    for peer in peers:
        pl.semaphore_signal(barrier, inc=1, device_id=peer, device_id_type=MESH)
    pl.semaphore_wait(barrier, len(peers))


def grid_peers(z, y, x, core):
    ahead = [index(lax.rem(z + d, NZ), y, x) for d in (1, 2, 3)]
    beside = [index(z, y, 1 - x), index(z, 1 - y, x)]
    return [(p, core) for p in ahead + beside]


def gather_kernel(rows, count, *refs):
    chunks_here = (*CHUNKS, NORM_CHUNK)
    src, dst = refs[:count], refs[count : 2 * count]
    local_sem, send_sem, recv_sem = refs[2 * count :]
    me, core = lax.axis_index("dp"), lax.axis_index("head")
    z, y, x = place(me)
    greet(grid_peers(z, y, x, core))

    def rows_of(device):
        return pl.ds(pl.multiple_of(device * rows, rows), rows)

    def copy(c, rz, ra, rb, to, there, k, own=False):
        p, first, width, order = chunks_here[c]
        device = relative(z, y, x, rz, ra, rb, order)
        columns = pl.ds(first, width)
        source = src[p].at[:, columns] if own else dst[p].at[rows_of(device), columns]
        return pltpu.make_async_remote_copy(
            src_ref=source,
            dst_ref=dst[p].at[rows_of(device), columns],
            send_sem=send_sem.at[c, k],
            recv_sem=recv_sem.at[c, there],
            device_id=(to, core),
            device_id_type=MESH,
        )

    def arrived(c, rz, ra, rb):
        copy(c, rz, ra, rb, me, slot(rz, ra, rb), 0).wait_recv()

    sends = []

    def send(*args, **kwargs):
        one = copy(*args, **kwargs)
        one.start()
        sends.append(one)

    kept = [
        pltpu.make_async_copy(src[p], dst[p].at[rows_of(me)], local_sem.at[p]) for p in range(count)
    ]
    for one in kept:
        one.start()
    chunks = range(len(chunks_here))
    along = [
        (index(z, y, 1 - x), index(z, 1 - y, x))[:: 1 if chunks_here[c][3] == 0 else -1] for c in chunks
    ]
    for c in chunks:
        for i, dz in enumerate((1, 3, 2)):
            to = index(lax.rem(z + dz, NZ), y, x)
            send(c, 0, 0, 0, to, slot(NZ - dz, 0, 0), i, own=True)
        send(c, 0, 0, 0, along[c][0], slot(0, 1, 0), 3, own=True)
        send(c, 0, 0, 0, along[c][1], slot(0, 0, 1), 7, own=True)
    for pair in range(0, len(chunks_here), 2):
        both = chunks[pair : pair + 2]
        for c in both:
            for i, rz in enumerate((1, 3, 2)):
                arrived(c, rz, 0, 0)
                send(c, rz, 0, 0, along[c][0], slot(rz, 1, 0), 4 + i)
                send(c, rz, 0, 0, along[c][1], slot(rz, 0, 1), 8 + i)
        for c in both:
            for i, rz in enumerate((0, 1, 3, 2)):
                arrived(c, rz, 1, 0)
                send(c, rz, 1, 0, along[c][1], slot(rz, 1, 1), 11 + i)
    for c in chunks:
        for ra in (0, 1):
            for rz in range(NZ):
                arrived(c, rz, ra, 1)
    for one in sends:
        one.wait_send()
    for one in kept:
        one.wait()


def gather(shards):
    rows, count = shards[0].shape[0], len(shards)
    space = pl.BlockSpec(memory_space=pl.ANY)
    return pl.pallas_call(
        functools.partial(gather_kernel, rows, count),
        out_shape=[jax.ShapeDtypeStruct((rows * GRID, s.shape[1]), s.dtype) for s in shards],
        in_specs=[space] * count,
        out_specs=[space] * count,
        scratch_shapes=[
            pltpu.SemaphoreType.DMA((count,)),
            pltpu.SemaphoreType.DMA((len(CHUNKS) + 1, 15)),
            pltpu.SemaphoreType.DMA((len(CHUNKS) + 1, 16)),
        ],
        compiler_params=pltpu.CompilerParams(collective_id=0, has_side_effects=True),
        name="weights_gather",
    )(*shards)


def scatter_kernel(rows, count, *refs):
    grads, outs = refs[:count], refs[count : 2 * count]
    refs = refs[2 * count :]
    get1, get2, get3, put2, put3, keep = (refs[i * count : (i + 1) * count] for i in range(6))
    send_sem, recv_sem = refs[6 * count :]
    me, core = lax.axis_index("dp"), lax.axis_index("head")
    z, y, x = place(me)
    greet(grid_peers(z, y, x, core))

    def rows_of(device):
        return pl.ds(pl.multiple_of(device * rows, rows), rows)

    sends = []

    def send(source, target, c, k, to):
        one = pltpu.make_async_remote_copy(
            src_ref=source,
            dst_ref=target,
            send_sem=send_sem.at[c, k],
            recv_sem=recv_sem.at[c, k],
            device_id=(to, core),
            device_id_type=MESH,
        )
        one.start()
        sends.append(one)

    def arrived(target, c, k):
        pltpu.make_async_remote_copy(
            src_ref=target,
            dst_ref=target,
            send_sem=send_sem.at[c, k],
            recv_sem=recv_sem.at[c, k],
            device_id=(me, core),
            device_id_type=MESH,
        ).wait_recv()

    order_of = range(len(CHUNKS))[::-1]
    along = [
        (index(z, y, 1 - x), index(z, 1 - y, x))[:: 1 if chunk[3] == 0 else -1] for chunk in CHUNKS
    ]
    depth = (1, 3, 2, 0)
    for c in order_of:
        p, first, width, order = CHUNKS[c]
        columns = pl.ds(first, width)
        for ra in (1, 0):
            for rz in depth:
                k = rz + NZ * ra
                block = rows_of(relative(z, y, x, rz, ra, 1, order))
                send(grads[p].at[block, columns], get1[p].at[k, :, columns], c, k, along[c][1])

    def second(c):
        p, first, width, order = CHUNKS[c]
        columns = pl.ds(first, width)
        for ra in (1, 0):
            for rz in depth:
                k = rz + NZ * ra
                arrived(get1[p].at[k, :, columns], c, k)
                block = rows_of(relative(z, y, x, rz, ra, 0, order))
                total = grads[p][block, columns].astype(jnp.float32) + get1[p][
                    k, :, columns
                ].astype(jnp.float32)
                if ra:
                    put2[p][rz, :, columns] = total.astype(jnp.bfloat16)
                    send(
                        put2[p].at[rz, :, columns],
                        get2[p].at[rz, :, columns],
                        c,
                        8 + rz,
                        along[c][0],
                    )
                else:
                    keep[p][rz, :, columns] = total

    def third(c):
        p, first, width, order = CHUNKS[c]
        columns = pl.ds(first, width)
        for rz in depth:
            arrived(get2[p].at[rz, :, columns], c, 8 + rz)
            total = keep[p][rz, :, columns] + get2[p][rz, :, columns].astype(jnp.float32)
            if rz:
                put3[p][rz - 1, :, columns] = total.astype(jnp.bfloat16)
                there = NZ - rz
                send(
                    put3[p].at[rz - 1, :, columns],
                    get3[p].at[there - 1, :, columns],
                    c,
                    11 + there,
                    index(lax.rem(z + rz, NZ), y, x),
                )
            else:
                keep[p][0, :, columns] = total

    def last(c):
        p, first, width, order = CHUNKS[c]
        columns = pl.ds(first, width)
        total = keep[p][0, :, columns]
        for there in (1, 2, 3):
            arrived(get3[p].at[there - 1, :, columns], c, 11 + there)
            total = total + get3[p][there - 1, :, columns].astype(jnp.float32)
        outs[p][:, columns] = total

    for c in order_of:
        second(c)
        if c < len(CHUNKS) - 1:
            third(c + 1)
        if c < len(CHUNKS) - 2:
            last(c + 2)
    third(0)
    last(1)
    last(0)
    for one in sends:
        one.wait_send()


def scatter(grads):
    count, rows = len(grads), grads[0].shape[0] // GRID
    space = pl.BlockSpec(memory_space=pltpu.VMEM)
    widths = [g.shape[1] for g in grads]
    scratch = []
    for blocks, kind in ((8, jnp.bfloat16), (4, jnp.bfloat16), (3, jnp.bfloat16), (4, jnp.bfloat16), (3, jnp.bfloat16), (4, jnp.float32)):
        scratch += [pltpu.VMEM((blocks, rows, w), kind) for w in widths]
    return pl.pallas_call(
        functools.partial(scatter_kernel, rows, count),
        out_shape=[jax.ShapeDtypeStruct((rows, w), jnp.float32) for w in widths],
        in_specs=[space] * count,
        out_specs=[space] * count,
        scratch_shapes=[
            *scratch,
            pltpu.SemaphoreType.DMA((len(CHUNKS), 15)),
            pltpu.SemaphoreType.DMA((len(CHUNKS), 15)),
        ],
        compiler_params=pltpu.CompilerParams(
            collective_id=1, has_side_effects=True, vmem_limit_bytes=48 << 20
        ),
        name="grads_scatter",
    )(*grads)


def total_kernel(both, src, out, mine, landed, send_sem, recv_sem):
    me, core = lax.axis_index("dp"), lax.axis_index("head")
    z, y, x = place(me)
    peers = grid_peers(z, y, x, core)
    steps = [(index(z, y, 1 - x), core), (index(z, 1 - y, x), core)]
    if both:
        steps = [(me, 1 - core), *steps]
    greet(peers[:3] + steps)
    sends = []

    def send(source, k, to):
        one = pltpu.make_async_remote_copy(
            src_ref=source,
            dst_ref=landed.at[k],
            send_sem=send_sem.at[k],
            recv_sem=recv_sem.at[k],
            device_id=to,
            device_id_type=MESH,
        )
        one.start()
        sends.append(one)
        return one

    mine[0] = src[...]
    for k, to in enumerate(steps):
        send(mine.at[k], k, to).wait_recv()
        mine[k + 1] = mine[k] + landed[k]
    n = len(steps)
    for dz in (1, 2, 3):
        send(mine.at[n], n + NZ - dz - 1, peers[dz - 1])
    for one in sends[n:]:
        one.wait_recv()
    planes = [mine[n], *(landed[n + r - 1] for r in (1, 2, 3))]
    total = None
    for plane in range(NZ):
        turn = lax.rem(plane - z + NZ, NZ)
        part = planes[0]
        for r in (1, 2, 3):
            part = jnp.where(turn == r, planes[r], part)
        total = part if total is None else total + part
    out[...] = total
    for one in sends:
        one.wait_send()


def grid_total(packed, both):
    space = pl.BlockSpec(memory_space=pltpu.VMEM)
    return pl.pallas_call(
        functools.partial(total_kernel, both),
        out_shape=jax.ShapeDtypeStruct(packed.shape, jnp.float32),
        in_specs=[space],
        out_specs=space,
        scratch_shapes=[
            pltpu.VMEM((4, *packed.shape), jnp.float32),
            pltpu.VMEM((6, *packed.shape), jnp.float32),
            pltpu.SemaphoreType.DMA((6,)),
            pltpu.SemaphoreType.DMA((6,)),
        ],
        compiler_params=pltpu.CompilerParams(
            collective_id=3 if both else 2, has_side_effects=True, vmem_limit_bytes=16 << 20
        ),
        name="norms_total" if both else "gates_total",
    )(packed)


NT = (((1,), (1,)), ((), ()))
NN = (((1,), (0,)), ((), ()))
PAIR = 2 * HEAD_DIM


def mul(a, b, dims=NN):
    return lax.dot_general(a, b, dims, preferred_element_type=jnp.float32)


def segments(lengths_ref, row, shape, axis):
    positions = lax.broadcasted_iota(jnp.int32, shape, axis)
    end = jnp.int32(0)
    found = jnp.zeros(shape, jnp.int32)
    for k in range(lengths_ref.shape[1]):
        end = end + lengths_ref[row, k]
        found = found + (positions >= end).astype(jnp.int32)
    return found


def flip(block):
    return jnp.transpose(block.astype(jnp.float32)).astype(block.dtype)


def head_lanes(block, head):
    lane = lax.broadcasted_iota(jnp.int32, block.shape, 1)
    inside = (lane < HEAD_DIM) if head == 0 else (lane >= HEAD_DIM)
    return jnp.where(inside, block, jnp.zeros_like(block))


def attention_kernel(lengths_ref, gate_ref, q_ref, k_ref, v_ref, mix_ref, context_ref, stats_ref):
    row = pl.program_id(0)
    same = segments(lengths_ref, row, (ROW, 1), 0) == segments(lengths_ref, row, (1, ROW), 1)
    queries = q_ref[...] * jnp.bfloat16(HEAD_DIM**-0.5)
    values_t = flip(v_ref[...])
    mixes = []
    for head in (0, 1):
        scores = mul(k_ref[...], head_lanes(queries, head), NT)
        scores = jnp.where(same, scores, MASK_FILL)
        top = jnp.max(scores, axis=0, keepdims=True)
        expo = jnp.exp(scores - top)
        total = jnp.sum(expo, axis=0, keepdims=True)
        probs = (expo * (1.0 / total)).astype(jnp.bfloat16)
        mixes.append(mul(values_t[head * HEAD_DIM : (head + 1) * HEAD_DIM], probs))
        stats_ref[0, 0, head : head + 1, :] = top + jnp.log(total)
    mix = jnp.transpose(jnp.concatenate(mixes, axis=0))
    mix_ref[...] = mix
    context_ref[...] = (mix * gate_ref[...]).astype(jnp.bfloat16)


def attention(qkv, lengths, gate_lanes):
    tokens, width = qkv.shape
    rows, pairs = lengths.shape[0], width // 3 // PAIR
    block = lambda part: pl.BlockSpec((ROW, PAIR), lambda r, h: (r, part * pairs + h))
    own = pl.BlockSpec((ROW, PAIR), lambda r, h: (r, h))
    return pl.pallas_call(
        attention_kernel,
        grid=(rows, pairs),
        in_specs=[
            pl.BlockSpec(memory_space=pltpu.SMEM),
            pl.BlockSpec((1, PAIR), lambda r, h: (0, h)),
            block(0),
            block(1),
            block(2),
        ],
        out_specs=[own, own, pl.BlockSpec((1, 1, 8, ROW), lambda r, h: (r, h, 0, 0))],
        out_shape=[
            jax.ShapeDtypeStruct((tokens, width // 3), jnp.float32),
            jax.ShapeDtypeStruct((tokens, width // 3), jnp.bfloat16),
            jax.ShapeDtypeStruct((rows, pairs, 8, ROW), jnp.float32),
        ],
        compiler_params=pltpu.CompilerParams(vmem_limit_bytes=32 << 20),
        cost_estimate=pl.CostEstimate(
            flops=4 * rows * pairs * 2 * ROW * ROW * HEAD_DIM,
            bytes_accessed=tokens * width * 4,
            transcendentals=rows * pairs * 2 * ROW * ROW,
        ),
        name="attention",
    )(lengths, gate_lanes, qkv, qkv, qkv)


def attention_back_kernel(
    lengths_ref, gate_ref, q_ref, k_ref, v_ref, stats_ref, mix_ref, d_ref, out_ref, heads_ref
):
    row, pair = pl.program_id(0), pl.program_id(1)
    same = segments(lengths_ref, row, (ROW, 1), 0) == segments(lengths_ref, row, (1, ROW), 1)
    queries = q_ref[...] * jnp.bfloat16(HEAD_DIM**-0.5)
    keys, values = k_ref[...], v_ref[...]
    keys_t = flip(keys)
    d_context = d_ref[...]
    heads_ref[0, 0] = jnp.broadcast_to(
        jnp.sum(d_context * mix_ref[...], axis=0, keepdims=True), (8, PAIR)
    )
    d_mix = (d_context * gate_ref[...]).astype(jnp.bfloat16)
    d_queries, d_keys, d_values = [], None, None
    for head in (0, 1):
        q_one, d_one = head_lanes(queries, head), head_lanes(d_mix, head)
        scores = jnp.where(same, mul(keys, q_one, NT), MASK_FILL)
        probs = jnp.exp(scores - stats_ref[0, 0, head : head + 1, :])
        d_probs = mul(values, d_one, NT)
        weighed = jnp.sum(probs * d_probs, axis=0, keepdims=True)
        d_scores = (probs * (d_probs - weighed)).astype(jnp.bfloat16)
        dv = mul(probs.astype(jnp.bfloat16), d_one)
        dk = mul(d_scores, q_one)
        d_values = dv if head == 0 else d_values + dv
        d_keys = dk if head == 0 else d_keys + dk
        d_queries.append(mul(keys_t[head * HEAD_DIM : (head + 1) * HEAD_DIM], d_scores))
    dq = jnp.transpose(jnp.concatenate(d_queries, axis=0)) * HEAD_DIM**-0.5
    width = out_ref.shape[1] // 3
    for part, value in enumerate((dq, d_keys, d_values)):
        start = pl.multiple_of(part * width + pair * PAIR, PAIR)
        out_ref[:, pl.ds(start, PAIR)] = value.astype(jnp.bfloat16)


def attention_back(qkv, lengths, gate_lanes, stats, mix, d_context):
    tokens, width = qkv.shape
    rows, pairs = lengths.shape[0], width // 3 // PAIR
    block = lambda part: pl.BlockSpec((ROW, PAIR), lambda r, h: (r, part * pairs + h))
    own = pl.BlockSpec((ROW, PAIR), lambda r, h: (r, h))
    small = pl.BlockSpec((1, 1, 8, ROW), lambda r, h: (r, h, 0, 0))
    return pl.pallas_call(
        attention_back_kernel,
        grid=(rows, pairs),
        in_specs=[
            pl.BlockSpec(memory_space=pltpu.SMEM),
            pl.BlockSpec((1, PAIR), lambda r, h: (0, h)),
            block(0),
            block(1),
            block(2),
            small,
            own,
            own,
        ],
        out_specs=[
            pl.BlockSpec((ROW, width), lambda r, h: (r, 0)),
            pl.BlockSpec((1, 1, 8, PAIR), lambda r, h: (r, h, 0, 0)),
        ],
        out_shape=[
            jax.ShapeDtypeStruct((tokens, width), jnp.bfloat16),
            jax.ShapeDtypeStruct((rows, pairs, 8, PAIR), jnp.float32),
        ],
        compiler_params=pltpu.CompilerParams(vmem_limit_bytes=32 << 20),
        cost_estimate=pl.CostEstimate(
            flops=10 * rows * pairs * 2 * ROW * ROW * HEAD_DIM,
            bytes_accessed=tokens * width * 8,
            transcendentals=rows * pairs * 2 * ROW * ROW,
        ),
        name="attention_back",
    )(lengths, gate_lanes, qkv, qkv, qkv, stats, mix, d_context)


def layer_norm(rows_in, norm_gain, norm_bias):
    center = rows_in - jnp.mean(rows_in, axis=-1, keepdims=True)
    spread = jnp.mean(center * center, axis=-1, keepdims=True)
    return center * lax.rsqrt(spread + LN_EPS) * norm_gain + norm_bias


def lamb_moments(master, first, second, grad, decay):
    new_first = MOMENT_DECAY * first + (1.0 - MOMENT_DECAY) * grad
    new_second = MOMENT_DECAY * second + (1.0 - MOMENT_DECAY) * grad * grad
    correction = 1.0 - MOMENT_DECAY**STEP_COUNT
    update = (
        new_first / correction / (jnp.sqrt(new_second / correction) + LAMB_EPS) + decay * master
    )
    return (new_first, new_second, update)


def core_sum(part):
    part = part.astype(jnp.bfloat16)
    other = lax.ppermute(part, "head", [(0, 1), (1, 0)])
    return part.astype(jnp.float32) + other.astype(jnp.float32)


def pack(pieces):
    flat = []
    for piece in pieces:
        piece = piece.reshape(-1)
        flat.append(jnp.pad(piece, (0, -piece.size % 128)))
    flat = jnp.concatenate(flat)
    return jnp.pad(flat, (0, -flat.size % 1024)).reshape(-1, 128)


def unpack(packed, pieces):
    flat, first, found = packed.reshape(-1), 0, []
    for piece in pieces:
        found.append(flat[first : first + piece.size].reshape(piece.shape))
        first += piece.size + -piece.size % 128
    return found


def rows_first(qkv):
    return jnp.transpose(qkv, (1, 0, 2))


def local(
    tokens,
    teacher,
    lengths,
    head_gate,
    unit_gate,
    hidden_gate,
    layer_gates,
    master_qkv,
    first_qkv,
    second_qkv,
    master_attn_out,
    first_attn_out,
    second_attn_out,
    master_ffn_in,
    first_ffn_in,
    second_ffn_in,
    master_ffn_out,
    first_ffn_out,
    second_ffn_out,
    master_norms,
    first_norms,
    second_norms,
):
    heads_here = head_gate.shape[0]
    local_width = heads_here * HEAD_DIM
    head_count = lax.axis_size("head")
    ours = lax.axis_size("dp") == GRID and head_count == 2
    shard = master_qkv.shape[0]
    weight_squares = jnp.concatenate(
        [
            jnp.stack(
                [
                    jnp.sum(master_qkv * master_qkv),
                    jnp.sum(master_attn_out * master_attn_out),
                    jnp.sum(master_ffn_in * master_ffn_in),
                    jnp.sum(master_ffn_out * master_ffn_out),
                ]
            ),
            jnp.sum(master_norms * master_norms, axis=1) / head_count,
        ]
    )
    shards = [
        master_qkv.astype(jnp.bfloat16).reshape(shard, 3 * local_width),
        master_attn_out.T.astype(jnp.bfloat16),
        master_ffn_in.astype(jnp.bfloat16),
        master_ffn_out.T.astype(jnp.bfloat16),
        jnp.pad(master_norms.T, ((0, 0), (0, 124))).astype(jnp.bfloat16),
    ]
    if ours:
        w_qkv, w_out_t, w_in, w_fo_t, norm_t = gather(shards)
    else:
        w_qkv, w_out_t, w_in, w_fo_t, norm_t = (
            lax.all_gather(s, "dp", axis=0, tiled=True) for s in shards
        )
    norm_p = norm_t[:, :4].T.astype(jnp.float32)
    total = jnp.sum(lengths, axis=1, keepdims=True)
    positions = jnp.arange(ROW, dtype=jnp.int32)
    valid_mask = (positions[None, :] < total).astype(jnp.float32).reshape(-1, 1)
    gate_lanes = jnp.repeat(head_gate, HEAD_DIM)[None, :]
    qkv = jnp.dot(tokens, w_qkv, preferred_element_type=jnp.float32).astype(jnp.bfloat16)
    head_mix, context, stats = attention(qkv, lengths, gate_lanes)
    attn_part = jnp.einsum("tc,dc->td", context, w_out_t, preferred_element_type=jnp.float32)
    attn_sum = core_sum(attn_part)
    residual_in = tokens.astype(jnp.float32)
    teach_rows = teacher.astype(jnp.float32)
    attention_out = attn_sum * layer_gates[0] * hidden_gate
    hidden, first_norm_back = jax.vjp(
        layer_norm, residual_in + attention_out, norm_p[0], norm_p[1]
    )
    hidden_low = hidden.astype(jnp.bfloat16)
    up_proj = jnp.dot(hidden_low, w_in, preferred_element_type=jnp.float32)
    gelu_out, gelu_back = jax.vjp(
        functools.partial(jax.nn.gelu, approximate=False), up_proj
    )
    gated = (gelu_out * unit_gate).astype(jnp.bfloat16)
    ffn_part = jnp.einsum("tu,du->td", gated, w_fo_t, preferred_element_type=jnp.float32)
    ffn_sum = core_sum(ffn_part)
    ffn_out = ffn_sum * layer_gates[1] * hidden_gate
    student, second_norm_back = jax.vjp(layer_norm, hidden + ffn_out, norm_p[2], norm_p[3])
    d_out = valid_mask * (student - teach_rows)
    d_res2, d_gain2, d_bias2 = second_norm_back(d_out)
    d_layer1 = jnp.sum(d_res2 * ffn_sum * hidden_gate)
    d_hidden_gate = jnp.sum(d_res2 * ffn_sum, axis=0) * layer_gates[1]
    d_ffn_part = (d_res2 * hidden_gate * layer_gates[1]).astype(jnp.bfloat16)
    student_low = student.astype(jnp.bfloat16)
    grad_fo_t = jnp.einsum("td,tu->du", d_ffn_part, gated, preferred_element_type=jnp.float32)
    d_gated = jnp.dot(d_ffn_part, w_fo_t, preferred_element_type=jnp.float32)
    d_unit = jnp.sum(d_gated * gelu_out, axis=0)
    (d_up,) = gelu_back(d_gated * unit_gate)
    d_up_low = d_up.astype(jnp.bfloat16)
    grad_in = jnp.einsum("tc,tu->cu", hidden_low, d_up_low, preferred_element_type=jnp.float32)
    back_part = jnp.einsum("tu,cu->tc", d_up_low, w_in, preferred_element_type=jnp.float32)
    d_hidden = d_res2 + core_sum(back_part)
    d_res1, d_gain1, d_bias1 = first_norm_back(d_hidden)
    d_layer0 = jnp.sum(d_res1 * attn_sum * hidden_gate)
    d_hidden_gate = d_hidden_gate + jnp.sum(d_res1 * attn_sum, axis=0) * layer_gates[0]
    d_attn_part = (d_res1 * hidden_gate * layer_gates[0]).astype(jnp.bfloat16)
    grad_out_t = jnp.einsum("td,tc->dc", d_attn_part, context, preferred_element_type=jnp.float32)
    d_context = jnp.dot(d_attn_part, w_out_t, preferred_element_type=jnp.float32)
    d_qkv, head_lanes_sum = attention_back(qkv, lengths, gate_lanes, stats, head_mix, d_context)
    d_heads = jnp.sum(
        head_lanes_sum[:, :, 0, :].reshape(-1, heads_here, HEAD_DIM), axis=(0, 2)
    )
    grad_qkv = jnp.einsum("tc,tk->ck", tokens, d_qkv, preferred_element_type=jnp.float32)
    input_part = jnp.einsum("tk,ck->tc", d_qkv, w_qkv, preferred_element_type=jnp.float32)
    grad_norm_rows = jnp.stack([d_gain1, d_bias1, d_gain2, d_bias2])
    layer_pair = jnp.stack([d_layer0, d_layer1])
    grad_tokens = d_res1 + core_sum(input_part)
    grads = [grad_qkv, grad_out_t, grad_in, grad_fo_t]
    small = [d_heads, d_unit, d_hidden_gate, layer_pair, grad_norm_rows]
    if ours:
        sums = list(scatter([g.astype(jnp.bfloat16) for g in grads]))
        gate_heads, gate_units, gate_hidden, gate_layers, norm_total = unpack(
            grid_total(pack(small), False), small
        )
    else:
        sums = [lax.psum_scatter(g, "dp", scatter_dimension=0, tiled=True) for g in grads]
        gate_heads, gate_units, gate_hidden, gate_layers, norm_total = lax.psum(small, "dp")
    columns = master_norms.shape[1]
    sum_norm = lax.dynamic_slice_in_dim(norm_total, lax.axis_index("dp") * columns, columns, 1)
    sums[0] = sums[0].reshape(shard, 3, local_width)
    mats = [
        (master_qkv, first_qkv, second_qkv, sums[0]),
        (master_attn_out, first_attn_out, second_attn_out, sums[1].T),
        (master_ffn_in, first_ffn_in, second_ffn_in, sums[2]),
        (master_ffn_out, first_ffn_out, second_ffn_out, sums[3].T),
    ]
    moments = [
        lamb_moments(master, first, second, grad, WEIGHT_DECAY)
        for master, first, second, grad in mats
    ]
    nf_norms, ns_norms, upd_norms = lamb_moments(
        master_norms, first_norms, second_norms, sum_norm, 0.0
    )
    update_squares = jnp.concatenate(
        [
            jnp.stack([jnp.sum(entry[2] * entry[2]) for entry in moments]),
            jnp.sum(upd_norms * upd_norms, axis=1) / head_count,
        ]
    )
    squares = [weight_squares, update_squares]
    if ours:
        weight_total, update_total = unpack(grid_total(pack(squares), True), squares)
    else:
        weight_total, update_total = lax.psum(squares, ("dp", "head"))
    weight_norm = jnp.sqrt(weight_total)
    update_norm = jnp.sqrt(update_total)
    trust_ratio = weight_norm / update_norm
    results = []
    for at in range(4):
        master, first, second, grad = mats[at]
        new_first, new_second, update = moments[at]
        new_master = master - LEARN_RATE * trust_ratio[at] * update
        results += [grad, new_first, new_second, new_master, new_master.astype(jnp.bfloat16)]
    new_norms = master_norms - LEARN_RATE * trust_ratio[4:][:, None] * upd_norms
    lamb_stats = jnp.stack([weight_norm, update_norm, trust_ratio])
    return (
        student_low,
        grad_tokens,
        gate_heads,
        gate_units,
        gate_hidden,
        gate_layers,
        *results,
        sum_norm,
        nf_norms,
        ns_norms,
        new_norms,
        new_norms.astype(jnp.bfloat16),
        lamb_stats,
    )


def solution(mesh):
    return jax.shard_map(
        local,
        mesh=mesh,
        in_specs=(
            P("dp", None),
            P("dp", None),
            P("dp", None),
            P("head"),
            P("head"),
            P(),
            P(),
            P("dp", None, "head"),
            P("dp", None, "head"),
            P("dp", None, "head"),
            P("head", "dp"),
            P("head", "dp"),
            P("head", "dp"),
            P("dp", "head"),
            P("dp", "head"),
            P("dp", "head"),
            P("head", "dp"),
            P("head", "dp"),
            P("head", "dp"),
            P(None, "dp"),
            P(None, "dp"),
            P(None, "dp"),
        ),
        out_specs=(
            P("dp", None),
            P("dp", None),
            P("head"),
            P("head"),
            P(),
            P(),
            P("dp", None, "head"),
            P("dp", None, "head"),
            P("dp", None, "head"),
            P("dp", None, "head"),
            P("dp", None, "head"),
            P("head", "dp"),
            P("head", "dp"),
            P("head", "dp"),
            P("head", "dp"),
            P("head", "dp"),
            P("dp", "head"),
            P("dp", "head"),
            P("dp", "head"),
            P("dp", "head"),
            P("dp", "head"),
            P("head", "dp"),
            P("head", "dp"),
            P("head", "dp"),
            P("head", "dp"),
            P("head", "dp"),
            P(None, "dp"),
            P(None, "dp"),
            P(None, "dp"),
            P(None, "dp"),
            P(None, "dp"),
            P(),
        ),
        check_vma=False,
    )
```

```python
import functools

import jax
import jax.numpy as jnp
from jax import lax
from jax.experimental import pallas as pl
from jax.experimental.pallas import tpu as pltpu
from jax.sharding import PartitionSpec as P

D = 768
HEAD_DIM = 64
ROW = 512
STEP_COUNT = 5

LN_EPS = 1e-05
LAMB_EPS = 1e-06
WEIGHT_DECAY = 0.01
LEARN_RATE = 0.5
MOMENT_DECAY = 0.5
MASK_FILL = -1000000000.0


MESH = pl.DeviceIdType.MESH
NZ, NY, NX = 4, 2, 2
GRID = NZ * NY * NX
CHUNKS = (
    (0, 0, 640, 0),
    (0, 640, 512, 1),
    (1, 0, 128, 0),
    (1, 128, 256, 1),
    (2, 0, 768, 0),
    (2, 768, 768, 1),
    (3, 0, 768, 0),
    (3, 768, 768, 1),
)
NORM_CHUNK = (4, 0, 128, 0)


def place(me):
    return me // (NY * NX), (me // NX) % NY, me % NX


def index(z, y, x):
    return (z * NY + y) * NX + x


def relative(z, y, x, rz, ra, rb, order):
    zz = lax.rem(z + rz, NZ)
    flip_x, flip_y = (ra, rb) if order == 0 else (rb, ra)
    return index(zz, 1 - y if flip_y else y, 1 - x if flip_x else x)


def slot(rz, ra, rb):
    return rz + NZ * (ra + 2 * rb)


def greet(peers):
    barrier = pltpu.get_barrier_semaphore()
    for peer in peers:
        pl.semaphore_signal(barrier, inc=1, device_id=peer, device_id_type=MESH)
    pl.semaphore_wait(barrier, len(peers))


def grid_peers(z, y, x, core):
    ahead = [index(lax.rem(z + d, NZ), y, x) for d in (1, 2, 3)]
    beside = [index(z, y, 1 - x), index(z, 1 - y, x)]
    return [(p, core) for p in ahead + beside]


def gather_kernel(rows, count, *refs):
    chunks_here = (*CHUNKS, NORM_CHUNK)
    src, dst = refs[:count], refs[count : 2 * count]
    local_sem, send_sem, recv_sem = refs[2 * count :]
    me, core = lax.axis_index("dp"), lax.axis_index("head")
    z, y, x = place(me)
    greet(grid_peers(z, y, x, core))

    def rows_of(device):
        return pl.ds(pl.multiple_of(device * rows, rows), rows)

    def copy(c, rz, ra, rb, to, there, k, own=False):
        p, first, width, order = chunks_here[c]
        device = relative(z, y, x, rz, ra, rb, order)
        columns = pl.ds(first, width)
        source = src[p].at[:, columns] if own else dst[p].at[rows_of(device), columns]
        return pltpu.make_async_remote_copy(
            src_ref=source,
            dst_ref=dst[p].at[rows_of(device), columns],
            send_sem=send_sem.at[c, k],
            recv_sem=recv_sem.at[c, there],
            device_id=(to, core),
            device_id_type=MESH,
        )

    def arrived(c, rz, ra, rb):
        copy(c, rz, ra, rb, me, slot(rz, ra, rb), 0).wait_recv()

    sends = []

    def send(*args, **kwargs):
        one = copy(*args, **kwargs)
        one.start()
        sends.append(one)

    kept = [
        pltpu.make_async_copy(src[p], dst[p].at[rows_of(me)], local_sem.at[p]) for p in range(count)
    ]
    for one in kept:
        one.start()
    chunks = range(len(chunks_here))
    along = [
        (index(z, y, 1 - x), index(z, 1 - y, x))[:: 1 if chunks_here[c][3] == 0 else -1] for c in chunks
    ]
    for c in chunks:
        for i, dz in enumerate((1, 3, 2)):
            to = index(lax.rem(z + dz, NZ), y, x)
            send(c, 0, 0, 0, to, slot(NZ - dz, 0, 0), i, own=True)
        send(c, 0, 0, 0, along[c][0], slot(0, 1, 0), 3, own=True)
        send(c, 0, 0, 0, along[c][1], slot(0, 0, 1), 7, own=True)
    for pair in range(0, len(chunks_here), 2):
        both = chunks[pair : pair + 2]
        for c in both:
            for i, rz in enumerate((1, 3, 2)):
                arrived(c, rz, 0, 0)
                send(c, rz, 0, 0, along[c][0], slot(rz, 1, 0), 4 + i)
                send(c, rz, 0, 0, along[c][1], slot(rz, 0, 1), 8 + i)
        for c in both:
            for i, rz in enumerate((0, 1, 3, 2)):
                arrived(c, rz, 1, 0)
                send(c, rz, 1, 0, along[c][1], slot(rz, 1, 1), 11 + i)
    for c in chunks:
        for ra in (0, 1):
            for rz in range(NZ):
                arrived(c, rz, ra, 1)
    for one in sends:
        one.wait_send()
    for one in kept:
        one.wait()


def gather(shards):
    rows, count = shards[0].shape[0], len(shards)
    space = pl.BlockSpec(memory_space=pl.ANY)
    return pl.pallas_call(
        functools.partial(gather_kernel, rows, count),
        out_shape=[jax.ShapeDtypeStruct((rows * GRID, s.shape[1]), s.dtype) for s in shards],
        in_specs=[space] * count,
        out_specs=[space] * count,
        scratch_shapes=[
            pltpu.SemaphoreType.DMA((count,)),
            pltpu.SemaphoreType.DMA((len(CHUNKS) + 1, 15)),
            pltpu.SemaphoreType.DMA((len(CHUNKS) + 1, 16)),
        ],
        compiler_params=pltpu.CompilerParams(collective_id=0, has_side_effects=True),
        name="weights_gather",
    )(*shards)


NT = (((1,), (1,)), ((), ()))
NN = (((1,), (0,)), ((), ()))
PAIR = 2 * HEAD_DIM


def mul(a, b, dims=NN):
    return lax.dot_general(a, b, dims, preferred_element_type=jnp.float32)


def segments(lengths_ref, row, shape, axis):
    positions = lax.broadcasted_iota(jnp.int32, shape, axis)
    end = jnp.int32(0)
    found = jnp.zeros(shape, jnp.int32)
    for k in range(lengths_ref.shape[1]):
        end = end + lengths_ref[row, k]
        found = found + (positions >= end).astype(jnp.int32)
    return found


def flip(block):
    return jnp.transpose(block.astype(jnp.float32)).astype(block.dtype)


def head_lanes(block, head):
    lane = lax.broadcasted_iota(jnp.int32, block.shape, 1)
    inside = (lane < HEAD_DIM) if head == 0 else (lane >= HEAD_DIM)
    return jnp.where(inside, block, jnp.zeros_like(block))


def attention_kernel(lengths_ref, gate_ref, q_ref, k_ref, v_ref, mix_ref, context_ref, stats_ref):
    row = pl.program_id(0)
    same = segments(lengths_ref, row, (ROW, 1), 0) == segments(lengths_ref, row, (1, ROW), 1)
    queries = q_ref[...] * jnp.bfloat16(HEAD_DIM**-0.5)
    values_t = flip(v_ref[...])
    mixes = []
    for head in (0, 1):
        scores = mul(k_ref[...], head_lanes(queries, head), NT)
        scores = jnp.where(same, scores, MASK_FILL)
        top = jnp.max(scores, axis=0, keepdims=True)
        expo = jnp.exp(scores - top)
        total = jnp.sum(expo, axis=0, keepdims=True)
        probs = (expo * (1.0 / total)).astype(jnp.bfloat16)
        mixes.append(mul(values_t[head * HEAD_DIM : (head + 1) * HEAD_DIM], probs))
        stats_ref[0, 0, head : head + 1, :] = top + jnp.log(total)
    mix = jnp.transpose(jnp.concatenate(mixes, axis=0))
    mix_ref[...] = mix
    context_ref[...] = (mix * gate_ref[...]).astype(jnp.bfloat16)


def attention(qkv, lengths, gate_lanes):
    tokens, width = qkv.shape
    rows, pairs = lengths.shape[0], width // 3 // PAIR
    block = lambda part: pl.BlockSpec((ROW, PAIR), lambda r, h: (r, part * pairs + h))
    own = pl.BlockSpec((ROW, PAIR), lambda r, h: (r, h))
    return pl.pallas_call(
        attention_kernel,
        grid=(rows, pairs),
        in_specs=[
            pl.BlockSpec(memory_space=pltpu.SMEM),
            pl.BlockSpec((1, PAIR), lambda r, h: (0, h)),
            block(0),
            block(1),
            block(2),
        ],
        out_specs=[own, own, pl.BlockSpec((1, 1, 8, ROW), lambda r, h: (r, h, 0, 0))],
        out_shape=[
            jax.ShapeDtypeStruct((tokens, width // 3), jnp.float32),
            jax.ShapeDtypeStruct((tokens, width // 3), jnp.bfloat16),
            jax.ShapeDtypeStruct((rows, pairs, 8, ROW), jnp.float32),
        ],
        compiler_params=pltpu.CompilerParams(vmem_limit_bytes=32 << 20),
        cost_estimate=pl.CostEstimate(
            flops=4 * rows * pairs * 2 * ROW * ROW * HEAD_DIM,
            bytes_accessed=tokens * width * 4,
            transcendentals=rows * pairs * 2 * ROW * ROW,
        ),
        name="attention",
    )(lengths, gate_lanes, qkv, qkv, qkv)


def attend_back(same, gate, queries, keys, values, stats, d_context):
    queries = queries * jnp.bfloat16(HEAD_DIM**-0.5)
    keys_t = flip(keys)
    d_mix = (d_context * gate).astype(jnp.bfloat16)
    d_queries, d_keys, d_values = [], None, None
    for head in (0, 1):
        q_one, d_one = head_lanes(queries, head), head_lanes(d_mix, head)
        scores = jnp.where(same, mul(keys, q_one, NT), MASK_FILL)
        probs = jnp.exp(scores - stats[head : head + 1, :])
        d_probs = mul(values, d_one, NT)
        weighed = jnp.sum(probs * d_probs, axis=0, keepdims=True)
        d_scores = (probs * (d_probs - weighed)).astype(jnp.bfloat16)
        dv = mul(probs.astype(jnp.bfloat16), d_one)
        dk = mul(d_scores, q_one)
        d_values = dv if head == 0 else d_values + dv
        d_keys = dk if head == 0 else d_keys + dk
        d_queries.append(mul(keys_t[head * HEAD_DIM : (head + 1) * HEAD_DIM], d_scores))
    dq = jnp.transpose(jnp.concatenate(d_queries, axis=0)) * HEAD_DIM**-0.5
    return dq, d_keys, d_values


def attention_back_kernel(
    lengths_ref, gate_ref, q_ref, k_ref, v_ref, stats_ref, mix_ref, d_ref, out_ref, heads_ref
):
    row, pair = pl.program_id(0), pl.program_id(1)
    same = segments(lengths_ref, row, (ROW, 1), 0) == segments(lengths_ref, row, (1, ROW), 1)
    d_context = d_ref[...]
    heads_ref[0, 0] = jnp.broadcast_to(
        jnp.sum(d_context * mix_ref[...], axis=0, keepdims=True), (8, PAIR)
    )
    parts = attend_back(
        same, gate_ref[...], q_ref[...], k_ref[...], v_ref[...], stats_ref[0, 0], d_context
    )
    width = out_ref.shape[1] // 3
    for part, value in enumerate(parts):
        start = pl.multiple_of(part * width + pair * PAIR, PAIR)
        out_ref[:, pl.ds(start, PAIR)] = value.astype(jnp.bfloat16)


def attention_back(qkv, lengths, gate_lanes, stats, mix, d_context):
    tokens, width = qkv.shape
    rows, pairs = lengths.shape[0], width // 3 // PAIR
    block = lambda part: pl.BlockSpec((ROW, PAIR), lambda r, h: (r, part * pairs + h))
    own = pl.BlockSpec((ROW, PAIR), lambda r, h: (r, h))
    small = pl.BlockSpec((1, 1, 8, ROW), lambda r, h: (r, h, 0, 0))
    return pl.pallas_call(
        attention_back_kernel,
        grid=(rows, pairs),
        in_specs=[
            pl.BlockSpec(memory_space=pltpu.SMEM),
            pl.BlockSpec((1, PAIR), lambda r, h: (0, h)),
            block(0),
            block(1),
            block(2),
            small,
            own,
            own,
        ],
        out_specs=[
            pl.BlockSpec((ROW, width), lambda r, h: (r, 0)),
            pl.BlockSpec((1, 1, 8, PAIR), lambda r, h: (r, h, 0, 0)),
        ],
        out_shape=[
            jax.ShapeDtypeStruct((tokens, width), jnp.bfloat16),
            jax.ShapeDtypeStruct((rows, pairs, 8, PAIR), jnp.float32),
        ],
        compiler_params=pltpu.CompilerParams(vmem_limit_bytes=32 << 20),
        cost_estimate=pl.CostEstimate(
            flops=10 * rows * pairs * 2 * ROW * ROW * HEAD_DIM,
            bytes_accessed=tokens * width * 8,
            transcendentals=rows * pairs * 2 * ROW * ROW,
        ),
        name="attention_back",
    )(lengths, gate_lanes, qkv, qkv, qkv, stats, mix, d_context)


TILE = 256
PART = 256
TAIL_STEP = 0.3
TAIL = (
    0.11963200569152832,
    0.12071217596530914,
    0.10017567127943039,
    0.1276927888393402,
    -0.052036140114068985,
    0.2045592963695526,
    -0.15616002678871155,
    0.035424139350652695,
)


def normal_parts(u):
    bell = jnp.exp(-0.5 * u * u)
    t = 1.0 / (1.0 + TAIL_STEP * jnp.abs(u))
    series = TAIL[-1]
    for term in TAIL[-2::-1]:
        series = series * t + term
    tail = series * t * bell
    return jnp.where(u < 0, tail, 1.0 - tail), u * bell * 0.3989422804014327


def fold(block):
    return jnp.sum(block.reshape(-1, 8, block.shape[1]), axis=0)


def norm_back(d_out, normal, scale, gain):
    d_normal = d_out * gain
    d_normal = (
        d_normal
        - jnp.mean(d_normal, axis=-1, keepdims=True)
        - normal * jnp.mean(d_normal * normal, axis=-1, keepdims=True)
    )
    return d_normal * scale


def normalize(rows_in):
    center = rows_in - jnp.mean(rows_in, axis=-1, keepdims=True)
    scale = lax.rsqrt(jnp.mean(center * center, axis=-1, keepdims=True) + LN_EPS)
    return center * scale, scale


def ffn_kernel(
    lengths_ref,
    gates_ref,
    norm_ref,
    hidden_gate_ref,
    unit_gate_ref,
    context_ref,
    w_out_ref,
    tokens_hbm,
    teacher_hbm,
    w_in_hbm,
    w_fo_hbm,
    student_hbm,
    d_res1_hbm,
    d_context_hbm,
    grads_hbm,
    small_ref,
    w_in,
    w_fo,
    tokens,
    teacher,
    own1,
    own2,
    got1,
    got2,
    got3,
    normal1,
    scale1,
    gated,
    slope,
    d_res,
    d_context,
    hidden_t,
    d_ffn_t,
    d_attn_t,
    grad_wide,
    grad_out,
    sums,
    unit_sum,
    load_sem,
    tile_sem,
    grad_sem,
    send_sem,
    recv_sem,
):
    dp, core = lax.axis_index("dp"), lax.axis_index("head")
    loads = [
        pltpu.make_async_copy(source, target, load_sem.at[i])
        for i, (source, target) in enumerate(
            ((tokens_hbm, tokens), (w_in_hbm, w_in), (w_fo_hbm, w_fo), (teacher_hbm, teacher))
        )
    ]
    for one in loads:
        one.start()
    greet([(dp, 1 - core)])
    tiles = tokens.shape[0] // TILE
    units, width = w_in.shape[1], w_in.shape[0]
    sums[...] = jnp.zeros_like(sums)
    unit_sum[...] = jnp.zeros_like(unit_sum)
    hidden_gate = hidden_gate_ref[...]
    gate0, gate1 = hidden_gate * gates_ref[0], hidden_gate * gates_ref[1]
    gain1, bias1, gain2, bias2 = (norm_ref[i : i + 1, :] for i in range(4))

    def rows(t):
        return pl.ds(pl.multiple_of(t * TILE, TILE), TILE)

    def lanes(n):
        return pl.ds(n * PART, PART)

    def exchange(step, t):
        source, target = ((own1, got1), (own2, got2), (own2, got3))[step]
        return pltpu.make_async_remote_copy(
            src_ref=source.at[rows(t)],
            dst_ref=target.at[rows(t)],
            send_sem=send_sem.at[step, t],
            recv_sem=recv_sem.at[step, t],
            device_id=(dp, 1 - core),
            device_id_type=MESH,
        )

    def tile_copy(which, t):
        source, target = ((own1, student_hbm), (d_res, d_res1_hbm), (d_context, d_context_hbm))[
            which
        ]
        return pltpu.make_async_copy(
            source.at[rows(t)], target.at[rows(t)], tile_sem.at[which, t]
        )

    def phase1(t, _):
        part = mul(context_ref[rows(t)], w_out_ref[...], NT)
        own1[rows(t)] = part.astype(jnp.bfloat16)
        exchange(0, t).start()

    lax.fori_loop(0, tiles, phase1, None)
    loads[0].wait()
    loads[1].wait()
    loads[2].wait()

    def summed(source, target, t):
        return source[rows(t)].astype(jnp.float32) + target[rows(t)].astype(jnp.float32)

    def phase2(t, _):
        exchange(0, t).wait()
        rows_in = tokens[rows(t)].astype(jnp.float32) + summed(own1, got1, t) * gate0
        normal, scale = normalize(rows_in)
        normal1[rows(t)] = normal
        scale1[rows(t)] = scale
        hidden = normal * gain1 + bias1
        low = hidden.astype(jnp.bfloat16)
        hidden_t[:, rows(t)] = jnp.transpose(hidden).astype(jnp.bfloat16)
        for n in range(units // PART):
            up = mul(low, w_in[:, lanes(n)])
            below, density = normal_parts(up)
            gate = unit_gate_ref[:, lanes(n)]
            gated[rows(t), lanes(n)] = (up * below * gate).astype(jnp.bfloat16)
            slope[rows(t), lanes(n)] = ((below + density) * gate).astype(jnp.bfloat16)
        part = mul(gated[rows(t)], w_fo[...], NT)
        own2[rows(t)] = part.astype(jnp.bfloat16)
        exchange(1, t).start()

    lax.fori_loop(0, tiles, phase2, None)
    loads[3].wait()

    def phase3(t, _):
        exchange(1, t).wait()
        ffn = summed(own2, got2, t)
        hidden = normal1[rows(t)] * gain1 + bias1
        normal, scale = normalize(hidden + ffn * gate1)
        student = normal * gain2 + bias2
        student_tile = student.astype(jnp.bfloat16)
        got2[rows(t)] = student_tile
        row = t // (ROW // TILE)
        end = lengths_ref[row, 0]
        for k in range(1, lengths_ref.shape[1]):
            end = end + lengths_ref[row, k]
        position = lax.broadcasted_iota(jnp.int32, (TILE, 1), 0) + (t % (ROW // TILE)) * TILE
        valid = (position < end).astype(jnp.float32)
        d_out = valid * (student - teacher[rows(t)].astype(jnp.float32))
        d_res2 = norm_back(d_out, normal, scale, gain2)
        d_res[rows(t)] = d_res2
        sums[2] += fold(d_out * normal)
        sums[3] += fold(d_out)
        sums[5] += fold(d_res2 * ffn)
        d_ffn = d_res2 * gate1
        d_ffn_t[:, rows(t)] = jnp.transpose(d_ffn).astype(jnp.bfloat16)
        d_ffn = d_ffn.astype(jnp.bfloat16)
        for n in range(units // PART):
            d_gated = mul(d_ffn, w_fo[:, lanes(n)])
            unit_sum[:, lanes(n)] += fold(
                d_gated * gated[rows(t), lanes(n)].astype(jnp.float32)
            )
            d_up = d_gated * slope[rows(t), lanes(n)].astype(jnp.float32)
            slope[rows(t), lanes(n)] = d_up.astype(jnp.bfloat16)
        part = mul(slope[rows(t)], w_in[...], NT)
        own2[rows(t)] = part.astype(jnp.bfloat16)
        exchange(2, t).start()
        pltpu.make_async_copy(
            got2.at[rows(t)], student_hbm.at[rows(t)], tile_sem.at[0, t]
        ).start()

    lax.fori_loop(0, tiles, phase3, None)

    def wide(which, n):
        target = grads_hbm.at[:, pl.ds(which * units + n * PART, PART)]
        return pltpu.make_async_copy(
            grad_wide.at[which, :, lanes(n)], target, grad_sem.at[which, n]
        )

    for n in range(units // PART):
        grad_wide[0, :, lanes(n)] = mul(d_ffn_t[...], gated[:, lanes(n)]).astype(jnp.bfloat16)
        wide(0, n).start()

    def phase4(t, _):
        exchange(2, t).wait()
        normal = normal1[rows(t)]
        d_hidden = d_res[rows(t)] + summed(own2, got3, t)
        sums[0] += fold(d_hidden * normal)
        sums[1] += fold(d_hidden)
        d_res1 = norm_back(d_hidden, normal, scale1[rows(t)], gain1)
        d_res[rows(t)] = d_res1
        tile_copy(1, t).start()
        sums[4] += fold(d_res1 * summed(own1, got1, t))
        d_attn = d_res1 * gate0
        d_attn_t[:, rows(t)] = jnp.transpose(d_attn).astype(jnp.bfloat16)
        d_context[rows(t)] = mul(d_attn.astype(jnp.bfloat16), w_out_ref[...])
        tile_copy(2, t).start()

    lax.fori_loop(0, tiles, phase4, None)
    for n in range(units // PART):
        grad_wide[1, :, lanes(n)] = mul(hidden_t[...], slope[:, lanes(n)]).astype(jnp.bfloat16)
        wide(1, n).start()
    grad_out[...] = mul(d_attn_t[...], context_ref[...]).astype(jnp.bfloat16)
    last = pltpu.make_async_copy(
        grad_out, grads_hbm.at[:, pl.ds(2 * units, grad_out.shape[1])], grad_sem.at[2, 0]
    )
    last.start()

    def line(i):
        return jnp.sum(sums[i], axis=0, keepdims=True)

    for i in range(4):
        small_ref[i : i + 1, :] = line(i)
    attn_line, ffn_line = line(4), line(5)
    small_ref[4:5, :] = ffn_line * gates_ref[1] + attn_line * gates_ref[0]
    unit_line = jnp.sum(unit_sum[...], axis=0, keepdims=True) / unit_gate_ref[...]
    for i in range(units // width):
        small_ref[5 + i : 6 + i, :] = unit_line[:, i * width : (i + 1) * width]
    lane = lax.broadcasted_iota(jnp.int32, (1, width), 1)
    layer0 = jnp.sum(attn_line * hidden_gate, axis=1, keepdims=True)
    layer1 = jnp.sum(ffn_line * hidden_gate, axis=1, keepdims=True)
    small_ref[7:8, :] = jnp.where(lane == 128, layer0, jnp.where(lane == 129, layer1, 0.0))

    def finish(t, _):
        pltpu.make_async_copy(
            got2.at[rows(t)], student_hbm.at[rows(t)], tile_sem.at[0, t]
        ).wait()
        tile_copy(1, t).wait()
        tile_copy(2, t).wait()

    lax.fori_loop(0, tiles, finish, None)
    for n in range(units // PART):
        wide(0, n).wait()
        wide(1, n).wait()
    last.wait()


def ffn(lengths, layer_gates, norm_p, hidden_gate, unit_gate, context, w_out_t, tokens, teacher, w_in, w_fo_t):
    count, width = tokens.shape
    units, heads = w_in.shape[1], context.shape[1]
    tiles = count // TILE
    vmem, smem = pl.BlockSpec(memory_space=pltpu.VMEM), pl.BlockSpec(memory_space=pltpu.SMEM)
    anywhere = pl.BlockSpec(memory_space=pl.ANY)
    low, full = jnp.bfloat16, jnp.float32
    return pl.pallas_call(
        ffn_kernel,
        in_specs=[smem, smem] + [vmem] * 5 + [anywhere] * 4,
        out_specs=[anywhere] * 4 + [vmem],
        out_shape=[
            jax.ShapeDtypeStruct((count, width), low),
            jax.ShapeDtypeStruct((count, width), full),
            jax.ShapeDtypeStruct((count, heads), full),
            jax.ShapeDtypeStruct((width, 2 * units + heads), low),
            jax.ShapeDtypeStruct((8, width), full),
        ],
        scratch_shapes=[
            pltpu.VMEM((width, units), low),
            pltpu.VMEM((width, units), low),
            pltpu.VMEM((count, width), low),
            pltpu.VMEM((count, width), low),
            *[pltpu.VMEM((count, width), low)] * 5,
            pltpu.VMEM((count, width), full),
            pltpu.VMEM((count, 1), full),
            pltpu.VMEM((count, units), low),
            pltpu.VMEM((count, units), low),
            pltpu.VMEM((count, width), full),
            pltpu.VMEM((count, heads), full),
            *[pltpu.VMEM((width, count), low)] * 3,
            pltpu.VMEM((2, width, units), low),
            pltpu.VMEM((width, heads), low),
            pltpu.VMEM((6, 8, width), full),
            pltpu.VMEM((8, units), full),
            pltpu.SemaphoreType.DMA((4,)),
            pltpu.SemaphoreType.DMA((3, tiles)),
            pltpu.SemaphoreType.DMA((3, units // PART)),
            pltpu.SemaphoreType.DMA((3, tiles)),
            pltpu.SemaphoreType.DMA((3, tiles)),
        ],
        compiler_params=pltpu.CompilerParams(
            collective_id=4, has_side_effects=True, vmem_limit_bytes=60 << 20
        ),
        name="ffn",
    )(lengths, layer_gates, norm_p, hidden_gate[None, :], unit_gate[None, :], context, w_out_t, tokens, teacher, w_in, w_fo_t)


def lamb_moments(master, first, second, grad, decay):
    new_first = MOMENT_DECAY * first + (1.0 - MOMENT_DECAY) * grad
    new_second = MOMENT_DECAY * second + (1.0 - MOMENT_DECAY) * grad * grad
    correction = 1.0 - MOMENT_DECAY**STEP_COUNT
    update = (
        new_first / correction / (jnp.sqrt(new_second / correction) + LAMB_EPS) + decay * master
    )
    return (new_first, new_second, update)


BLOCK = 384


def tail_kernel(
    lengths_ref,
    gate_ref,
    small_ref,
    stats_ref,
    norms_ref,
    *refs,
):
    params, refs = refs[:12], refs[12:]
    (
        grads_hbm,
        qkv_hbm,
        mix_hbm,
        d_context_hbm,
        tokens_hbm,
        w_qkv_hbm,
        d_res1_hbm,
        grad_tokens_hbm,
        sums_ref,
        small_out,
        norm_out,
        total_out,
        grads,
        qkv,
        mix,
        d_context,
        tokens,
        w_qkv,
        d_res,
        d_qkv,
        tokens_t,
        own,
        got,
        heads,
        get1,
        put2,
        get2,
        keep,
        put3,
        get3,
        small_plane,
        small_mine,
        small_line,
        norm_plane,
        norm_mine,
        norm_line,
        load_sem,
        out_sem,
        own_send,
        own_recv,
        send_sem,
        recv_sem,
        small_send,
        small_recv,
    ) = refs
    me, core = lax.axis_index("dp"), lax.axis_index("head")
    z, y, x = place(me)
    rows = sums_ref.shape[0]
    early, blocks = grads_hbm.shape[1] // BLOCK, sums_ref.shape[1] // BLOCK
    loads = [
        pltpu.make_async_copy(source, target, load_sem.at[i])
        for i, (source, target) in enumerate(
            (
                (grads_hbm, grads.at[:, : early * BLOCK]),
                (qkv_hbm, qkv),
                (d_context_hbm, d_context),
                (mix_hbm, mix),
                (tokens_hbm, tokens),
                (w_qkv_hbm, w_qkv),
                (d_res1_hbm, d_res),
            )
        )
    ]
    for one in loads:
        one.start()
    line_peers = [index(lax.rem(z + d, NZ), y, x) for d in (1, 2, 3)]
    plane_peers = [
        index(z, y + (1 - 2 * y) * (d // 2), x + (1 - 2 * x) * (d % 2)) for d in (0, 1, 2, 3)
    ]
    greet(
        [(p, core) for p in line_peers + plane_peers[1:]] + [(p, 1 - core) for p in plane_peers]
    )

    def rows_of(device):
        return pl.ds(pl.multiple_of(device * rows, rows), rows)

    def columns(c):
        return pl.ds(pl.multiple_of(c * BLOCK, BLOCK), BLOCK)

    def turned(c, rz, ra, rb):
        odd = c % 2
        flip_x = ra * (1 - odd) + rb * odd
        flip_y = rb * (1 - odd) + ra * odd
        return index(lax.rem(z + rz, NZ), y + (1 - 2 * y) * flip_y, x + (1 - 2 * x) * flip_x)

    def remote(source, target, c, k, to):
        return pltpu.make_async_remote_copy(
            src_ref=source,
            dst_ref=target,
            send_sem=send_sem.at[c, k],
            recv_sem=recv_sem.at[c, k],
            device_id=(to, core),
            device_id_type=MESH,
        )

    depth = (1, 3, 2, 0)

    def leg1(c, k):
        block = rows_of(turned(c, k % NZ, k // NZ, 1))
        return remote(grads.at[block, columns(c)], get1.at[c, k], c, k, turned(c, 0, 0, 1))

    def leg2(c, rz):
        return remote(put2.at[c, rz], get2.at[c, rz], c, 8 + rz, turned(c, 0, 1, 0))

    def leg3(c, rz):
        there = NZ - rz
        to = index(lax.rem(z + rz, NZ), y, x)
        return remote(put3.at[c, rz - 1], get3.at[c, there - 1], c, 11 + there, to)

    def first(c):
        for ra in (1, 0):
            for rz in depth:
                leg1(c, rz + NZ * ra).start()

    def second(c):
        for ra in (1, 0):
            for rz in depth:
                k = rz + NZ * ra
                leg1(c, k).wait_recv()
                block = rows_of(turned(c, rz, ra, 0))
                total = grads[block, columns(c)].astype(jnp.float32) + get1[c, k].astype(
                    jnp.float32
                )
                if ra:
                    put2[c, rz] = total.astype(jnp.bfloat16)
                    leg2(c, rz).start()
                else:
                    keep[c, rz] = total

    def third(c):
        for rz in depth:
            leg2(c, rz).wait_recv()
            total = keep[c, rz] + get2[c, rz].astype(jnp.float32)
            if rz:
                put3[c, rz - 1] = total.astype(jnp.bfloat16)
                leg3(c, rz).start()
            else:
                keep[c, 0] = total

    def last(c):
        total = keep[c, 0]
        for rz in (1, 2, 3):
            leg3(c, rz).wait_recv()
        for at in range(3):
            total = total + get3[c, at].astype(jnp.float32)
        sums_ref[:, columns(c)] = total

    def each(action, begin, end):
        lax.fori_loop(begin, end, lambda c, _: action(c), None)

    heads[...] = jnp.zeros_like(heads)
    loads[0].wait()
    each(first, 0, 4)
    for one in loads[1:]:
        one.wait()

    def exchange(r):
        here = pl.ds(pl.multiple_of(r * ROW, ROW), ROW)
        return pltpu.make_async_remote_copy(
            src_ref=own.at[here],
            dst_ref=got.at[here],
            send_sem=own_send.at[r],
            recv_sem=own_recv.at[r],
            device_id=(me, 1 - core),
            device_id_type=MESH,
        )

    width = qkv.shape[1] // 3

    def attend(r, _):
        here = pl.ds(pl.multiple_of(r * ROW, ROW), ROW)
        same = segments(lengths_ref, r, (ROW, 1), 0) == segments(lengths_ref, r, (1, ROW), 1)
        tokens_t[:, here] = jnp.transpose(tokens[here].astype(jnp.float32)).astype(jnp.bfloat16)
        for pair in range(width // PAIR):
            lanes = slice(pair * PAIR, (pair + 1) * PAIR)
            heads[:, lanes] += fold(d_context[here, lanes] * mix[here, lanes])
            parts = attend_back(
                same,
                gate_ref[:, lanes],
                *(qkv[here, part * width + pair * PAIR : part * width + (pair + 1) * PAIR] for part in range(3)),
                stats_ref[r, pair],
                d_context[here, lanes],
            )
            for part, value in enumerate(parts):
                start = part * width + pair * PAIR
                d_qkv[here, start : start + PAIR] = value.astype(jnp.bfloat16)
        part = mul(d_qkv[here], w_qkv[...], NT)
        own[here] = part.astype(jnp.bfloat16)
        exchange(r).start()
        each(second, 2 * r, 2 * r + 2)
        each(first, 2 * r + 4, jnp.minimum(2 * r + 6, early))

        @pl.when(r > 0)
        def _():
            each(third, 2 * r - 2, 2 * r)

        @pl.when(r > 1)
        def _():
            each(last, 2 * r - 4, 2 * r - 2)

    tall = tokens.shape[0] // ROW
    lax.fori_loop(0, tall, attend, None)

    def weigh(c, _):
        part = pl.ds(pl.multiple_of((c - early) * BLOCK, BLOCK), BLOCK)
        grads[:, columns(c)] = mul(tokens_t[...], d_qkv[:, part]).astype(jnp.bfloat16)
        first(c)

    lax.fori_loop(early, blocks, weigh, None)

    here_plane = y * NX + x
    small_plane[here_plane] = small_ref[...]
    line = jnp.sum(heads[...], axis=0, keepdims=True)
    lane = lax.broadcasted_iota(jnp.int32, (1, small_ref.shape[1]), 1)
    extra = small_ref[7:8, :]
    for head in range(width // HEAD_DIM):
        value = jnp.sum(line[:, head * HEAD_DIM : (head + 1) * HEAD_DIM], axis=1, keepdims=True)
        extra = jnp.where(lane == head, value, extra)
    small_plane[here_plane, 7:8, :] = extra

    def spread(plane, base, to, to_core, at):
        return pltpu.make_async_remote_copy(
            src_ref=plane.at[at],
            dst_ref=plane.at[at],
            send_sem=small_send.at[base],
            recv_sem=small_recv.at[base],
            device_id=(to, to_core),
            device_id_type=MESH,
        )

    def swap(plane, base, targets, at):
        copies = [
            spread(plane, base + i, to, to_core, at) for i, (to, to_core) in enumerate(targets)
        ]
        for one in copies:
            one.start()
        return copies

    sent = swap(small_plane, 0, [(p, core) for p in plane_peers[1:]], here_plane)
    each(second, 2 * tall, early)
    each(third, 2 * tall - 2, 2 * tall)
    each(last, 2 * tall - 4, 2 * tall - 2)
    each(third, 2 * tall, early)

    def finish(r, _):
        here = pl.ds(pl.multiple_of(r * ROW, ROW), ROW)
        exchange(r).wait()
        d_res[here] += own[here].astype(jnp.float32) + got[here].astype(jnp.float32)
        pltpu.make_async_copy(d_res.at[here], grad_tokens_hbm.at[here], out_sem.at[r]).start()

    lax.fori_loop(0, tall, finish, None)
    for one in sent:
        one.wait_recv()
    total = small_plane[0]
    for at in range(1, NX * NY):
        total = total + small_plane[at]
    small_line[z] = total
    sent_line = swap(small_line, 3, [(p, core) for p in line_peers], z)
    each(second, early, blocks)
    each(last, 2 * tall - 2, early)
    for one in sent_line:
        one.wait_recv()
    total = small_line[0]
    for at in range(1, NZ):
        total = total + small_line[at]
    small_out[...] = total
    norm_grad = pltpu.roll(total, (total.shape[1] - me * rows) % total.shape[1], 1)[:, :128]
    norm_out[...] = norm_grad
    each(third, early, blocks)

    row8 = lax.broadcasted_iota(jnp.int32, (8, 128), 0)
    lane8 = lax.broadcasted_iota(jnp.int32, (8, 128), 1)

    def put(tile, row, weight, update):
        here = row8 == row
        return jnp.where(here & (lane8 == 0), weight, jnp.where(here & (lane8 == 1), update, tile))

    def square(block):
        return jnp.sum(jnp.sum(block * block, axis=0, keepdims=True), axis=1, keepdims=True)

    tile = jnp.zeros((8, 128), jnp.float32)
    master, first_moment, second_moment = (norms_ref[i] for i in range(3))
    update = lamb_moments(master, first_moment, second_moment, norm_grad[:4, : master.shape[1]], 0.0)[2]
    for i in range(4):
        tile = put(tile, 4 + i, 0.5 * square(master[i : i + 1]), 0.5 * square(update[i : i + 1]))
    start = 0
    for row, p in ((3, 3), (2, 2), (1, 1)):
        master = params[p][...]
        span = slice(start, start + master.shape[1])
        update = lamb_moments(master, params[4 + p][...], params[8 + p][...], sums_ref[:, span], WEIGHT_DECAY)[2]
        tile = put(tile, row, square(master), square(update))
        start += master.shape[1]
    weights, updates = 0.0, 0.0
    each(last, early, blocks)
    for j in range(3):
        master = params[0][j]
        span = slice(start + j * width, start + (j + 1) * width)
        update = lamb_moments(master, params[4][j], params[8][j], sums_ref[:, span], WEIGHT_DECAY)[2]
        weights, updates = weights + square(master), updates + square(update)
    tile = put(tile, 0, weights, updates)
    here_cores = core * (NX * NY) + here_plane
    norm_plane[here_cores] = tile
    targets = [(p, core) for p in plane_peers[1:]] + [(p, 1 - core) for p in plane_peers]
    sent_tile = swap(norm_plane, 6, targets, here_cores)
    for one in sent_tile:
        one.wait_recv()
    total = norm_plane[0]
    for at in range(1, 2 * NX * NY):
        total = total + norm_plane[at]
    norm_line[z] = total
    sent_last = swap(norm_line, 13, [(p, core) for p in line_peers], z)
    for one in sent_last:
        one.wait_recv()
    total = norm_line[0]
    for at in range(1, NZ):
        total = total + norm_line[at]
    total_out[...] = total
    for one in (*sent, *sent_line, *sent_tile, *sent_last):
        one.wait_send()

    def drain(c, _):
        for k in range(8):
            leg1(c, k).wait_send()
        for rz in range(NZ):
            leg2(c, rz).wait_send()
        for rz in (1, 2, 3):
            leg3(c, rz).wait_send()

    lax.fori_loop(0, blocks, drain, None)

    def drain_rows(r, _):
        here = pl.ds(pl.multiple_of(r * ROW, ROW), ROW)
        pltpu.make_async_copy(d_res.at[here], grad_tokens_hbm.at[here], out_sem.at[r]).wait()

    lax.fori_loop(0, tall, drain_rows, None)


def tail(lengths, gate_lanes, small_rows, stats, norms, params, grads, qkv, mix, d_context, tokens, w_qkv, d_res1):
    count, width = tokens.shape
    heads3, rows = qkv.shape[1], norms.shape[2]
    columns = grads.shape[1] + heads3
    tall, blocks = count // ROW, columns // BLOCK
    vmem, smem = pl.BlockSpec(memory_space=pltpu.VMEM), pl.BlockSpec(memory_space=pltpu.SMEM)
    anywhere = pl.BlockSpec(memory_space=pl.ANY)
    low, full = jnp.bfloat16, jnp.float32
    landing = lambda n, kind: pltpu.VMEM((blocks, n, rows, BLOCK), kind)
    return pl.pallas_call(
        tail_kernel,
        in_specs=[smem] + [vmem] * (4 + len(params)) + [anywhere] * 7,
        out_specs=[anywhere] + [vmem] * 4,
        out_shape=[
            jax.ShapeDtypeStruct((count, width), full),
            jax.ShapeDtypeStruct((rows, columns), full),
            jax.ShapeDtypeStruct((8, width), full),
            jax.ShapeDtypeStruct((8, 128), full),
            jax.ShapeDtypeStruct((8, 128), full),
        ],
        scratch_shapes=[
            pltpu.VMEM((width, columns), low),
            pltpu.VMEM((count, heads3), low),
            pltpu.VMEM((count, heads3 // 3), full),
            pltpu.VMEM((count, heads3 // 3), full),
            pltpu.VMEM((count, width), low),
            pltpu.VMEM((width, heads3), low),
            pltpu.VMEM((count, width), full),
            pltpu.VMEM((count, heads3), low),
            pltpu.VMEM((width, count), low),
            pltpu.VMEM((count, width), low),
            pltpu.VMEM((count, width), low),
            pltpu.VMEM((8, heads3 // 3), full),
            landing(8, low),
            landing(NZ, low),
            landing(NZ, low),
            landing(NZ, full),
            landing(3, low),
            landing(3, low),
            pltpu.VMEM((NX * NY, 8, width), full),
            pltpu.VMEM((8, width), full),
            pltpu.VMEM((NZ, 8, width), full),
            pltpu.VMEM((2 * NX * NY, 8, 128), full),
            pltpu.VMEM((8, 128), full),
            pltpu.VMEM((NZ, 8, 128), full),
            pltpu.SemaphoreType.DMA((7,)),
            pltpu.SemaphoreType.DMA((tall,)),
            pltpu.SemaphoreType.DMA((tall,)),
            pltpu.SemaphoreType.DMA((tall,)),
            pltpu.SemaphoreType.DMA((blocks, 15)),
            pltpu.SemaphoreType.DMA((blocks, 15)),
            pltpu.SemaphoreType.DMA((16,)),
            pltpu.SemaphoreType.DMA((16,)),
        ],
        compiler_params=pltpu.CompilerParams(
            collective_id=5, has_side_effects=True, vmem_limit_bytes=61 << 20
        ),
        name="tail",
    )(lengths, gate_lanes, small_rows, stats, norms, *params, grads, qkv, mix, d_context, tokens, w_qkv, d_res1)


def update_kernel(order, sums_ref, small_ref, norm_ref, total_ref, norms_ref, *refs):
    params, outs = refs[:12], refs[12:]
    weight_norm = jnp.sqrt(total_ref[:, 0:1])
    update_norm = jnp.sqrt(total_ref[:, 1:2])
    trust = weight_norm / update_norm

    def step(row, targets, at, values, decay):
        master, first_moment, second_moment, grad = values
        new_first, new_second, update = lamb_moments(
            master, first_moment, second_moment, grad, decay
        )
        new_master = master - LEARN_RATE * trust[row] * update
        made = (grad, new_first, new_second, new_master, new_master.astype(jnp.bfloat16))
        for target, value in zip(targets, made, strict=True):
            target[at] = value

    start = 0
    for p in order:
        master = params[p]
        width = master.shape[-1]
        targets = outs[5 * p : 5 * p + 5]
        for j in range(3 if p == 0 else 1):
            at = (j,) if p == 0 else (Ellipsis,)
            grad = sums_ref[:, start : start + width]
            values = (*(params[4 * i + p][at] for i in range(3)), grad)
            step(slice(p, p + 1), targets, at, values, WEIGHT_DECAY)
            start += width
    norm_grad = norm_ref[:4, : norms_ref.shape[2]]
    values = (*(norms_ref[i] for i in range(3)), norm_grad)
    step(slice(4, 8), outs[20:25], (Ellipsis,), values, 0.0)
    stats_out, heads_out, units_out, hidden_out, layers_out = outs[25:]
    lane = lax.broadcasted_iota(jnp.int32, (8, 128), 1)
    stats_out[...] = jnp.where(lane == 0, weight_norm, jnp.where(lane == 1, update_norm, trust))
    heads_out[...] = small_ref[7:8, : heads_out.shape[1]]
    width = small_ref.shape[1]
    for i in range(units_out.shape[1] // width):
        units_out[:, i * width : (i + 1) * width] = small_ref[5 + i : 6 + i, :]
    hidden_out[...] = small_ref[4:5, :]
    layers_out[...] = small_ref[7:8, 128:130]


def update(sums, small, norm_grad, totals, norms, params, sizes):
    vmem = pl.BlockSpec(memory_space=pltpu.VMEM)
    shapes = []
    for master in params[:4]:
        shapes += [jax.ShapeDtypeStruct(master.shape, jnp.float32)] * 4
        shapes += [jax.ShapeDtypeStruct(master.shape, jnp.bfloat16)]
    shapes += [jax.ShapeDtypeStruct(norms.shape[1:], jnp.float32)] * 4
    shapes += [jax.ShapeDtypeStruct(norms.shape[1:], jnp.bfloat16)]
    shapes += [jax.ShapeDtypeStruct((8, 128), jnp.float32)]
    shapes += [jax.ShapeDtypeStruct((1, size), jnp.float32) for size in sizes]
    return pl.pallas_call(
        functools.partial(update_kernel, (3, 2, 1, 0)),
        in_specs=[vmem] * (5 + len(params)),
        out_specs=[vmem] * len(shapes),
        out_shape=shapes,
        compiler_params=pltpu.CompilerParams(vmem_limit_bytes=48 << 20),
        name="update",
    )(sums, small, norm_grad, totals, norms, *params)


def core_sum(part):
    part = part.astype(jnp.bfloat16)
    other = lax.ppermute(part, "head", [(0, 1), (1, 0)])
    return part.astype(jnp.float32) + other.astype(jnp.float32)


def plain_totals(sums, norm_grad, norms, params, head_count):
    pairs, start = [None] * 4, 0
    for p in (3, 2, 1, 0):
        master, first_moment, second_moment = params[p], params[4 + p], params[8 + p]
        width = master.size // norms.shape[2]
        grad = sums[:, start : start + width]
        if p == 0:
            grad = jnp.stack(jnp.split(grad, 3, axis=1))
        update = lamb_moments(master, first_moment, second_moment, grad, WEIGHT_DECAY)[2]
        pairs[p] = jnp.stack([jnp.sum(master * master), jnp.sum(update * update)])
        start += width
    master, first_moment, second_moment = norms
    update = lamb_moments(master, first_moment, second_moment, norm_grad[:4, : norms.shape[2]], 0.0)[2]
    rows = jnp.stack([jnp.sum(master * master, axis=1), jnp.sum(update * update, axis=1)], axis=1)
    found = jnp.concatenate([jnp.stack(pairs), rows / head_count])
    return jnp.pad(lax.psum(found, ("dp", "head")), ((0, 0), (0, 126)))


def rows_first(qkv):
    return jnp.transpose(qkv, (1, 0, 2))


def local(
    tokens,
    teacher,
    lengths,
    head_gate,
    unit_gate,
    hidden_gate,
    layer_gates,
    master_qkv,
    first_qkv,
    second_qkv,
    master_attn_out,
    first_attn_out,
    second_attn_out,
    master_ffn_in,
    first_ffn_in,
    second_ffn_in,
    master_ffn_out,
    first_ffn_out,
    second_ffn_out,
    master_norms,
    first_norms,
    second_norms,
):
    heads_here = head_gate.shape[0]
    local_width = heads_here * HEAD_DIM
    head_count = lax.axis_size("head")
    ours = lax.axis_size("dp") == GRID and head_count == 2
    shard = master_qkv.shape[0]
    shards = [
        master_qkv.astype(jnp.bfloat16).reshape(shard, 3 * local_width),
        master_attn_out.T.astype(jnp.bfloat16),
        master_ffn_in.astype(jnp.bfloat16),
        master_ffn_out.T.astype(jnp.bfloat16),
        jnp.pad(master_norms.T, ((0, 0), (0, 124))).astype(jnp.bfloat16),
    ]
    if ours:
        w_qkv, w_out_t, w_in, w_fo_t, norm_t = gather(shards)
    else:
        w_qkv, w_out_t, w_in, w_fo_t, norm_t = (
            lax.all_gather(s, "dp", axis=0, tiled=True) for s in shards
        )
    norm_p = norm_t[:, :4].T.astype(jnp.float32)
    gate_lanes = jnp.repeat(head_gate, HEAD_DIM)[None, :]
    qkv = jnp.dot(tokens, w_qkv, preferred_element_type=jnp.float32).astype(jnp.bfloat16)
    head_mix, context, stats = attention(qkv, lengths, gate_lanes)
    student_low, d_res1, d_context, grads, small_rows = ffn(
        lengths,
        layer_gates,
        norm_p,
        hidden_gate,
        unit_gate,
        context,
        w_out_t,
        tokens,
        teacher,
        w_in,
        w_fo_t,
    )
    params = [
        rows_first(master_qkv),
        master_attn_out.T,
        master_ffn_in,
        master_ffn_out.T,
        rows_first(first_qkv),
        first_attn_out.T,
        first_ffn_in,
        first_ffn_out.T,
        rows_first(second_qkv),
        second_attn_out.T,
        second_ffn_in,
        second_ffn_out.T,
    ]
    norms = jnp.stack([master_norms, first_norms, second_norms])
    if ours:
        grad_tokens, sums, small, norm_grad, totals = tail(
            lengths,
            gate_lanes,
            small_rows,
            stats,
            norms,
            params,
            grads,
            qkv,
            head_mix,
            d_context,
            tokens,
            w_qkv,
            d_res1,
        )
    else:
        d_qkv, head_sums = attention_back(qkv, lengths, gate_lanes, stats, head_mix, d_context)
        d_heads = jnp.sum(
            head_sums[:, :, 0, :].reshape(-1, heads_here, HEAD_DIM), axis=(0, 2)
        )
        grad_qkv = jnp.einsum("tc,tk->ck", tokens, d_qkv, preferred_element_type=jnp.float32)
        input_part = jnp.einsum("tk,ck->tc", d_qkv, w_qkv, preferred_element_type=jnp.float32)
        grad_tokens = d_res1 + core_sum(input_part)
        grads = jnp.concatenate([grads.astype(jnp.float32), grad_qkv], axis=1)
        sums = lax.psum_scatter(grads, "dp", scatter_dimension=0, tiled=True)
        small = lax.psum(small_rows.at[7, :heads_here].set(d_heads), "dp")
        start = lax.axis_index("dp") * shard
        norm_grad = lax.dynamic_slice_in_dim(small, start, shard, 1)
        norm_grad = jnp.pad(norm_grad, ((0, 0), (0, 128 - shard)))
        totals = plain_totals(sums, norm_grad, norms, params, head_count)
    made = update(
        sums, small, norm_grad, totals, norms, params, (heads_here, unit_gate.shape[0], D, 2)
    )
    results = []
    for p in range(4):
        for value in made[5 * p : 5 * p + 5]:
            results.append(rows_first(value) if p == 0 else value if p == 2 else value.T)
    norm_results, (stats_rows, *gate_rows) = made[20:25], made[25:]
    gate_results = [row.reshape(-1) for row in gate_rows]
    return (
        student_low,
        grad_tokens,
        *gate_results,
        *results,
        *norm_results,
        stats_rows[:, :3].T,
    )


def solution(mesh):
    return jax.shard_map(
        local,
        mesh=mesh,
        in_specs=(
            P("dp", None),
            P("dp", None),
            P("dp", None),
            P("head"),
            P("head"),
            P(),
            P(),
            P("dp", None, "head"),
            P("dp", None, "head"),
            P("dp", None, "head"),
            P("head", "dp"),
            P("head", "dp"),
            P("head", "dp"),
            P("dp", "head"),
            P("dp", "head"),
            P("dp", "head"),
            P("head", "dp"),
            P("head", "dp"),
            P("head", "dp"),
            P(None, "dp"),
            P(None, "dp"),
            P(None, "dp"),
        ),
        out_specs=(
            P("dp", None),
            P("dp", None),
            P("head"),
            P("head"),
            P(),
            P(),
            P("dp", None, "head"),
            P("dp", None, "head"),
            P("dp", None, "head"),
            P("dp", None, "head"),
            P("dp", None, "head"),
            P("head", "dp"),
            P("head", "dp"),
            P("head", "dp"),
            P("head", "dp"),
            P("head", "dp"),
            P("dp", "head"),
            P("dp", "head"),
            P("dp", "head"),
            P("dp", "head"),
            P("dp", "head"),
            P("head", "dp"),
            P("head", "dp"),
            P("head", "dp"),
            P("head", "dp"),
            P("head", "dp"),
            P(None, "dp"),
            P(None, "dp"),
            P(None, "dp"),
            P(None, "dp"),
            P(None, "dp"),
            P(),
        ),
        check_vma=False,
    )
```

```python
import functools

import jax
import jax.numpy as jnp
from jax import lax
from jax.experimental import pallas as pl
from jax.experimental.pallas import tpu as pltpu
from jax.sharding import PartitionSpec as P

D = 768
HEAD_DIM = 64
ROW = 512
STEP_COUNT = 5

LN_EPS = 1e-05
LAMB_EPS = 1e-06
WEIGHT_DECAY = 0.01
LEARN_RATE = 0.5
MOMENT_DECAY = 0.5
MASK_FILL = -1000000000.0


MESH = pl.DeviceIdType.MESH
NZ, NY, NX = 4, 2, 2
GRID = NZ * NY * NX


def place(me):
    return me // (NY * NX), (me // NX) % NY, me % NX


def index(z, y, x):
    return (z * NY + y) * NX + x


def slot(rz, ra, rb):
    return rz + NZ * (ra + 2 * rb)


def greet(peers):
    barrier = pltpu.get_barrier_semaphore()
    for peer in peers:
        pl.semaphore_signal(barrier, inc=1, device_id=peer, device_id_type=MESH)
    pl.semaphore_wait(barrier, len(peers))


NT = (((1,), (1,)), ((), ()))
NN = (((1,), (0,)), ((), ()))
PAIR = 2 * HEAD_DIM


def mul(a, b, dims=NN):
    return lax.dot_general(a, b, dims, preferred_element_type=jnp.float32)


def segments(lengths_ref, row, shape, axis):
    positions = lax.broadcasted_iota(jnp.int32, shape, axis)
    end = jnp.int32(0)
    found = jnp.zeros(shape, jnp.int32)
    for k in range(lengths_ref.shape[1]):
        end = end + lengths_ref[row, k]
        found = found + (positions >= end).astype(jnp.int32)
    return found


def flip(block):
    return jnp.transpose(block.astype(jnp.float32)).astype(block.dtype)


def head_lanes(block, head):
    lane = lax.broadcasted_iota(jnp.int32, block.shape, 1)
    inside = (lane < HEAD_DIM) if head == 0 else (lane >= HEAD_DIM)
    return jnp.where(inside, block, jnp.zeros_like(block))


def attend_pair(same, queries, keys, values):
    queries = queries * jnp.bfloat16(HEAD_DIM**-0.5)
    values_t = flip(values)
    mixes, totals = [], []
    for head in (0, 1):
        scores = mul(keys, head_lanes(queries, head), NT)
        scores = jnp.where(same, scores, MASK_FILL)
        top = jnp.max(scores, axis=0, keepdims=True)
        expo = jnp.exp(scores - top)
        total = jnp.sum(expo, axis=0, keepdims=True)
        probs = (expo * (1.0 / total)).astype(jnp.bfloat16)
        mixes.append(mul(values_t[head * HEAD_DIM : (head + 1) * HEAD_DIM], probs))
        totals.append(top + jnp.log(total))
    return jnp.transpose(jnp.concatenate(mixes, axis=0)), totals


def attend_back(same, queries, keys, values, stats, d_mix):
    queries = queries * jnp.bfloat16(HEAD_DIM**-0.5)
    keys_t = flip(keys)
    d_queries, d_keys, d_values, sums = [], None, None, []
    for head in (0, 1):
        q_one, d_one = head_lanes(queries, head), head_lanes(d_mix, head)
        scores = jnp.where(same, mul(keys, q_one, NT), MASK_FILL)
        probs = jnp.exp(scores - stats[head : head + 1, :])
        d_probs = mul(values, d_one, NT)
        weighed = jnp.sum(probs * d_probs, axis=0, keepdims=True)
        sums.append(jnp.sum(weighed, axis=1, keepdims=True))
        d_scores = (probs * (d_probs - weighed)).astype(jnp.bfloat16)
        dv = mul(probs.astype(jnp.bfloat16), d_one)
        dk = mul(d_scores, q_one)
        d_values = dv if head == 0 else d_values + dv
        d_keys = dk if head == 0 else d_keys + dk
        d_queries.append(mul(keys_t[head * HEAD_DIM : (head + 1) * HEAD_DIM], d_scores))
    dq = jnp.transpose(jnp.concatenate(d_queries, axis=0)) * HEAD_DIM**-0.5
    return (dq, d_keys, d_values), sums


def attention_kernel(lengths_ref, gate_ref, qkv_ref, context_ref, stats_ref):
    row = pl.program_id(0)
    same = segments(lengths_ref, row, (ROW, 1), 0) == segments(lengths_ref, row, (1, ROW), 1)
    mix, totals = attend_pair(same, *(qkv_ref[:, i * PAIR : (i + 1) * PAIR] for i in range(3)))
    for head in (0, 1):
        stats_ref[0, 0, head : head + 1, :] = totals[head]
    context_ref[...] = (mix * gate_ref[...]).astype(jnp.bfloat16)


def attention(qkv, lengths, gate_lanes):
    tokens, width = qkv.shape
    rows, pairs = lengths.shape[0], width // 3 // PAIR
    return pl.pallas_call(
        attention_kernel,
        grid=(rows, pairs),
        in_specs=[
            pl.BlockSpec(memory_space=pltpu.SMEM),
            pl.BlockSpec((1, PAIR), lambda r, h: (0, h)),
            pl.BlockSpec((ROW, 3 * PAIR), lambda r, h: (r, h)),
        ],
        out_specs=[
            pl.BlockSpec((ROW, PAIR), lambda r, h: (r, h)),
            pl.BlockSpec((1, 1, 8, ROW), lambda r, h: (r, h, 0, 0)),
        ],
        out_shape=[
            jax.ShapeDtypeStruct((tokens, width // 3), jnp.bfloat16),
            jax.ShapeDtypeStruct((rows, pairs, 8, ROW), jnp.float32),
        ],
        compiler_params=pltpu.CompilerParams(vmem_limit_bytes=32 << 20),
        name="attention",
    )(lengths, gate_lanes, qkv)


def attention_back_kernel(lengths_ref, gate_ref, qkv_ref, stats_ref, d_ref, out_ref, heads_ref):
    row = pl.program_id(0)
    same = segments(lengths_ref, row, (ROW, 1), 0) == segments(lengths_ref, row, (1, ROW), 1)
    gate = gate_ref[...]
    d_mix = (d_ref[...] * gate).astype(jnp.bfloat16)
    parts, weighed = attend_back(
        same, *(qkv_ref[:, i * PAIR : (i + 1) * PAIR] for i in range(3)), stats_ref[0, 0], d_mix
    )
    for i, value in enumerate(parts):
        out_ref[:, i * PAIR : (i + 1) * PAIR] = value.astype(jnp.bfloat16)
    lane = lax.broadcasted_iota(jnp.int32, (8, PAIR), 1)
    found = jnp.zeros((8, PAIR), jnp.float32)
    for head in (0, 1):
        value = weighed[head] / gate[:, head * HEAD_DIM : head * HEAD_DIM + 1]
        found = jnp.where(lane == head, value, found)
    heads_ref[0, 0] = found


def attention_back(qkv, lengths, gate_lanes, stats, d_context):
    tokens, width = qkv.shape
    rows, pairs = lengths.shape[0], width // 3 // PAIR
    wide = pl.BlockSpec((ROW, 3 * PAIR), lambda r, h: (r, h))
    return pl.pallas_call(
        attention_back_kernel,
        grid=(rows, pairs),
        in_specs=[
            pl.BlockSpec(memory_space=pltpu.SMEM),
            pl.BlockSpec((1, PAIR), lambda r, h: (0, h)),
            wide,
            pl.BlockSpec((1, 1, 8, ROW), lambda r, h: (r, h, 0, 0)),
            pl.BlockSpec((ROW, PAIR), lambda r, h: (r, h)),
        ],
        out_specs=[wide, pl.BlockSpec((1, 1, 8, PAIR), lambda r, h: (r, h, 0, 0))],
        out_shape=[
            jax.ShapeDtypeStruct((tokens, width), jnp.bfloat16),
            jax.ShapeDtypeStruct((rows, pairs, 8, PAIR), jnp.float32),
        ],
        compiler_params=pltpu.CompilerParams(vmem_limit_bytes=32 << 20),
        name="attention_back",
    )(lengths, gate_lanes, qkv, stats, d_context)


TILE = 256
PART = 256
TAIL_STEP = 0.3
TAIL = (
    0.11963200569152832,
    0.12071217596530914,
    0.10017567127943039,
    0.1276927888393402,
    -0.052036140114068985,
    0.2045592963695526,
    -0.15616002678871155,
    0.035424139350652695,
)


def normal_parts(u):
    bell = jnp.exp(-0.5 * u * u)
    t = 1.0 / (1.0 + TAIL_STEP * jnp.abs(u))
    series = TAIL[-1]
    for term in TAIL[-2::-1]:
        series = series * t + term
    tail = series * t * bell
    return jnp.where(u < 0, tail, 1.0 - tail), u * bell * 0.3989422804014327


def fold(block):
    return jnp.sum(block.reshape(-1, 8, block.shape[1]), axis=0)


def norm_back(d_out, normal, scale, gain):
    d_normal = d_out * gain
    d_normal = (
        d_normal
        - jnp.mean(d_normal, axis=-1, keepdims=True)
        - normal * jnp.mean(d_normal * normal, axis=-1, keepdims=True)
    )
    return d_normal * scale


def normalize(rows_in):
    center = rows_in - jnp.mean(rows_in, axis=-1, keepdims=True)
    scale = lax.rsqrt(jnp.mean(center * center, axis=-1, keepdims=True) + LN_EPS)
    return center * scale, scale


def ffn_kernel(
    lengths_ref,
    gates_ref,
    norm_ref,
    hidden_gate_ref,
    unit_gate_ref,
    context_ref,
    w_out_ref,
    tokens_hbm,
    teacher_hbm,
    w_in_hbm,
    w_fo_hbm,
    student_hbm,
    d_res1_hbm,
    d_context_hbm,
    grads_hbm,
    small_ref,
    w_in,
    w_fo,
    tokens,
    teacher,
    own1,
    own2,
    got1,
    got2,
    got3,
    normal1,
    scale1,
    gated,
    slope,
    d_res,
    d_context,
    hidden_t,
    d_ffn_t,
    d_attn_t,
    grad_wide,
    grad_out,
    sums,
    unit_sum,
    load_sem,
    tile_sem,
    grad_sem,
    send_sem,
    recv_sem,
):
    dp, core = lax.axis_index("dp"), lax.axis_index("head")
    loads = [
        pltpu.make_async_copy(source, target, load_sem.at[i])
        for i, (source, target) in enumerate(
            ((tokens_hbm, tokens), (w_in_hbm, w_in), (w_fo_hbm, w_fo), (teacher_hbm, teacher))
        )
    ]
    for one in loads:
        one.start()
    greet([(dp, 1 - core)])
    tiles = tokens.shape[0] // TILE
    units, width = w_in.shape[1], w_in.shape[0]
    sums[...] = jnp.zeros_like(sums)
    unit_sum[...] = jnp.zeros_like(unit_sum)
    hidden_gate = hidden_gate_ref[...]
    gate0, gate1 = hidden_gate * gates_ref[0], hidden_gate * gates_ref[1]
    gain1, bias1, gain2, bias2 = (norm_ref[i : i + 1, :] for i in range(4))

    def rows(t):
        return pl.ds(pl.multiple_of(t * TILE, TILE), TILE)

    def lanes(n):
        return pl.ds(n * PART, PART)

    def exchange(step, t):
        source, target = ((own1, got1), (own2, got2), (own2, got3))[step]
        return pltpu.make_async_remote_copy(
            src_ref=source.at[rows(t)],
            dst_ref=target.at[rows(t)],
            send_sem=send_sem.at[step, t],
            recv_sem=recv_sem.at[step, t],
            device_id=(dp, 1 - core),
            device_id_type=MESH,
        )

    def tile_copy(which, t):
        source, target = ((own1, student_hbm), (d_res, d_res1_hbm), (d_context, d_context_hbm))[
            which
        ]
        return pltpu.make_async_copy(
            source.at[rows(t)], target.at[rows(t)], tile_sem.at[which, t]
        )

    def phase1(t, _):
        part = mul(context_ref[rows(t)], w_out_ref[...], NT)
        own1[rows(t)] = part.astype(jnp.bfloat16)
        exchange(0, t).start()

    lax.fori_loop(0, tiles, phase1, None)
    loads[0].wait()
    loads[1].wait()
    loads[2].wait()

    def summed(source, target, t):
        return source[rows(t)].astype(jnp.float32) + target[rows(t)].astype(jnp.float32)

    def phase2(t, _):
        exchange(0, t).wait()
        rows_in = tokens[rows(t)].astype(jnp.float32) + summed(own1, got1, t) * gate0
        normal, scale = normalize(rows_in)
        normal1[rows(t)] = normal
        scale1[rows(t)] = scale
        hidden = normal * gain1 + bias1
        low = hidden.astype(jnp.bfloat16)
        hidden_t[:, rows(t)] = jnp.transpose(hidden).astype(jnp.bfloat16)
        for n in range(units // PART):
            up = mul(low, w_in[:, lanes(n)])
            below, density = normal_parts(up)
            gate = unit_gate_ref[:, lanes(n)]
            gated[rows(t), lanes(n)] = (up * below * gate).astype(jnp.bfloat16)
            slope[rows(t), lanes(n)] = ((below + density) * gate).astype(jnp.bfloat16)
        part = mul(gated[rows(t)], w_fo[...], NT)
        own2[rows(t)] = part.astype(jnp.bfloat16)
        exchange(1, t).start()

    lax.fori_loop(0, tiles, phase2, None)
    loads[3].wait()

    def phase3(t, _):
        exchange(1, t).wait()
        ffn = summed(own2, got2, t)
        hidden = normal1[rows(t)] * gain1 + bias1
        normal, scale = normalize(hidden + ffn * gate1)
        student = normal * gain2 + bias2
        student_tile = student.astype(jnp.bfloat16)
        got2[rows(t)] = student_tile
        row = t // (ROW // TILE)
        end = lengths_ref[row, 0]
        for k in range(1, lengths_ref.shape[1]):
            end = end + lengths_ref[row, k]
        position = lax.broadcasted_iota(jnp.int32, (TILE, 1), 0) + (t % (ROW // TILE)) * TILE
        valid = (position < end).astype(jnp.float32)
        d_out = valid * (student - teacher[rows(t)].astype(jnp.float32))
        d_res2 = norm_back(d_out, normal, scale, gain2)
        d_res[rows(t)] = d_res2
        sums[2] += fold(d_out * normal)
        sums[3] += fold(d_out)
        sums[5] += fold(d_res2 * ffn)
        d_ffn = d_res2 * gate1
        d_ffn_t[:, rows(t)] = jnp.transpose(d_ffn).astype(jnp.bfloat16)
        d_ffn = d_ffn.astype(jnp.bfloat16)
        for n in range(units // PART):
            d_gated = mul(d_ffn, w_fo[:, lanes(n)])
            unit_sum[:, lanes(n)] += fold(
                d_gated * gated[rows(t), lanes(n)].astype(jnp.float32)
            )
            d_up = d_gated * slope[rows(t), lanes(n)].astype(jnp.float32)
            slope[rows(t), lanes(n)] = d_up.astype(jnp.bfloat16)
        part = mul(slope[rows(t)], w_in[...], NT)
        own2[rows(t)] = part.astype(jnp.bfloat16)
        exchange(2, t).start()
        pltpu.make_async_copy(
            got2.at[rows(t)], student_hbm.at[rows(t)], tile_sem.at[0, t]
        ).start()

    lax.fori_loop(0, tiles, phase3, None)

    def wide(which, n):
        target = grads_hbm.at[:, pl.ds(which * units + n * PART, PART)]
        return pltpu.make_async_copy(
            grad_wide.at[which, :, lanes(n)], target, grad_sem.at[which, n]
        )

    for n in range(units // PART):
        grad_wide[0, :, lanes(n)] = mul(d_ffn_t[...], gated[:, lanes(n)]).astype(jnp.bfloat16)
        wide(0, n).start()

    def phase4(t, _):
        exchange(2, t).wait()
        normal = normal1[rows(t)]
        d_hidden = d_res[rows(t)] + summed(own2, got3, t)
        sums[0] += fold(d_hidden * normal)
        sums[1] += fold(d_hidden)
        d_res1 = norm_back(d_hidden, normal, scale1[rows(t)], gain1)
        d_res[rows(t)] = d_res1
        tile_copy(1, t).start()
        sums[4] += fold(d_res1 * summed(own1, got1, t))
        d_attn = d_res1 * gate0
        d_attn_t[:, rows(t)] = jnp.transpose(d_attn).astype(jnp.bfloat16)
        d_context[rows(t)] = mul(d_attn.astype(jnp.bfloat16), w_out_ref[...])
        tile_copy(2, t).start()

    lax.fori_loop(0, tiles, phase4, None)
    for n in range(units // PART):
        grad_wide[1, :, lanes(n)] = mul(hidden_t[...], slope[:, lanes(n)]).astype(jnp.bfloat16)
        wide(1, n).start()
    grad_out[...] = mul(d_attn_t[...], context_ref[...]).astype(jnp.bfloat16)
    last = pltpu.make_async_copy(
        grad_out, grads_hbm.at[:, pl.ds(2 * units, grad_out.shape[1])], grad_sem.at[2, 0]
    )
    last.start()

    def line(i):
        return jnp.sum(sums[i], axis=0, keepdims=True)

    for i in range(4):
        small_ref[i : i + 1, :] = line(i)
    attn_line, ffn_line = line(4), line(5)
    small_ref[4:5, :] = ffn_line * gates_ref[1] + attn_line * gates_ref[0]
    unit_line = jnp.sum(unit_sum[...], axis=0, keepdims=True) / unit_gate_ref[...]
    for i in range(units // width):
        small_ref[5 + i : 6 + i, :] = unit_line[:, i * width : (i + 1) * width]
    lane = lax.broadcasted_iota(jnp.int32, (1, width), 1)
    layer0 = jnp.sum(attn_line * hidden_gate, axis=1, keepdims=True)
    layer1 = jnp.sum(ffn_line * hidden_gate, axis=1, keepdims=True)
    small_ref[7:8, :] = jnp.where(lane == 128, layer0, jnp.where(lane == 129, layer1, 0.0))

    def finish(t, _):
        pltpu.make_async_copy(
            got2.at[rows(t)], student_hbm.at[rows(t)], tile_sem.at[0, t]
        ).wait()
        tile_copy(1, t).wait()
        tile_copy(2, t).wait()

    lax.fori_loop(0, tiles, finish, None)
    for n in range(units // PART):
        wide(0, n).wait()
        wide(1, n).wait()
    last.wait()


def ffn(lengths, layer_gates, norm_p, hidden_gate, unit_gate, context, w_out_t, tokens, teacher, w_in, w_fo_t):
    count, width = tokens.shape
    units, heads = w_in.shape[1], context.shape[1]
    tiles = count // TILE
    vmem, smem = pl.BlockSpec(memory_space=pltpu.VMEM), pl.BlockSpec(memory_space=pltpu.SMEM)
    anywhere = pl.BlockSpec(memory_space=pl.ANY)
    low, full = jnp.bfloat16, jnp.float32
    return pl.pallas_call(
        ffn_kernel,
        in_specs=[smem, smem] + [vmem] * 5 + [anywhere] * 4,
        out_specs=[anywhere] * 4 + [vmem],
        out_shape=[
            jax.ShapeDtypeStruct((count, width), low),
            jax.ShapeDtypeStruct((count, width), full),
            jax.ShapeDtypeStruct((count, heads), full),
            jax.ShapeDtypeStruct((width, 2 * units + heads), low),
            jax.ShapeDtypeStruct((8, width), full),
        ],
        scratch_shapes=[
            pltpu.VMEM((width, units), low),
            pltpu.VMEM((width, units), low),
            pltpu.VMEM((count, width), low),
            pltpu.VMEM((count, width), low),
            *[pltpu.VMEM((count, width), low)] * 5,
            pltpu.VMEM((count, width), full),
            pltpu.VMEM((count, 1), full),
            pltpu.VMEM((count, units), low),
            pltpu.VMEM((count, units), low),
            pltpu.VMEM((count, width), full),
            pltpu.VMEM((count, heads), full),
            *[pltpu.VMEM((width, count), low)] * 3,
            pltpu.VMEM((2, width, units), low),
            pltpu.VMEM((width, heads), low),
            pltpu.VMEM((6, 8, width), full),
            pltpu.VMEM((8, units), full),
            pltpu.SemaphoreType.DMA((4,)),
            pltpu.SemaphoreType.DMA((3, tiles)),
            pltpu.SemaphoreType.DMA((3, units // PART)),
            pltpu.SemaphoreType.DMA((3, tiles)),
            pltpu.SemaphoreType.DMA((3, tiles)),
        ],
        compiler_params=pltpu.CompilerParams(
            collective_id=4, has_side_effects=True, vmem_limit_bytes=60 << 20
        ),
        name="ffn",
    )(lengths, layer_gates, norm_p, hidden_gate[None, :], unit_gate[None, :], context, w_out_t, tokens, teacher, w_in, w_fo_t)


def lamb_moments(master, first, second, grad, decay):
    new_first = MOMENT_DECAY * first + (1.0 - MOMENT_DECAY) * grad
    new_second = MOMENT_DECAY * second + (1.0 - MOMENT_DECAY) * grad * grad
    correction = 1.0 - MOMENT_DECAY**STEP_COUNT
    update = (
        new_first / correction / (jnp.sqrt(new_second / correction) + LAMB_EPS) + decay * master
    )
    return (new_first, new_second, update)


BLOCK = 384
DEPTH = (1, 3, 2, 0)


def layer_kernel(
    lengths_ref,
    gates_ref,
    gate_ref,
    hidden_gate_ref,
    unit_gate_ref,
    norms_ref,
    norm_shard_ref,
    *refs,
):
    params, refs = refs[:12], refs[12:]
    (
        tokens_hbm,
        teacher_hbm,
        student_hbm,
        grad_tokens_hbm,
        sums_ref,
        small_out,
        norm_out,
        total_out,
        w,
        w_norm,
        tokens,
        qkv,
        d_mix,
        context,
        stats,
        left_t,
        hidden_t,
        own1,
        got1,
        own2,
        got2,
        got3,
        normal1,
        scale1,
        gated,
        slope,
        d_res,
        keep,
        gains,
        sums,
        unit_sum,
        heads,
        small_plane,
        small_line,
        norm_plane,
        norm_line,
        load_sem,
        tile_sem,
        all_send,
        all_recv,
        swap_send,
        swap_recv,
        send_sem,
        recv_sem,
        small_send,
        small_recv,
        free1,
        free2,
    ) = refs
    me, core = lax.axis_index("dp"), lax.axis_index("head")
    z, y, x = place(me)
    rows, blocks = sums_ref.shape[0], sums_ref.shape[1] // BLOCK
    count, width = tokens.shape
    tiles, tall = count // TILE, count // ROW
    units, own_width = unit_gate_ref.shape[1], gate_ref.shape[1]
    pairs = own_width // PAIR
    at_out, at_in = 3 * own_width, 4 * own_width
    at_fo = at_in + units

    def load(which, t):
        source = (tokens_hbm, teacher_hbm)[which % 2]
        return pltpu.make_async_copy(
            source.at[tile(t)], tokens.at[tile(t)], load_sem.at[which, t]
        )

    def tile(t):
        return pl.ds(pl.multiple_of(t * TILE, TILE), TILE)

    def tall_row(r):
        return pl.ds(pl.multiple_of(r * ROW, ROW), ROW)

    def each(action, begin, end):
        lax.fori_loop(begin, end, lambda i, _: action(i), None)

    each(lambda t: load(0, t).start(), 0, tiles)

    line_peers = [(index(lax.rem(z + d, NZ), y, x), core) for d in (1, 2, 3)]
    plane = [index(z, y + (1 - 2 * y) * (d // 2), x + (1 - 2 * x) * (d % 2)) for d in range(4)]
    ring = [(plane[1], core), (plane[2], core), *line_peers]
    sibling = (me, 1 - core)
    greet([(p, core) for p in plane[1:]] + [(p, 1 - core) for p in plane] + line_peers)

    def rows_of(device):
        return pl.ds(pl.multiple_of(device * rows, rows), rows)

    def columns(c):
        start = c * BLOCK
        return pl.ds(start if isinstance(c, int) else pl.multiple_of(start, BLOCK), BLOCK)

    def turned(odd, rz, ra, rb):
        flip_x = ra * (1 - odd) + rb * odd
        flip_y = rb * (1 - odd) + ra * odd
        return index(lax.rem(z + rz, NZ), y + (1 - 2 * y) * flip_y, x + (1 - 2 * x) * flip_x)

    def view(c, device):
        if isinstance(c, int) and c == blocks:
            return w_norm.at[rows_of(device)]
        return w.at[rows_of(device), columns(c)]

    def move(c, place_of, to, there, k):
        block = view(c, turned(c % 2, *place_of))
        return pltpu.make_async_remote_copy(
            src_ref=block,
            dst_ref=block,
            send_sem=all_send.at[c, k],
            recv_sem=all_recv.at[c, there],
            device_id=(to, core),
            device_id_type=MESH,
        )

    def near(c):
        return turned(c % 2, 0, 1, 0)

    def far(c):
        return turned(c % 2, 0, 0, 1)

    def arrived(c, rz, ra, rb):
        move(c, (rz, ra, rb), me, slot(rz, ra, rb), 0).wait_recv()

    def all_first(c):
        for i, dz in enumerate((1, 3, 2)):
            move(c, (0, 0, 0), line_peers[dz - 1][0], slot(NZ - dz, 0, 0), i).start()
        move(c, (0, 0, 0), near(c), slot(0, 1, 0), 3).start()
        move(c, (0, 0, 0), far(c), slot(0, 0, 1), 7).start()

    def all_second(c):
        for i, rz in enumerate((1, 3, 2)):
            arrived(c, rz, 0, 0)
            move(c, (rz, 0, 0), near(c), slot(rz, 1, 0), 4 + i).start()
            move(c, (rz, 0, 0), far(c), slot(rz, 0, 1), 8 + i).start()

    def all_third(c):
        for i, rz in enumerate((0, 1, 3, 2)):
            arrived(c, rz, 1, 0)
            move(c, (rz, 1, 0), far(c), slot(rz, 1, 1), 11 + i).start()

    def all_last(c):
        for ra in (0, 1):
            for rz in range(NZ):
                arrived(c, rz, ra, 1)

    def all_sent(c):
        for k in range(15):
            move(c, (0, 0, 0), me, 0, k).wait_send()

    mine = rows_of(me)
    for pair in range(pairs):
        for part in range(3):
            lanes = slice((3 * pair + part) * PAIR, (3 * pair + part + 1) * PAIR)
            w[mine, lanes] = params[0][part, :, pair * PAIR : (pair + 1) * PAIR].astype(jnp.bfloat16)
    w_norm[mine] = norm_shard_ref[...]
    w[mine, at_out:at_in] = params[1][...].astype(jnp.bfloat16)
    each(all_first, 0, 4)
    all_first(blocks)
    w[mine, at_in:at_fo] = params[2][...].astype(jnp.bfloat16)
    w[mine, at_fo:] = params[3][...].astype(jnp.bfloat16)
    sums[...] = jnp.zeros_like(sums)
    unit_sum[...] = jnp.zeros_like(unit_sum)
    heads[...] = jnp.zeros_like(heads)

    def upto(c):
        return min(c, blocks) if isinstance(c, int) else jnp.minimum(c, blocks)

    def serve(p):
        each(all_second, 2 * p, 2 * p + 2)
        each(all_first, 2 * p + 4, upto(2 * p + 6))
        each(all_third, 2 * p, 2 * p + 2)

    serve(0)
    all_second(blocks)
    serve(1)
    all_third(blocks)
    each(lambda t: load(0, t).wait(), 0, tiles)
    each(all_last, 0, 3)

    def attend(r, _):
        here = tall_row(r)
        same = segments(lengths_ref, r, (ROW, 1), 0) == segments(lengths_ref, r, (1, ROW), 1)
        for pair in range(pairs):
            span = slice(3 * pair * PAIR, 3 * (pair + 1) * PAIR)
            qkv[here, span] = mul(tokens[here], w[:, span]).astype(jnp.bfloat16)
        for pair in range(pairs):
            start = 3 * pair * PAIR
            mix, totals = attend_pair(
                same, *(qkv[here, start + i * PAIR : start + (i + 1) * PAIR] for i in range(3))
            )
            for head in (0, 1):
                stats[r, pair, head : head + 1, :] = totals[head]
            lanes = slice(pair * PAIR, (pair + 1) * PAIR)
            context[here, lanes] = (mix * gate_ref[:, lanes]).astype(jnp.bfloat16)
        serve(2 + r)

    lax.fori_loop(0, tall, attend, None)
    all_last(3)

    def swap(step, t):
        source, target = ((own1, got1), (own2, got2), (own2, got3), (own2, got2))[step]
        return pltpu.make_async_remote_copy(
            src_ref=source.at[tile(t)],
            dst_ref=target.at[tile(t)],
            send_sem=swap_send.at[step, t],
            recv_sem=swap_recv.at[step, t],
            device_id=sibling,
            device_id_type=MESH,
        )

    def phase1(t, _):
        part = mul(context[tile(t)], w[:, at_out:at_in], NT)
        own1[tile(t)] = part.astype(jnp.bfloat16)
        swap(0, t).start()

    lax.fori_loop(0, tiles, phase1, None)
    all_last(blocks)
    gains[...] = jnp.transpose(w_norm[...].astype(jnp.float32))[:8]
    gain1, bias1, gain2, bias2 = (gains[i : i + 1, :] for i in range(4))
    hidden_gate = hidden_gate_ref[...]
    gate0, gate1 = hidden_gate * gates_ref[0], hidden_gate * gates_ref[1]
    each(all_last, 4, 8)

    def summed(source, target, t):
        return source[tile(t)].astype(jnp.float32) + target[tile(t)].astype(jnp.float32)

    def part_lanes(n):
        return slice(n * PART, (n + 1) * PART)

    def phase2(t, _):
        swap(0, t).wait()
        rows_in = tokens[tile(t)].astype(jnp.float32) + summed(own1, got1, t) * gate0
        load(1, t).start()
        normal, scale = normalize(rows_in)
        normal1[tile(t)] = normal
        scale1[tile(t)] = scale
        hidden = normal * gain1 + bias1
        low = hidden.astype(jnp.bfloat16)
        hidden_t[:, tile(t)] = jnp.transpose(hidden).astype(jnp.bfloat16)
        for n in range(units // PART):
            up = mul(low, w[:, at_in + n * PART : at_in + (n + 1) * PART])
            below, density = normal_parts(up)
            gate = unit_gate_ref[:, part_lanes(n)]
            gated[tile(t), part_lanes(n)] = (up * below * gate).astype(jnp.bfloat16)
            slope[tile(t), part_lanes(n)] = ((below + density) * gate).astype(jnp.bfloat16)

        @pl.when(t == 2)
        def _():
            serve(5)

    lax.fori_loop(0, tiles, phase2, None)
    each(all_last, 8, blocks)

    def down(t, _):
        part = mul(gated[tile(t)], w[:, at_fo:], NT)
        own2[tile(t)] = part.astype(jnp.bfloat16)
        swap(1, t).start()

    lax.fori_loop(0, tiles, down, None)
    each(all_sent, 0, blocks)
    all_sent(blocks)

    def student_out(t):
        return pltpu.make_async_copy(
            got2.at[tile(t)], student_hbm.at[tile(t)], tile_sem.at[0, t]
        )

    def phase3(t, _):
        swap(1, t).wait()
        load(1, t).wait()
        ffn = summed(own2, got2, t)
        hidden = normal1[tile(t)] * gain1 + bias1
        normal, scale = normalize(hidden + ffn * gate1)
        student = normal * gain2 + bias2
        got2[tile(t)] = student.astype(jnp.bfloat16)
        student_out(t).start()
        row = t // (ROW // TILE)
        end = lengths_ref[row, 0]
        for k in range(1, lengths_ref.shape[1]):
            end = end + lengths_ref[row, k]
        position = lax.broadcasted_iota(jnp.int32, (TILE, 1), 0) + (t % (ROW // TILE)) * TILE
        valid = (position < end).astype(jnp.float32)
        d_out = valid * (student - tokens[tile(t)].astype(jnp.float32))
        load(2, t).start()
        d_res2 = norm_back(d_out, normal, scale, gain2)
        d_res[tile(t)] = d_res2
        sums[2] += fold(d_out * normal)
        sums[3] += fold(d_out)
        sums[5] += fold(d_res2 * ffn)
        d_ffn = d_res2 * gate1
        left_t[:, tile(t)] = jnp.transpose(d_ffn).astype(jnp.bfloat16)
        d_ffn = d_ffn.astype(jnp.bfloat16)
        for n in range(units // PART):
            d_gated = mul(d_ffn, w[:, at_fo + n * PART : at_fo + (n + 1) * PART])
            unit_sum[:, part_lanes(n)] += fold(
                d_gated * gated[tile(t), part_lanes(n)].astype(jnp.float32)
            )
            d_up = d_gated * slope[tile(t), part_lanes(n)].astype(jnp.float32)
            slope[tile(t), part_lanes(n)] = d_up.astype(jnp.bfloat16)
        part = mul(slope[tile(t)], w[:, at_in:at_fo], NT)
        own2[tile(t)] = part.astype(jnp.bfloat16)
        swap(2, t).start()

    lax.fori_loop(0, tiles, phase3, None)

    def spot(buffer, i):
        across = buffer.shape[1] // BLOCK
        return buffer.at[
            pl.ds(pl.multiple_of((i // across) * rows, rows), rows),
            pl.ds(pl.multiple_of((i % across) * BLOCK, BLOCK), BLOCK),
        ]

    def get1(c, k):
        return spot(gated, c * 8 + k)

    def get2(c, rz):
        return spot(slope, c * 7 + rz)

    def get3(c, i):
        return spot(slope, c * 7 + 4 + i)

    def remote(source, target, c, k, to):
        return pltpu.make_async_remote_copy(
            src_ref=source,
            dst_ref=target,
            send_sem=send_sem.at[c, k],
            recv_sem=recv_sem.at[c, k],
            device_id=(to, core),
            device_id_type=MESH,
        )

    def block_of(c, rz, ra, rb):
        return w.at[rows_of(turned(c % 2, rz, ra, rb)), columns(c)]

    def leg1(c, k):
        return remote(block_of(c, k % NZ, k // NZ, 1), get1(c, k), c, k, far(c))

    def leg2(c, rz):
        return remote(block_of(c, rz, 1, 0), get2(c, rz), c, 8 + rz, near(c))

    def leg3(c, rz):
        there = NZ - rz
        to = line_peers[rz - 1][0]
        return remote(block_of(c, rz, 0, 0), get3(c, there - 1), c, 11 + there, to)

    def first(c):
        for ra in (1, 0):
            for rz in DEPTH:
                leg1(c, rz + NZ * ra).start()

    def second(c):
        for ra in (1, 0):
            for rz in DEPTH:
                k = rz + NZ * ra
                leg1(c, k).wait_recv()
                block = block_of(c, rz, ra, 0)
                total = block[...].astype(jnp.float32) + get1(c, k)[...].astype(jnp.float32)
                if ra:
                    block[...] = total.astype(jnp.bfloat16)
                    leg2(c, rz).start()
                else:
                    keep[c, rz] = total

    def third(c):
        for rz in DEPTH:
            leg2(c, rz).wait_recv()
            total = keep[c, rz] + get2(c, rz)[...].astype(jnp.float32)
            if rz:
                block_of(c, rz, 0, 0)[...] = total.astype(jnp.bfloat16)
                leg3(c, rz).start()
            else:
                keep[c, 0] = total

    def last(c):
        total = keep[c, 0]
        for rz in (1, 2, 3):
            leg3(c, rz).wait_recv()
        for i in range(3):
            total = total + get3(c, i)[...].astype(jnp.float32)
        sums_ref[:, columns(c)] = total

    def weigh(left, right, start, size):
        for n in range(size // BLOCK):
            lanes = slice(start + n * BLOCK, start + (n + 1) * BLOCK)
            w[:, lanes] = mul(left[...], right[:, n * BLOCK : (n + 1) * BLOCK]).astype(jnp.bfloat16)

    def ready(semaphore, peers):
        for peer in peers:
            pl.semaphore_signal(semaphore, inc=1, device_id=peer, device_id_type=MESH)
        pl.semaphore_wait(semaphore, len(peers))

    weigh(left_t, gated, at_fo, units)
    ready(free1, ring[:2])
    for c in (11, 10, 9, 8):
        first(c)
    weigh(hidden_t, slope, at_in, units)
    each(lambda t: student_out(t).wait(), 0, tiles)
    ready(free2, [*ring, sibling])

    def phase4(t, _):
        swap(2, t).wait()
        normal = normal1[tile(t)]
        d_hidden = d_res[tile(t)] + summed(own2, got3, t)
        sums[0] += fold(d_hidden * normal)
        sums[1] += fold(d_hidden)
        d_res1 = norm_back(d_hidden, normal, scale1[tile(t)], gain1)
        d_res[tile(t)] = d_res1
        sums[4] += fold(d_res1 * summed(own1, got1, t))
        d_attn = d_res1 * gate0
        left_t[:, tile(t)] = jnp.transpose(d_attn).astype(jnp.bfloat16)
        d_context = mul(d_attn.astype(jnp.bfloat16), w[:, at_out:at_in])
        d_mix[tile(t)] = (d_context * gate_ref[...]).astype(jnp.bfloat16)
        load(2, t).wait()
        hidden_t[:, tile(t)] = jnp.transpose(tokens[tile(t)].astype(jnp.float32)).astype(jnp.bfloat16)

    lax.fori_loop(0, tiles, phase4, None)
    weigh(left_t, context, at_out, own_width)

    def down_from(action, i, n):
        lax.fori_loop(0, n, lambda j, _: action(blocks - 1 - i - j), None)

    def pair_back(j, _):
        pair = pairs - 1 - j
        span = pl.multiple_of(pair * BLOCK, BLOCK)
        gate = gate_ref[:, pl.ds(pl.multiple_of(pair * PAIR, PAIR), PAIR)]

        def row_back(r, _):
            here = tall_row(r)
            same = segments(lengths_ref, r, (ROW, 1), 0) == segments(lengths_ref, r, (1, ROW), 1)
            spans = [pl.ds(pl.multiple_of(span + i * PAIR, PAIR), PAIR) for i in range(3)]
            parts, weighed = attend_back(
                same,
                *(qkv[here, lanes] for lanes in spans),
                stats[r, pair],
                d_mix[here, pl.ds(pl.multiple_of(pair * PAIR, PAIR), PAIR)],
            )
            lane = lax.broadcasted_iota(jnp.int32, heads.shape, 1)
            for head in (0, 1):
                value = weighed[head] / gate[:, head * HEAD_DIM : head * HEAD_DIM + 1]
                heads[...] += jnp.where(lane == 2 * pair + head, value, 0.0)
            for lanes, value in zip(spans, parts, strict=True):
                qkv[here, lanes] = value.astype(jnp.bfloat16)

            @pl.when(r == 1)
            def _():
                down_from(second, 2 * j, 2)
                down_from(first, 2 * j + 4, jnp.where(j == 2, 1, 2))

        lax.fori_loop(0, tall, row_back, None)

        def back(t, _):
            part = mul(qkv[tile(t), pl.ds(span, BLOCK)], w[:, pl.ds(span, BLOCK)], NT)
            normal1[tile(t)] = part + jnp.where(j == 0, 0.0, 1.0) * normal1[tile(t)]

        lax.fori_loop(0, tiles, back, None)
        w[:, pl.ds(span, BLOCK)] = mul(hidden_t[...], qkv[:, pl.ds(span, BLOCK)]).astype(jnp.bfloat16)
        first(pair)
        down_from(third, 2 * j, 2)

        @pl.when(j > 0)
        def _():
            down_from(last, 2 * j - 2, 2)

    lax.fori_loop(0, pairs, pair_back, None)

    def tokens_out(t):
        return pltpu.make_async_copy(
            d_res.at[tile(t)], grad_tokens_hbm.at[tile(t)], tile_sem.at[1, t]
        )

    def share(t, _):
        own2[tile(t)] = normal1[tile(t)].astype(jnp.bfloat16)
        swap(3, t).start()

    lax.fori_loop(0, tiles, share, None)

    here_plane = y * NX + x

    def line_of(i):
        return jnp.sum(sums[i], axis=0, keepdims=True)

    for i in range(4):
        small_plane[here_plane, i : i + 1, :] = line_of(i)
    attn_line, ffn_line = line_of(4), line_of(5)
    small_plane[here_plane, 4:5, :] = ffn_line * gates_ref[1] + attn_line * gates_ref[0]
    unit_line = jnp.sum(unit_sum[...], axis=0, keepdims=True) / unit_gate_ref[...]
    for i in range(units // width):
        small_plane[here_plane, 5 + i : 6 + i, :] = unit_line[:, i * width : (i + 1) * width]
    lane = lax.broadcasted_iota(jnp.int32, (1, width), 1)
    layer0 = jnp.sum(attn_line * hidden_gate, axis=1, keepdims=True)
    layer1 = jnp.sum(ffn_line * hidden_gate, axis=1, keepdims=True)
    pair_line = jnp.where(lane == 128, layer0, jnp.where(lane == 129, layer1, 0.0))
    small_plane[here_plane, 7:8, :] = pair_line
    small_plane[here_plane, 7:8, :128] = heads[0:1]

    def spread(buffer, base, targets, at):
        copies = [
            pltpu.make_async_remote_copy(
                src_ref=buffer.at[at],
                dst_ref=buffer.at[at],
                send_sem=small_send.at[base + i],
                recv_sem=small_recv.at[base + i],
                device_id=to,
                device_id_type=MESH,
            )
            for i, to in enumerate(targets)
        ]
        for one in copies:
            one.start()
        return copies

    def added(buffer, copies):
        for one in copies:
            one.wait_recv()
        total = buffer[0]
        for at in range(1, buffer.shape[0]):
            total = total + buffer[at]
        return total

    sent1 = spread(small_plane, 0, [(p, core) for p in plane[1:]], here_plane)
    down_from(second, 6, 2)

    def finish(t, _):
        swap(3, t).wait()
        d_res[tile(t)] += summed(own2, got2, t)
        tokens_out(t).start()

    lax.fori_loop(0, tiles, finish, None)
    down_from(second, 9, 2)
    down_from(second, 8, 1)
    small_line[z] = added(small_plane, sent1)
    sent2 = spread(small_line, 3, line_peers, z)
    down_from(last, 4, 2)
    down_from(third, 6, 2)
    down_from(second, 11, 1)
    down_from(third, 8, 3)
    down_from(last, 6, 2)
    total = added(small_line, sent2)
    small_out[...] = total
    norm_grad = pltpu.roll(total, (width - me * rows) % width, 1)[:, :128]
    norm_out[...] = norm_grad
    down_from(third, 11, 1)

    row8 = lax.broadcasted_iota(jnp.int32, (8, 128), 0)
    lane8 = lax.broadcasted_iota(jnp.int32, (8, 128), 1)

    def put(tile8, row, weight, update):
        here = row8 == row
        return jnp.where(here & (lane8 == 0), weight, jnp.where(here & (lane8 == 1), update, tile8))

    def square(block):
        return jnp.sum(jnp.sum(block * block, axis=0, keepdims=True), axis=1, keepdims=True)

    tile8 = jnp.zeros((8, 128), jnp.float32)
    master, first_moment, second_moment = (norms_ref[i] for i in range(3))
    update = lamb_moments(master, first_moment, second_moment, norm_grad[:4, : master.shape[1]], 0.0)[2]
    for i in range(4):
        tile8 = put(tile8, 4 + i, 0.5 * square(master[i : i + 1]), 0.5 * square(update[i : i + 1]))

    def matrix(tile8, p, start):
        master = params[p][...]
        grad = sums_ref[:, start : start + master.shape[1]]
        update = lamb_moments(master, params[4 + p][...], params[8 + p][...], grad, WEIGHT_DECAY)[2]
        return put(tile8, p, square(master), square(update))

    tile8 = matrix(matrix(tile8, 3, at_fo), 2, at_in)
    down_from(last, 8, 1)
    tile8 = matrix(tile8, 1, at_out)
    weights, updates = 0.0, 0.0
    for pair in range(pairs - 1, -1, -1):
        down_from(last, blocks - 1 - pair, 1)
        for part in range(3):
            lanes = slice(pair * PAIR, (pair + 1) * PAIR)
            master = params[0][part, :, lanes]
            start = (3 * pair + part) * PAIR
            grad = sums_ref[:, start : start + PAIR]
            update = lamb_moments(master, params[4][part, :, lanes], params[8][part, :, lanes], grad, WEIGHT_DECAY)[2]
            weights, updates = weights + square(master), updates + square(update)
    tile8 = put(tile8, 0, weights, updates)
    here_cores = core * (NX * NY) + here_plane
    norm_plane[here_cores] = tile8
    targets = [(p, core) for p in plane[1:]] + [(p, 1 - core) for p in plane]
    sent3 = spread(norm_plane, 6, targets, here_cores)
    norm_line[z] = added(norm_plane, sent3)
    sent4 = spread(norm_line, 13, line_peers, z)
    total_out[...] = added(norm_line, sent4)
    for one in (*sent1, *sent2, *sent3, *sent4):
        one.wait_send()

    def drain(c):
        for k in range(8):
            leg1(c, k).wait_send()
        for rz in range(NZ):
            leg2(c, rz).wait_send()
        for rz in (1, 2, 3):
            leg3(c, rz).wait_send()

    each(drain, 0, blocks)
    each(lambda t: tokens_out(t).wait(), 0, tiles)


def layer(lengths, layer_gates, gate_lanes, hidden_gate, unit_gate, norms, norm_shard, params, tokens, teacher):
    count, width = tokens.shape
    own_width, units, rows = gate_lanes.shape[1], unit_gate.shape[0], norms.shape[2]
    total = 4 * own_width + 2 * units
    tiles, tall, blocks = count // TILE, count // ROW, total // BLOCK
    vmem, smem = pl.BlockSpec(memory_space=pltpu.VMEM), pl.BlockSpec(memory_space=pltpu.SMEM)
    anywhere = pl.BlockSpec(memory_space=pl.ANY)
    low, full = jnp.bfloat16, jnp.float32
    return pl.pallas_call(
        layer_kernel,
        in_specs=[smem, smem] + [vmem] * (5 + len(params)) + [anywhere] * 2,
        out_specs=[anywhere] * 2 + [vmem] * 4,
        out_shape=[
            jax.ShapeDtypeStruct((count, width), low),
            jax.ShapeDtypeStruct((count, width), full),
            jax.ShapeDtypeStruct((rows, total), full),
            jax.ShapeDtypeStruct((8, width), full),
            jax.ShapeDtypeStruct((8, 128), full),
            jax.ShapeDtypeStruct((8, 128), full),
        ],
        scratch_shapes=[
            pltpu.VMEM((width, total), low),
            pltpu.VMEM((width, 128), low),
            pltpu.VMEM((count, width), low),
            pltpu.VMEM((count, 3 * own_width), low),
            pltpu.VMEM((count, own_width), low),
            pltpu.VMEM((count, own_width), low),
            pltpu.VMEM((tall, own_width // PAIR, 8, ROW), full),
            pltpu.VMEM((width, count), low),
            pltpu.VMEM((width, count), low),
            *[pltpu.VMEM((count, width), low)] * 5,
            pltpu.VMEM((count, width), full),
            pltpu.VMEM((count, 1), full),
            pltpu.VMEM((count, units), low),
            pltpu.VMEM((count, units), low),
            pltpu.VMEM((count, width), full),
            pltpu.VMEM((blocks, NZ, rows, BLOCK), full),
            pltpu.VMEM((8, width), full),
            pltpu.VMEM((6, 8, width), full),
            pltpu.VMEM((8, units), full),
            pltpu.VMEM((8, 128), full),
            pltpu.VMEM((NX * NY, 8, width), full),
            pltpu.VMEM((NZ, 8, width), full),
            pltpu.VMEM((2 * NX * NY, 8, 128), full),
            pltpu.VMEM((NZ, 8, 128), full),
            pltpu.SemaphoreType.DMA((3, tiles)),
            pltpu.SemaphoreType.DMA((2, tiles)),
            pltpu.SemaphoreType.DMA((blocks + 1, 15)),
            pltpu.SemaphoreType.DMA((blocks + 1, 16)),
            pltpu.SemaphoreType.DMA((4, tiles)),
            pltpu.SemaphoreType.DMA((4, tiles)),
            pltpu.SemaphoreType.DMA((blocks, 15)),
            pltpu.SemaphoreType.DMA((blocks, 15)),
            pltpu.SemaphoreType.DMA((16,)),
            pltpu.SemaphoreType.DMA((16,)),
            pltpu.SemaphoreType.REGULAR,
            pltpu.SemaphoreType.REGULAR,
        ],
        compiler_params=pltpu.CompilerParams(
            collective_id=0, has_side_effects=True, vmem_limit_bytes=62 << 20
        ),
        name="layer",
    )(lengths, layer_gates, gate_lanes, hidden_gate[None, :], unit_gate[None, :], norms, norm_shard, *params, tokens, teacher)


def spans(shape):
    if len(shape) == 2:
        return [(slice(None), slice(None))]
    pairs = shape[2] // PAIR
    return [
        (part, slice(None), slice(pair * PAIR, (pair + 1) * PAIR))
        for pair in range(pairs)
        for part in range(3)
    ]


def update_kernel(sums_ref, small_ref, norm_ref, total_ref, norms_ref, *refs):
    params, outs = refs[:12], refs[12:]
    weight_norm = jnp.sqrt(total_ref[:, 0:1])
    update_norm = jnp.sqrt(total_ref[:, 1:2])
    trust = weight_norm / update_norm

    def step(row, targets, at, values, decay):
        master, first_moment, second_moment, grad = values
        new_first, new_second, update = lamb_moments(
            master, first_moment, second_moment, grad, decay
        )
        new_master = master - LEARN_RATE * trust[row] * update
        made = (grad, new_first, new_second, new_master, new_master.astype(jnp.bfloat16))
        for target, value in zip(targets, made, strict=True):
            target[at] = value

    start = 0
    for p in range(4):
        targets = outs[5 * p : 5 * p + 5]
        for at in spans(params[p].shape):
            width = params[p][at].shape[-1]
            grad = sums_ref[:, start : start + width]
            values = (*(params[4 * i + p][at] for i in range(3)), grad)
            step(slice(p, p + 1), targets, at, values, WEIGHT_DECAY)
            start += width
    norm_grad = norm_ref[:4, : norms_ref.shape[2]]
    values = (*(norms_ref[i] for i in range(3)), norm_grad)
    step(slice(4, 8), outs[20:25], (Ellipsis,), values, 0.0)
    stats_out, heads_out, units_out, hidden_out, layers_out = outs[25:]
    lane = lax.broadcasted_iota(jnp.int32, (8, 128), 1)
    stats_out[...] = jnp.where(lane == 0, weight_norm, jnp.where(lane == 1, update_norm, trust))
    heads_out[...] = small_ref[7:8, : heads_out.shape[1]]
    width = small_ref.shape[1]
    for i in range(units_out.shape[1] // width):
        units_out[:, i * width : (i + 1) * width] = small_ref[5 + i : 6 + i, :]
    hidden_out[...] = small_ref[4:5, :]
    layers_out[...] = small_ref[7:8, 128:130]


def update(sums, small, norm_grad, totals, norms, params, sizes):
    vmem = pl.BlockSpec(memory_space=pltpu.VMEM)
    shapes = []
    for master in params[:4]:
        shapes += [jax.ShapeDtypeStruct(master.shape, jnp.float32)] * 4
        shapes += [jax.ShapeDtypeStruct(master.shape, jnp.bfloat16)]
    shapes += [jax.ShapeDtypeStruct(norms.shape[1:], jnp.float32)] * 4
    shapes += [jax.ShapeDtypeStruct(norms.shape[1:], jnp.bfloat16)]
    shapes += [jax.ShapeDtypeStruct((8, 128), jnp.float32)]
    shapes += [jax.ShapeDtypeStruct((1, size), jnp.float32) for size in sizes]
    return pl.pallas_call(
        update_kernel,
        in_specs=[vmem] * (5 + len(params)),
        out_specs=[vmem] * len(shapes),
        out_shape=shapes,
        compiler_params=pltpu.CompilerParams(vmem_limit_bytes=48 << 20),
        name="update",
    )(sums, small, norm_grad, totals, norms, *params)


def core_sum(part):
    part = part.astype(jnp.bfloat16)
    other = lax.ppermute(part, "head", [(0, 1), (1, 0)])
    return part.astype(jnp.float32) + other.astype(jnp.float32)


def plain_totals(sums, norm_grad, norms, params, head_count):
    found, start = [], 0
    for p in range(4):
        pair = jnp.zeros((2,), jnp.float32)
        for at in spans(params[p].shape):
            master, first_moment, second_moment = (params[4 * i + p][at] for i in range(3))
            grad = sums[:, start : start + master.shape[1]]
            update = lamb_moments(master, first_moment, second_moment, grad, WEIGHT_DECAY)[2]
            pair = pair + jnp.stack([jnp.sum(master * master), jnp.sum(update * update)])
            start += master.shape[1]
        found.append(pair)
    master, first_moment, second_moment = norms
    update = lamb_moments(master, first_moment, second_moment, norm_grad[:4, : norms.shape[2]], 0.0)[2]
    rows = jnp.stack([jnp.sum(master * master, axis=1), jnp.sum(update * update, axis=1)], axis=1)
    found = jnp.concatenate([jnp.stack(found), rows / head_count])
    return jnp.pad(lax.psum(found, ("dp", "head")), ((0, 0), (0, 126)))


def rows_first(qkv):
    return jnp.transpose(qkv, (1, 0, 2))


def plain_layer(lengths, layer_gates, gate_lanes, hidden_gate, unit_gate, norms, norm_shard, params, tokens, teacher):
    heads_here, rows = gate_lanes.shape[1] // HEAD_DIM, norms.shape[2]
    own_width, units = gate_lanes.shape[1], unit_gate.shape[0]
    shards = [params[p][at] for p in range(4) for at in spans(params[p].shape)]
    shards = jnp.concatenate(shards, axis=1).astype(jnp.bfloat16)
    w, norm_t = (lax.all_gather(s, "dp", axis=0, tiled=True) for s in (shards, norm_shard))
    norm_p = norm_t[:, :4].T.astype(jnp.float32)
    w_qkv, w_out_t, w_in, w_fo_t = jnp.split(
        w, (3 * own_width, 4 * own_width, 4 * own_width + units), axis=1
    )
    qkv = jnp.dot(tokens, w_qkv, preferred_element_type=jnp.float32).astype(jnp.bfloat16)
    context, stats = attention(qkv, lengths, gate_lanes)
    student, d_res1, d_context, grads, small = ffn(
        lengths,
        layer_gates,
        norm_p,
        hidden_gate,
        unit_gate,
        context,
        w_out_t,
        tokens,
        teacher,
        w_in,
        w_fo_t,
    )
    d_qkv, head_sums = attention_back(qkv, lengths, gate_lanes, stats, d_context)
    d_heads = jnp.sum(head_sums[:, :, 0, :2], axis=0).reshape(-1)
    grad_qkv = jnp.einsum("tc,tk->ck", tokens, d_qkv, preferred_element_type=jnp.float32)
    input_part = jnp.einsum("tk,ck->tc", d_qkv, w_qkv, preferred_element_type=jnp.float32)
    grad_tokens = d_res1 + core_sum(input_part)
    grad_fo, grad_in, grad_out = jnp.split(grads.astype(jnp.float32), (units, 2 * units), axis=1)
    grads = jnp.concatenate([grad_qkv, grad_out, grad_in, grad_fo], axis=1)
    sums = lax.psum_scatter(grads, "dp", scatter_dimension=0, tiled=True)
    small = lax.psum(small.at[7, :heads_here].set(d_heads), "dp")
    norm_grad = lax.dynamic_slice_in_dim(small, lax.axis_index("dp") * rows, rows, 1)
    norm_grad = jnp.pad(norm_grad, ((0, 0), (0, 128 - rows)))
    totals = plain_totals(sums, norm_grad, norms, params, lax.axis_size("head"))
    return student, grad_tokens, sums, small, norm_grad, totals


def local(
    tokens,
    teacher,
    lengths,
    head_gate,
    unit_gate,
    hidden_gate,
    layer_gates,
    master_qkv,
    first_qkv,
    second_qkv,
    master_attn_out,
    first_attn_out,
    second_attn_out,
    master_ffn_in,
    first_ffn_in,
    second_ffn_in,
    master_ffn_out,
    first_ffn_out,
    second_ffn_out,
    master_norms,
    first_norms,
    second_norms,
):
    ours = lax.axis_size("dp") == GRID and lax.axis_size("head") == 2
    gate_lanes = jnp.repeat(head_gate, HEAD_DIM)[None, :]
    params = [
        rows_first(master_qkv),
        master_attn_out.T,
        master_ffn_in,
        master_ffn_out.T,
        rows_first(first_qkv),
        first_attn_out.T,
        first_ffn_in,
        first_ffn_out.T,
        rows_first(second_qkv),
        second_attn_out.T,
        second_ffn_in,
        second_ffn_out.T,
    ]
    norms = jnp.stack([master_norms, first_norms, second_norms])
    norm_shard = jnp.pad(master_norms.T, ((0, 0), (0, 124))).astype(jnp.bfloat16)
    run = layer if ours else plain_layer
    student, grad_tokens, sums, small, norm_grad, totals = run(
        lengths,
        layer_gates,
        gate_lanes,
        hidden_gate,
        unit_gate,
        norms,
        norm_shard,
        params,
        tokens,
        teacher,
    )
    sizes = (head_gate.shape[0], unit_gate.shape[0], hidden_gate.shape[0], 2)
    made = update(sums, small, norm_grad, totals, norms, params, sizes)
    results = []
    for p in range(4):
        for value in made[5 * p : 5 * p + 5]:
            results.append(rows_first(value) if p == 0 else value if p == 2 else value.T)
    norm_results, (stats_rows, *gate_rows) = made[20:25], made[25:]
    gate_results = [row.reshape(-1) for row in gate_rows]
    return (
        student,
        grad_tokens,
        *gate_results,
        *results,
        *norm_results,
        stats_rows[:, :3].T,
    )


def solution(mesh):
    return jax.shard_map(
        local,
        mesh=mesh,
        in_specs=(
            P("dp", None),
            P("dp", None),
            P("dp", None),
            P("head"),
            P("head"),
            P(),
            P(),
            P("dp", None, "head"),
            P("dp", None, "head"),
            P("dp", None, "head"),
            P("head", "dp"),
            P("head", "dp"),
            P("head", "dp"),
            P("dp", "head"),
            P("dp", "head"),
            P("dp", "head"),
            P("head", "dp"),
            P("head", "dp"),
            P("head", "dp"),
            P(None, "dp"),
            P(None, "dp"),
            P(None, "dp"),
        ),
        out_specs=(
            P("dp", None),
            P("dp", None),
            P("head"),
            P("head"),
            P(),
            P(),
            P("dp", None, "head"),
            P("dp", None, "head"),
            P("dp", None, "head"),
            P("dp", None, "head"),
            P("dp", None, "head"),
            P("head", "dp"),
            P("head", "dp"),
            P("head", "dp"),
            P("head", "dp"),
            P("head", "dp"),
            P("dp", "head"),
            P("dp", "head"),
            P("dp", "head"),
            P("dp", "head"),
            P("dp", "head"),
            P("head", "dp"),
            P("head", "dp"),
            P("head", "dp"),
            P("head", "dp"),
            P("head", "dp"),
            P(None, "dp"),
            P(None, "dp"),
            P(None, "dp"),
            P(None, "dp"),
            P(None, "dp"),
            P(),
        ),
        check_vma=False,
    )
```

```python
import functools

import jax
import jax.numpy as jnp
from jax import lax
from jax.experimental import pallas as pl
from jax.experimental.pallas import tpu as pltpu
from jax.sharding import PartitionSpec as P

D = 768
HEAD_DIM = 64
ROW = 512
STEP_COUNT = 5

LN_EPS = 1e-05
LAMB_EPS = 1e-06
WEIGHT_DECAY = 0.01
LEARN_RATE = 0.5
MOMENT_DECAY = 0.5
MASK_FILL = -1000000000.0


MESH = pl.DeviceIdType.MESH
NZ, NY, NX = 4, 2, 2
GRID = NZ * NY * NX


def place(me):
    return me // (NY * NX), (me // NX) % NY, me % NX


def index(z, y, x):
    return (z * NY + y) * NX + x


def slot(rz, ra, rb):
    return rz + NZ * (ra + 2 * rb)


def greet(peers):
    barrier = pltpu.get_barrier_semaphore()
    for peer in peers:
        pl.semaphore_signal(barrier, inc=1, device_id=peer, device_id_type=MESH)
    pl.semaphore_wait(barrier, len(peers))


NT = (((1,), (1,)), ((), ()))
NN = (((1,), (0,)), ((), ()))
PAIR = 2 * HEAD_DIM


def mul(a, b, dims=NN):
    return lax.dot_general(a, b, dims, preferred_element_type=jnp.float32)


def segments(lengths_ref, row, shape, axis):
    positions = lax.broadcasted_iota(jnp.int32, shape, axis)
    end = jnp.int32(0)
    found = jnp.zeros(shape, jnp.int32)
    for k in range(lengths_ref.shape[1]):
        end = end + lengths_ref[row, k]
        found = found + (positions >= end).astype(jnp.int32)
    return found


def flip(block):
    return jnp.transpose(block.astype(jnp.float32)).astype(block.dtype)


def head_lanes(block, head):
    lane = lax.broadcasted_iota(jnp.int32, block.shape, 1)
    inside = (lane < HEAD_DIM) if head == 0 else (lane >= HEAD_DIM)
    return jnp.where(inside, block, jnp.zeros_like(block))


def attend_pair(same, queries, keys, values):
    queries = queries * jnp.bfloat16(HEAD_DIM**-0.5)
    values_t = flip(values)
    mixes, totals = [], []
    for head in (0, 1):
        scores = mul(keys, head_lanes(queries, head), NT)
        scores = jnp.where(same, scores, MASK_FILL)
        top = jnp.max(scores, axis=0, keepdims=True)
        expo = jnp.exp(scores - top)
        total = jnp.sum(expo, axis=0, keepdims=True)
        probs = (expo * (1.0 / total)).astype(jnp.bfloat16)
        mixes.append(mul(values_t[head * HEAD_DIM : (head + 1) * HEAD_DIM], probs))
        totals.append(top + jnp.log(total))
    return jnp.transpose(jnp.concatenate(mixes, axis=0)), totals


def attend_back(same, queries, keys, values, stats, d_mix):
    queries = queries * jnp.bfloat16(HEAD_DIM**-0.5)
    keys_t = flip(keys)
    d_queries, d_keys, d_values, sums = [], None, None, []
    for head in (0, 1):
        q_one, d_one = head_lanes(queries, head), head_lanes(d_mix, head)
        scores = jnp.where(same, mul(keys, q_one, NT), MASK_FILL)
        probs = jnp.exp(scores - stats[head : head + 1, :])
        d_probs = mul(values, d_one, NT)
        weighed = jnp.sum(probs * d_probs, axis=0, keepdims=True)
        sums.append(jnp.sum(weighed, axis=1, keepdims=True))
        d_scores = (probs * (d_probs - weighed)).astype(jnp.bfloat16)
        dv = mul(probs.astype(jnp.bfloat16), d_one)
        dk = mul(d_scores, q_one)
        d_values = dv if head == 0 else d_values + dv
        d_keys = dk if head == 0 else d_keys + dk
        d_queries.append(mul(keys_t[head * HEAD_DIM : (head + 1) * HEAD_DIM], d_scores))
    dq = jnp.transpose(jnp.concatenate(d_queries, axis=0)) * HEAD_DIM**-0.5
    return (dq, d_keys, d_values), sums


def attention_kernel(lengths_ref, gate_ref, qkv_ref, context_ref, stats_ref):
    row = pl.program_id(0)
    same = segments(lengths_ref, row, (ROW, 1), 0) == segments(lengths_ref, row, (1, ROW), 1)
    mix, totals = attend_pair(same, *(qkv_ref[:, i * PAIR : (i + 1) * PAIR] for i in range(3)))
    for head in (0, 1):
        stats_ref[0, 0, head : head + 1, :] = totals[head]
    context_ref[...] = (mix * gate_ref[...]).astype(jnp.bfloat16)


def attention(qkv, lengths, gate_lanes):
    tokens, width = qkv.shape
    rows, pairs = lengths.shape[0], width // 3 // PAIR
    return pl.pallas_call(
        attention_kernel,
        grid=(rows, pairs),
        in_specs=[
            pl.BlockSpec(memory_space=pltpu.SMEM),
            pl.BlockSpec((1, PAIR), lambda r, h: (0, h)),
            pl.BlockSpec((ROW, 3 * PAIR), lambda r, h: (r, h)),
        ],
        out_specs=[
            pl.BlockSpec((ROW, PAIR), lambda r, h: (r, h)),
            pl.BlockSpec((1, 1, 8, ROW), lambda r, h: (r, h, 0, 0)),
        ],
        out_shape=[
            jax.ShapeDtypeStruct((tokens, width // 3), jnp.bfloat16),
            jax.ShapeDtypeStruct((rows, pairs, 8, ROW), jnp.float32),
        ],
        compiler_params=pltpu.CompilerParams(vmem_limit_bytes=32 << 20),
        name="attention",
    )(lengths, gate_lanes, qkv)


def attention_back_kernel(lengths_ref, gate_ref, qkv_ref, stats_ref, d_ref, out_ref, heads_ref):
    row = pl.program_id(0)
    same = segments(lengths_ref, row, (ROW, 1), 0) == segments(lengths_ref, row, (1, ROW), 1)
    gate = gate_ref[...]
    d_mix = (d_ref[...] * gate).astype(jnp.bfloat16)
    parts, weighed = attend_back(
        same, *(qkv_ref[:, i * PAIR : (i + 1) * PAIR] for i in range(3)), stats_ref[0, 0], d_mix
    )
    for i, value in enumerate(parts):
        out_ref[:, i * PAIR : (i + 1) * PAIR] = value.astype(jnp.bfloat16)
    lane = lax.broadcasted_iota(jnp.int32, (8, PAIR), 1)
    found = jnp.zeros((8, PAIR), jnp.float32)
    for head in (0, 1):
        value = weighed[head] / gate[:, head * HEAD_DIM : head * HEAD_DIM + 1]
        found = jnp.where(lane == head, value, found)
    heads_ref[0, 0] = found


def attention_back(qkv, lengths, gate_lanes, stats, d_context):
    tokens, width = qkv.shape
    rows, pairs = lengths.shape[0], width // 3 // PAIR
    wide = pl.BlockSpec((ROW, 3 * PAIR), lambda r, h: (r, h))
    return pl.pallas_call(
        attention_back_kernel,
        grid=(rows, pairs),
        in_specs=[
            pl.BlockSpec(memory_space=pltpu.SMEM),
            pl.BlockSpec((1, PAIR), lambda r, h: (0, h)),
            wide,
            pl.BlockSpec((1, 1, 8, ROW), lambda r, h: (r, h, 0, 0)),
            pl.BlockSpec((ROW, PAIR), lambda r, h: (r, h)),
        ],
        out_specs=[wide, pl.BlockSpec((1, 1, 8, PAIR), lambda r, h: (r, h, 0, 0))],
        out_shape=[
            jax.ShapeDtypeStruct((tokens, width), jnp.bfloat16),
            jax.ShapeDtypeStruct((rows, pairs, 8, PAIR), jnp.float32),
        ],
        compiler_params=pltpu.CompilerParams(vmem_limit_bytes=32 << 20),
        name="attention_back",
    )(lengths, gate_lanes, qkv, stats, d_context)


TILE = 256
PART = 256
TAIL_STEP = 0.3
TAIL = (
    0.11963200569152832,
    0.12071217596530914,
    0.10017567127943039,
    0.1276927888393402,
    -0.052036140114068985,
    0.2045592963695526,
    -0.15616002678871155,
    0.035424139350652695,
)


def normal_parts(u):
    bell = jnp.exp(-0.5 * u * u)
    t = 1.0 / (1.0 + TAIL_STEP * jnp.abs(u))
    series = TAIL[-1]
    for term in TAIL[-2::-1]:
        series = series * t + term
    tail = series * t * bell
    return jnp.where(u < 0, tail, 1.0 - tail), u * bell * 0.3989422804014327


def fold(block):
    return jnp.sum(block.reshape(-1, 8, block.shape[1]), axis=0)


def norm_back(d_out, normal, scale, gain):
    d_normal = d_out * gain
    d_normal = (
        d_normal
        - jnp.mean(d_normal, axis=-1, keepdims=True)
        - normal * jnp.mean(d_normal * normal, axis=-1, keepdims=True)
    )
    return d_normal * scale


def normalize(rows_in):
    center = rows_in - jnp.mean(rows_in, axis=-1, keepdims=True)
    scale = lax.rsqrt(jnp.mean(center * center, axis=-1, keepdims=True) + LN_EPS)
    return center * scale, scale


def ffn_kernel(
    lengths_ref,
    gates_ref,
    norm_ref,
    hidden_gate_ref,
    unit_gate_ref,
    context_ref,
    w_out_ref,
    tokens_hbm,
    teacher_hbm,
    w_in_hbm,
    w_fo_hbm,
    student_hbm,
    d_res1_hbm,
    d_context_hbm,
    grads_hbm,
    small_ref,
    w_in,
    w_fo,
    tokens,
    teacher,
    own1,
    own2,
    got1,
    got2,
    got3,
    normal1,
    scale1,
    gated,
    slope,
    d_res,
    d_context,
    hidden_t,
    d_ffn_t,
    d_attn_t,
    grad_wide,
    grad_out,
    sums,
    unit_sum,
    load_sem,
    tile_sem,
    grad_sem,
    send_sem,
    recv_sem,
):
    dp, core = lax.axis_index("dp"), lax.axis_index("head")
    loads = [
        pltpu.make_async_copy(source, target, load_sem.at[i])
        for i, (source, target) in enumerate(
            ((tokens_hbm, tokens), (w_in_hbm, w_in), (w_fo_hbm, w_fo), (teacher_hbm, teacher))
        )
    ]
    for one in loads:
        one.start()
    greet([(dp, 1 - core)])
    tiles = tokens.shape[0] // TILE
    units, width = w_in.shape[1], w_in.shape[0]
    sums[...] = jnp.zeros_like(sums)
    unit_sum[...] = jnp.zeros_like(unit_sum)
    hidden_gate = hidden_gate_ref[...]
    gate0, gate1 = hidden_gate * gates_ref[0], hidden_gate * gates_ref[1]
    gain1, bias1, gain2, bias2 = (norm_ref[i : i + 1, :] for i in range(4))

    def rows(t):
        return pl.ds(pl.multiple_of(t * TILE, TILE), TILE)

    def lanes(n):
        return pl.ds(n * PART, PART)

    def exchange(step, t):
        source, target = ((own1, got1), (own2, got2), (own2, got3))[step]
        return pltpu.make_async_remote_copy(
            src_ref=source.at[rows(t)],
            dst_ref=target.at[rows(t)],
            send_sem=send_sem.at[step, t],
            recv_sem=recv_sem.at[step, t],
            device_id=(dp, 1 - core),
            device_id_type=MESH,
        )

    def tile_copy(which, t):
        source, target = ((own1, student_hbm), (d_res, d_res1_hbm), (d_context, d_context_hbm))[
            which
        ]
        return pltpu.make_async_copy(
            source.at[rows(t)], target.at[rows(t)], tile_sem.at[which, t]
        )

    def phase1(t, _):
        part = mul(context_ref[rows(t)], w_out_ref[...], NT)
        own1[rows(t)] = part.astype(jnp.bfloat16)
        exchange(0, t).start()

    lax.fori_loop(0, tiles, phase1, None)
    loads[0].wait()
    loads[1].wait()
    loads[2].wait()

    def summed(source, target, t):
        return source[rows(t)].astype(jnp.float32) + target[rows(t)].astype(jnp.float32)

    def phase2(t, _):
        exchange(0, t).wait()
        rows_in = tokens[rows(t)].astype(jnp.float32) + summed(own1, got1, t) * gate0
        normal, scale = normalize(rows_in)
        normal1[rows(t)] = normal
        scale1[rows(t)] = scale
        hidden = normal * gain1 + bias1
        low = hidden.astype(jnp.bfloat16)
        hidden_t[:, rows(t)] = jnp.transpose(hidden).astype(jnp.bfloat16)
        for n in range(units // PART):
            up = mul(low, w_in[:, lanes(n)])
            below, density = normal_parts(up)
            gate = unit_gate_ref[:, lanes(n)]
            gated[rows(t), lanes(n)] = (up * below * gate).astype(jnp.bfloat16)
            slope[rows(t), lanes(n)] = ((below + density) * gate).astype(jnp.bfloat16)
        part = mul(gated[rows(t)], w_fo[...], NT)
        own2[rows(t)] = part.astype(jnp.bfloat16)
        exchange(1, t).start()

    lax.fori_loop(0, tiles, phase2, None)
    loads[3].wait()

    def phase3(t, _):
        exchange(1, t).wait()
        ffn = summed(own2, got2, t)
        hidden = normal1[rows(t)] * gain1 + bias1
        normal, scale = normalize(hidden + ffn * gate1)
        student = normal * gain2 + bias2
        student_tile = student.astype(jnp.bfloat16)
        got2[rows(t)] = student_tile
        row = t // (ROW // TILE)
        end = lengths_ref[row, 0]
        for k in range(1, lengths_ref.shape[1]):
            end = end + lengths_ref[row, k]
        position = lax.broadcasted_iota(jnp.int32, (TILE, 1), 0) + (t % (ROW // TILE)) * TILE
        valid = (position < end).astype(jnp.float32)
        d_out = valid * (student - teacher[rows(t)].astype(jnp.float32))
        d_res2 = norm_back(d_out, normal, scale, gain2)
        d_res[rows(t)] = d_res2
        sums[2] += fold(d_out * normal)
        sums[3] += fold(d_out)
        sums[5] += fold(d_res2 * ffn)
        d_ffn = d_res2 * gate1
        d_ffn_t[:, rows(t)] = jnp.transpose(d_ffn).astype(jnp.bfloat16)
        d_ffn = d_ffn.astype(jnp.bfloat16)
        for n in range(units // PART):
            d_gated = mul(d_ffn, w_fo[:, lanes(n)])
            unit_sum[:, lanes(n)] += fold(
                d_gated * gated[rows(t), lanes(n)].astype(jnp.float32)
            )
            d_up = d_gated * slope[rows(t), lanes(n)].astype(jnp.float32)
            slope[rows(t), lanes(n)] = d_up.astype(jnp.bfloat16)
        part = mul(slope[rows(t)], w_in[...], NT)
        own2[rows(t)] = part.astype(jnp.bfloat16)
        exchange(2, t).start()
        pltpu.make_async_copy(
            got2.at[rows(t)], student_hbm.at[rows(t)], tile_sem.at[0, t]
        ).start()

    lax.fori_loop(0, tiles, phase3, None)

    def wide(which, n):
        target = grads_hbm.at[:, pl.ds(which * units + n * PART, PART)]
        return pltpu.make_async_copy(
            grad_wide.at[which, :, lanes(n)], target, grad_sem.at[which, n]
        )

    for n in range(units // PART):
        grad_wide[0, :, lanes(n)] = mul(d_ffn_t[...], gated[:, lanes(n)]).astype(jnp.bfloat16)
        wide(0, n).start()

    def phase4(t, _):
        exchange(2, t).wait()
        normal = normal1[rows(t)]
        d_hidden = d_res[rows(t)] + summed(own2, got3, t)
        sums[0] += fold(d_hidden * normal)
        sums[1] += fold(d_hidden)
        d_res1 = norm_back(d_hidden, normal, scale1[rows(t)], gain1)
        d_res[rows(t)] = d_res1
        tile_copy(1, t).start()
        sums[4] += fold(d_res1 * summed(own1, got1, t))
        d_attn = d_res1 * gate0
        d_attn_t[:, rows(t)] = jnp.transpose(d_attn).astype(jnp.bfloat16)
        d_context[rows(t)] = mul(d_attn.astype(jnp.bfloat16), w_out_ref[...])
        tile_copy(2, t).start()

    lax.fori_loop(0, tiles, phase4, None)
    for n in range(units // PART):
        grad_wide[1, :, lanes(n)] = mul(hidden_t[...], slope[:, lanes(n)]).astype(jnp.bfloat16)
        wide(1, n).start()
    grad_out[...] = mul(d_attn_t[...], context_ref[...]).astype(jnp.bfloat16)
    last = pltpu.make_async_copy(
        grad_out, grads_hbm.at[:, pl.ds(2 * units, grad_out.shape[1])], grad_sem.at[2, 0]
    )
    last.start()

    def line(i):
        return jnp.sum(sums[i], axis=0, keepdims=True)

    for i in range(4):
        small_ref[i : i + 1, :] = line(i)
    attn_line, ffn_line = line(4), line(5)
    small_ref[4:5, :] = ffn_line * gates_ref[1] + attn_line * gates_ref[0]
    unit_line = jnp.sum(unit_sum[...], axis=0, keepdims=True) / unit_gate_ref[...]
    for i in range(units // width):
        small_ref[5 + i : 6 + i, :] = unit_line[:, i * width : (i + 1) * width]
    lane = lax.broadcasted_iota(jnp.int32, (1, width), 1)
    layer0 = jnp.sum(attn_line * hidden_gate, axis=1, keepdims=True)
    layer1 = jnp.sum(ffn_line * hidden_gate, axis=1, keepdims=True)
    small_ref[7:8, :] = jnp.where(lane == 128, layer0, jnp.where(lane == 129, layer1, 0.0))

    def finish(t, _):
        pltpu.make_async_copy(
            got2.at[rows(t)], student_hbm.at[rows(t)], tile_sem.at[0, t]
        ).wait()
        tile_copy(1, t).wait()
        tile_copy(2, t).wait()

    lax.fori_loop(0, tiles, finish, None)
    for n in range(units // PART):
        wide(0, n).wait()
        wide(1, n).wait()
    last.wait()


def ffn(lengths, layer_gates, norm_p, hidden_gate, unit_gate, context, w_out_t, tokens, teacher, w_in, w_fo_t):
    count, width = tokens.shape
    units, heads = w_in.shape[1], context.shape[1]
    tiles = count // TILE
    vmem, smem = pl.BlockSpec(memory_space=pltpu.VMEM), pl.BlockSpec(memory_space=pltpu.SMEM)
    anywhere = pl.BlockSpec(memory_space=pl.ANY)
    low, full = jnp.bfloat16, jnp.float32
    return pl.pallas_call(
        ffn_kernel,
        in_specs=[smem, smem] + [vmem] * 5 + [anywhere] * 4,
        out_specs=[anywhere] * 4 + [vmem],
        out_shape=[
            jax.ShapeDtypeStruct((count, width), low),
            jax.ShapeDtypeStruct((count, width), full),
            jax.ShapeDtypeStruct((count, heads), full),
            jax.ShapeDtypeStruct((width, 2 * units + heads), low),
            jax.ShapeDtypeStruct((8, width), full),
        ],
        scratch_shapes=[
            pltpu.VMEM((width, units), low),
            pltpu.VMEM((width, units), low),
            pltpu.VMEM((count, width), low),
            pltpu.VMEM((count, width), low),
            *[pltpu.VMEM((count, width), low)] * 5,
            pltpu.VMEM((count, width), full),
            pltpu.VMEM((count, 1), full),
            pltpu.VMEM((count, units), low),
            pltpu.VMEM((count, units), low),
            pltpu.VMEM((count, width), full),
            pltpu.VMEM((count, heads), full),
            *[pltpu.VMEM((width, count), low)] * 3,
            pltpu.VMEM((2, width, units), low),
            pltpu.VMEM((width, heads), low),
            pltpu.VMEM((6, 8, width), full),
            pltpu.VMEM((8, units), full),
            pltpu.SemaphoreType.DMA((4,)),
            pltpu.SemaphoreType.DMA((3, tiles)),
            pltpu.SemaphoreType.DMA((3, units // PART)),
            pltpu.SemaphoreType.DMA((3, tiles)),
            pltpu.SemaphoreType.DMA((3, tiles)),
        ],
        compiler_params=pltpu.CompilerParams(
            collective_id=4, has_side_effects=True, vmem_limit_bytes=60 << 20
        ),
        name="ffn",
    )(lengths, layer_gates, norm_p, hidden_gate[None, :], unit_gate[None, :], context, w_out_t, tokens, teacher, w_in, w_fo_t)


def lamb_moments(master, first, second, grad, decay):
    new_first = MOMENT_DECAY * first + (1.0 - MOMENT_DECAY) * grad
    new_second = MOMENT_DECAY * second + (1.0 - MOMENT_DECAY) * grad * grad
    correction = 1.0 - MOMENT_DECAY**STEP_COUNT
    update = (
        new_first / correction / (jnp.sqrt(new_second / correction) + LAMB_EPS) + decay * master
    )
    return (new_first, new_second, update)


BLOCK = 384
DEPTH = (1, 3, 2, 0)


def layer_kernel(
    lengths_ref,
    gates_ref,
    head_gate_ref,
    hidden_gate_ref,
    unit_gate_ref,
    *refs,
):
    masters, norms_refs, moments_hbm, refs = refs[:4], refs[4:7], refs[7:15], refs[15:]
    (
        tokens_hbm,
        teacher_hbm,
        student_hbm,
        grad_tokens_hbm,
        sums_ref,
        small_out,
        norm_out,
        total_out,
        w,
        w_norm,
        tokens,
        qkv,
        d_mix,
        context,
        stats,
        left_t,
        hidden_t,
        own1,
        got1,
        own2,
        got2,
        got3,
        normal1,
        scale1,
        gated,
        slope,
        d_res,
        keep,
        gains,
        sums,
        unit_sum,
        heads,
        small_plane,
        small_line,
        norm_plane,
        norm_line,
        gate_row,
        unit_row,
        norm_pad,
        fo_copy,
        load_sem,
        tile_sem,
        all_send,
        all_recv,
        swap_send,
        swap_recv,
        send_sem,
        recv_sem,
        small_send,
        small_recv,
        stash_sem,
        moment_sem,
        free1,
        free2,
        free3,
    ) = refs
    me, core = lax.axis_index("dp"), lax.axis_index("head")
    z, y, x = place(me)
    rows, blocks = sums_ref.shape[0], sums_ref.shape[1] // BLOCK
    count, width = tokens.shape
    tiles, tall = count // TILE, count // ROW
    units, own_width = unit_gate_ref.shape[0], masters[1].shape[1]
    lane = lax.broadcasted_iota(jnp.int32, (1, own_width), 1)
    gate_lanes = jnp.zeros((1, own_width), jnp.float32)
    for head in range(own_width // HEAD_DIM):
        gate_lanes = jnp.where(lane // HEAD_DIM == head, head_gate_ref[head], gate_lanes)
    gate_row[...] = gate_lanes
    unit_row[...] = unit_gate_ref[...].reshape(1, units)
    pairs = own_width // PAIR
    at_out, at_in = 3 * own_width, 4 * own_width
    at_fo = at_in + units

    def load(which, t):
        source = (tokens_hbm, teacher_hbm)[which % 2]
        return pltpu.make_async_copy(
            source.at[tile(t)], tokens.at[tile(t)], load_sem.at[which, t]
        )

    def tile(t):
        return pl.ds(pl.multiple_of(t * TILE, TILE), TILE)

    def tall_row(r):
        return pl.ds(pl.multiple_of(r * ROW, ROW), ROW)

    def each(action, begin, end):
        lax.fori_loop(begin, end, lambda i, _: action(i), None)

    each(lambda t: load(0, t).start(), 0, tiles)

    line_peers = [(index(lax.rem(z + d, NZ), y, x), core) for d in (1, 2, 3)]
    plane = [index(z, y + (1 - 2 * y) * (d // 2), x + (1 - 2 * x) * (d % 2)) for d in range(4)]
    ring = [(plane[1], core), (plane[2], core), *line_peers]
    sibling = (me, 1 - core)
    greet([(p, core) for p in plane[1:]] + [(p, 1 - core) for p in plane] + line_peers)

    def rows_of(device):
        return pl.ds(pl.multiple_of(device * rows, rows), rows)

    def columns(c):
        start = c * BLOCK
        return pl.ds(start if isinstance(c, int) else pl.multiple_of(start, BLOCK), BLOCK)

    def turned(odd, rz, ra, rb):
        flip_x = ra * (1 - odd) + rb * odd
        flip_y = rb * (1 - odd) + ra * odd
        return index(lax.rem(z + rz, NZ), y + (1 - 2 * y) * flip_y, x + (1 - 2 * x) * flip_x)

    def view(c, device):
        if isinstance(c, int) and c == blocks:
            return w_norm.at[rows_of(device)]
        return w.at[rows_of(device), columns(c)]

    def move(c, place_of, to, there, k):
        block = view(c, turned(c % 2, *place_of))
        return pltpu.make_async_remote_copy(
            src_ref=block,
            dst_ref=block,
            send_sem=all_send.at[c, k],
            recv_sem=all_recv.at[c, there],
            device_id=(to, core),
            device_id_type=MESH,
        )

    def near(c):
        return turned(c % 2, 0, 1, 0)

    def far(c):
        return turned(c % 2, 0, 0, 1)

    def arrived(c, rz, ra, rb):
        move(c, (rz, ra, rb), me, slot(rz, ra, rb), 0).wait_recv()

    def all_first(c):
        for i, dz in enumerate((1, 3, 2)):
            move(c, (0, 0, 0), line_peers[dz - 1][0], slot(NZ - dz, 0, 0), i).start()
        move(c, (0, 0, 0), near(c), slot(0, 1, 0), 3).start()
        move(c, (0, 0, 0), far(c), slot(0, 0, 1), 7).start()

    def all_second(c):
        for i, rz in enumerate((1, 3, 2)):
            arrived(c, rz, 0, 0)
            move(c, (rz, 0, 0), near(c), slot(rz, 1, 0), 4 + i).start()
            move(c, (rz, 0, 0), far(c), slot(rz, 0, 1), 8 + i).start()

    def all_third(c):
        for i, rz in enumerate((0, 1, 3, 2)):
            arrived(c, rz, 1, 0)
            move(c, (rz, 1, 0), far(c), slot(rz, 1, 1), 11 + i).start()

    def all_turn(c):
        arrived(c, 0, 1, 0)
        for i, dz in enumerate((1, 3, 2)):
            move(c, (0, 1, 0), line_peers[dz - 1][0], slot(NZ - dz, 1, 0), 4 + i).start()
        move(c, (0, 1, 0), far(c), slot(0, 1, 1), 11).start()

    def all_lined(c, ra):
        for i, rz in enumerate((1, 3, 2)):
            arrived(c, rz, ra, 0)
            move(c, (rz, ra, 0), far(c), slot(rz, ra, 1), 8 + 4 * ra + i).start()

    def all_own_line(c):
        all_lined(c, 0)

    def all_near_line(c):
        all_lined(c, 1)

    def all_last(c):
        for ra in (0, 1):
            for rz in range(NZ):
                arrived(c, rz, ra, 1)

    def all_sent(c):
        for k in range(15):
            move(c, (0, 0, 0), me, 0, k).wait_send()

    mine = rows_of(me)
    for pair in range(pairs):
        for part in range(3):
            lanes = slice((3 * pair + part) * PAIR, (3 * pair + part + 1) * PAIR)
            w[mine, lanes] = masters[0][part, :, pair * PAIR : (pair + 1) * PAIR].astype(jnp.bfloat16)
    norm_pad[...] = jnp.zeros_like(norm_pad)
    norm_pad[0:4, 0:rows] = norms_refs[0][...]
    w_norm[mine] = jnp.transpose(norm_pad[...])[:rows].astype(jnp.bfloat16)
    w[mine, at_out:at_in] = masters[1][...].astype(jnp.bfloat16)
    each(all_first, 0, 2)
    all_first(blocks)
    w[mine, at_in:at_fo] = masters[2][...].astype(jnp.bfloat16)
    w[mine, at_fo:] = masters[3][...].astype(jnp.bfloat16)
    each(all_first, 2, blocks)
    sums[...] = jnp.zeros_like(sums)
    heads[...] = jnp.zeros_like(heads)

    def two(action, p):
        each(action, 2 * p, 2 * p + 2)

    two(all_second, 0)
    all_second(blocks)
    two(all_second, 1)
    two(all_third, 0)
    all_third(blocks)
    two(all_turn, 4)
    two(all_turn, 5)
    each(lambda t: load(0, t).wait(), 0, tiles)

    def pair_lanes(pair):
        return pl.ds(pl.multiple_of(pair * PAIR, PAIR), PAIR)

    def attend(pair, _):
        all_last(pair)
        span = pl.multiple_of(pair * BLOCK, BLOCK)

        def row(r, _):
            here = tall_row(r)
            same = segments(lengths_ref, r, (ROW, 1), 0) == segments(lengths_ref, r, (1, ROW), 1)
            part = mul(tokens[here], w[:, pl.ds(span, BLOCK)]).astype(jnp.bfloat16)
            qkv[here, pl.ds(span, BLOCK)] = part
            mix, totals = attend_pair(
                same, *(part[:, i * PAIR : (i + 1) * PAIR] for i in range(3))
            )
            for head in (0, 1):
                stats[r, pair, head : head + 1, :] = totals[head]
            lanes = pair_lanes(pair)
            context[here, lanes] = (mix * gate_row[:, lanes]).astype(jnp.bfloat16)

            @pl.when((r == 1) & (pair < 2))
            def _():
                two(all_second, 2 + pair)
                two(all_third, 1 + pair)

            @pl.when((r == 1) & (pair == 2))
            def _():
                two(all_own_line, 4)
                two(all_third, 3)

        lax.fori_loop(0, tall, row, None)

    lax.fori_loop(0, pairs, attend, None)
    two(all_own_line, 5)
    all_last(3)

    def swap(step, t):
        source, target = ((own1, got1), (own2, got2), (own2, got3), (own2, got3))[step]
        return pltpu.make_async_remote_copy(
            src_ref=source.at[tile(t)],
            dst_ref=target.at[tile(t)],
            send_sem=swap_send.at[step, t],
            recv_sem=swap_recv.at[step, t],
            device_id=sibling,
            device_id_type=MESH,
        )

    def phase1(t, _):
        part = mul(context[tile(t)], w[:, at_out:at_in], NT)
        own1[tile(t)] = part.astype(jnp.bfloat16)
        swap(0, t).start()

    lax.fori_loop(0, tiles, phase1, None)
    all_last(blocks)
    gains[...] = jnp.transpose(w_norm[...].astype(jnp.float32))[:8]
    gain1, bias1, gain2, bias2 = (gains[i : i + 1, :] for i in range(4))
    hidden_gate = hidden_gate_ref[...].reshape(1, width)
    gate0, gate1 = hidden_gate * gates_ref[0], hidden_gate * gates_ref[1]
    each(all_last, 4, 8)

    def summed(source, target, t):
        return source[tile(t)].astype(jnp.float32) + target[tile(t)].astype(jnp.float32)

    def part_lanes(n):
        return slice(n * PART, (n + 1) * PART)

    def phase2(t, _):
        swap(0, t).wait()
        rows_in = tokens[tile(t)].astype(jnp.float32) + summed(own1, got1, t) * gate0
        load(1, t).start()
        normal, scale = normalize(rows_in)
        normal1[tile(t)] = normal
        scale1[tile(t)] = scale
        hidden = normal * gain1 + bias1
        low = hidden.astype(jnp.bfloat16)
        hidden_t[:, tile(t)] = jnp.transpose(hidden).astype(jnp.bfloat16)
        for n in range(units // PART):
            up = mul(low, w[:, at_in + n * PART : at_in + (n + 1) * PART])
            below, density = normal_parts(up)
            gate = unit_row[:, part_lanes(n)]
            gated[tile(t), part_lanes(n)] = (up * below * gate).astype(jnp.bfloat16)
            slope[tile(t), part_lanes(n)] = ((below + density) * gate).astype(jnp.bfloat16)

        @pl.when(t == 1)
        def _():
            two(all_near_line, 4)

        @pl.when(t == 3)
        def _():
            two(all_near_line, 5)

    lax.fori_loop(0, tiles, phase2, None)
    each(all_last, 8, blocks)
    stash_fo = pltpu.make_async_copy(w.at[:, at_fo:], fo_copy, stash_sem.at[2])
    stash_fo.start()

    def down(t, _):
        part = mul(gated[tile(t)], w[:, at_fo:], NT)
        own2[tile(t)] = part.astype(jnp.bfloat16)
        swap(1, t).start()

    lax.fori_loop(0, tiles, down, None)
    each(all_sent, 0, blocks)
    all_sent(blocks)

    def student_out(t):
        return pltpu.make_async_copy(
            got2.at[tile(t)], student_hbm.at[tile(t)], tile_sem.at[0, t]
        )

    def phase3(t, _):
        swap(1, t).wait()
        load(1, t).wait()
        ffn = summed(own2, got2, t)
        hidden = normal1[tile(t)] * gain1 + bias1
        normal, scale = normalize(hidden + ffn * gate1)
        student = normal * gain2 + bias2
        got2[tile(t)] = student.astype(jnp.bfloat16)
        student_out(t).start()
        row = t // (ROW // TILE)
        end = lengths_ref[row, 0]
        for k in range(1, lengths_ref.shape[1]):
            end = end + lengths_ref[row, k]
        position = lax.broadcasted_iota(jnp.int32, (TILE, 1), 0) + (t % (ROW // TILE)) * TILE
        valid = (position < end).astype(jnp.float32)
        d_out = valid * (student - tokens[tile(t)].astype(jnp.float32))
        load(2, t).start()
        d_res2 = norm_back(d_out, normal, scale, gain2)
        d_res[tile(t)] = d_res2
        sums[2] += fold(d_out * normal)
        sums[3] += fold(d_out)
        sums[5] += fold(d_res2 * ffn)
        d_ffn = d_res2 * gate1
        left_t[:, tile(t)] = jnp.transpose(d_ffn).astype(jnp.bfloat16)

    lax.fori_loop(0, tiles, phase3, None)

    late_fo = at_fo // BLOCK
    grid_w = w.reshape(NZ, NY, NX, rows, w.shape[1])

    def landing(c, stage, i=0):
        buffer, n = (got2, c - late_fo) if c >= late_fo else (gated, c)
        across = buffer.shape[1] // BLOCK
        if stage == 1:
            view = buffer.reshape(4, NZ, 2, rows, buffer.shape[1])
            return view.at[n // across, :, :, :, pl.ds(n % across * BLOCK, BLOCK)]
        if stage == 2:
            view = buffer.reshape(8, NZ, rows, buffer.shape[1])
            return view.at[4 + n // across, :, :, pl.ds(n % across * BLOCK, BLOCK)]
        at = 24 * across + 3 * n + i
        view = buffer.reshape(32, rows, buffer.shape[1])
        return view.at[at // across, :, pl.ds(at % across * BLOCK, BLOCK)]

    def remote(source, target, c, k, to):
        return pltpu.make_async_remote_copy(
            src_ref=source,
            dst_ref=target,
            send_sem=send_sem.at[c, k],
            recv_sem=recv_sem.at[c, k],
            device_id=(to, core),
            device_id_type=MESH,
        )

    def half(c, other):
        if c % 2:
            return grid_w.at[:, :, 1 - x if other else x, :, columns(c)]
        return grid_w.at[:, 1 - y if other else y, :, :, columns(c)]

    def quarter(c, other):
        if c % 2:
            return grid_w.at[:, 1 - y if other else y, x, :, columns(c)]
        return grid_w.at[:, y, 1 - x if other else x, :, columns(c)]

    def side(c, other):
        mine_at = y if c % 2 else x
        return 1 - mine_at if other else mine_at

    def leg1(c):
        return remote(half(c, True), landing(c, 1), c, 0, far(c))

    def leg2(c):
        return remote(quarter(c, True), landing(c, 2), c, 1, near(c))

    def leg3(c, rz):
        source = grid_w.at[lax.rem(z + rz, NZ), y, x, :, columns(c)]
        there = NZ - rz
        return remote(source, landing(c, 3, there - 1), c, 1 + there, line_peers[rz - 1][0])

    def first(c):
        leg1(c).start()

    def second(c):
        leg1(c).wait_recv()
        came = landing(c, 1)
        block = quarter(c, True)
        total = block[...].astype(jnp.float32) + came[:, side(c, True)].astype(jnp.float32)
        block[...] = total.astype(jnp.bfloat16)
        leg2(c).start()
        block = quarter(c, False)
        total = block[...].astype(jnp.float32) + came[:, side(c, False)].astype(jnp.float32)
        keep[c % 8] = total

    def third(c):
        leg2(c).wait_recv()
        total = keep[c % 8] + landing(c, 2)[...].astype(jnp.float32)
        keep[c % 8] = total
        quarter(c, False)[...] = total.astype(jnp.bfloat16)
        for rz in (1, 3, 2):
            leg3(c, rz).start()

    def last(c):
        for rz in (1, 2, 3):
            leg3(c, rz).wait_recv()
        total = keep[c % 8, z]
        for i in range(3):
            total = total + landing(c, 3, i)[...].astype(jnp.float32)
        sums_ref[:, columns(c)] = total

    def down_from(action, i, n):
        for j in range(i, i + n):
            action(blocks - 1 - j)

    def weigh(left, right, start, size):
        for n in range(size // BLOCK):
            lanes = slice(start + n * BLOCK, start + (n + 1) * BLOCK)
            w[:, lanes] = mul(left[...], right[:, n * BLOCK : (n + 1) * BLOCK]).astype(jnp.bfloat16)

    def ready(semaphore, peers):
        for peer in peers:
            pl.semaphore_signal(semaphore, inc=1, device_id=peer, device_id_type=MESH)
        pl.semaphore_wait(semaphore, len(peers))

    each(lambda t: student_out(t).wait(), 0, tiles)
    stash_fo.wait()
    ready(free1, ring)
    for n in range(units // BLOCK - 1, -1, -1):
        lanes = slice(n * BLOCK, (n + 1) * BLOCK)
        grad = mul(left_t[...], gated[:, lanes])
        w[:, at_fo + n * BLOCK : at_fo + (n + 1) * BLOCK] = grad.astype(jnp.bfloat16)
        unit_sum[:, lanes] = fold(grad * fo_copy[:, lanes].astype(jnp.float32))
        first(late_fo + n)

    def phase3_units(t, _):
        d_ffn = (d_res[tile(t)] * gate1).astype(jnp.bfloat16)
        for n in range(units // PART):
            d_gated = mul(d_ffn, fo_copy[:, part_lanes(n)])
            d_up = d_gated * slope[tile(t), part_lanes(n)].astype(jnp.float32)
            slope[tile(t), part_lanes(n)] = d_up.astype(jnp.bfloat16)
        part = mul(slope[tile(t)], w[:, at_in:at_fo], NT)
        own2[tile(t)] = part.astype(jnp.bfloat16)
        swap(2, t).start()

        @pl.when(t == 3)
        def _():
            down_from(second, 0, 2)

    lax.fori_loop(0, tiles, phase3_units, None)
    down_from(second, 2, 2)
    ready(free2, ring)
    down_from(third, 0, 2)
    for n in range(units // BLOCK - 1, -1, -1):
        weigh(hidden_t, slope.at[:, n * BLOCK : (n + 1) * BLOCK], at_in + n * BLOCK, BLOCK)
        first(at_in // BLOCK + n)

    def moment(i, p, n):
        band = (8 * i + (0, 3, 4, 6)[p] + n) * rows
        return normal1.at[band : band + rows, : own_width if p < 2 else width]

    def moment_pieces(i):
        qkv_m, out_m, in_m, fo_m = moments_hbm[4 * i : 4 * i + 4]
        found = [(0, n, qkv_m.at[n]) for n in range(3)] + [(1, 0, out_m)]
        for p, array in ((2, in_m), (3, fo_m)):
            found += [(p, n, array.at[:, n * width : (n + 1) * width]) for n in range(2)]
        return found

    def phase4(t, _):
        swap(2, t).wait()
        normal = normal1[tile(t)]
        d_hidden = d_res[tile(t)] + summed(own2, got3, t)
        sums[0] += fold(d_hidden * normal)
        sums[1] += fold(d_hidden)
        d_res1 = norm_back(d_hidden, normal, scale1[tile(t)], gain1)
        d_res[tile(t)] = d_res1
        sums[4] += fold(d_res1 * summed(own1, got1, t))
        d_attn = d_res1 * gate0
        left_t[:, tile(t)] = jnp.transpose(d_attn).astype(jnp.bfloat16)
        d_context = mul(d_attn.astype(jnp.bfloat16), w[:, at_out:at_in])
        d_mix[tile(t)] = (d_context * gate_row[...]).astype(jnp.bfloat16)
        load(2, t).wait()
        hidden_t[:, tile(t)] = jnp.transpose(tokens[tile(t)].astype(jnp.float32)).astype(jnp.bfloat16)

    lax.fori_loop(0, tiles, phase4, None)
    pl.semaphore_signal(free3, inc=1, device_id=sibling, device_id_type=MESH)
    stash = [
        pltpu.make_async_copy(
            w.at[:, i * width : min((i + 1) * width, at_out)],
            own1.at[i * width : (i + 1) * width, : min((i + 1) * width, at_out) - i * width],
            stash_sem.at[i],
        )
        for i in range(2)
    ]
    for one in stash:
        one.start()
    moment_loads = [
        pltpu.make_async_copy(source, moment(i, p, n), moment_sem.at[i, at])
        for i in range(2)
        for at, (p, n, source) in enumerate(moment_pieces(i))
    ]
    for one in moment_loads:
        one.start()
    weigh(left_t, context, at_out, own_width)
    first(at_out // BLOCK)
    down_from(third, 2, 2)
    down_from(last, 0, 2)
    down_from(second, 4, 2)

    def pair_back(j, _):
        pair = pairs - 1 - j
        span = pl.multiple_of(pair * BLOCK, BLOCK)
        gate = gate_row[:, pl.ds(pl.multiple_of(pair * PAIR, PAIR), PAIR)]

        def row_back(r, _):
            here = tall_row(r)
            same = segments(lengths_ref, r, (ROW, 1), 0) == segments(lengths_ref, r, (1, ROW), 1)
            spans = [pl.ds(pl.multiple_of(span + i * PAIR, PAIR), PAIR) for i in range(3)]
            parts, weighed = attend_back(
                same,
                *(qkv[here, lanes] for lanes in spans),
                stats[r, pair],
                d_mix[here, pl.ds(pl.multiple_of(pair * PAIR, PAIR), PAIR)],
            )
            lane = lax.broadcasted_iota(jnp.int32, heads.shape, 1)
            for head in (0, 1):
                value = weighed[head] / gate[:, head * HEAD_DIM : head * HEAD_DIM + 1]
                heads[...] += jnp.where(lane == 2 * pair + head, value, 0.0)
            for lanes, value in zip(spans, parts, strict=True):
                qkv[here, lanes] = value.astype(jnp.bfloat16)

            @pl.when((r == 1) & (j == 1))
            def _():
                down_from(second, 6, 2)

            @pl.when((r == 1) & (j == 2))
            def _():
                down_from(second, 8, 1)

        lax.fori_loop(0, tall, row_back, None)

        @pl.when(j == 0)
        def _():
            for one in stash:
                one.wait()

        w[:, pl.ds(span, BLOCK)] = mul(hidden_t[...], qkv[:, pl.ds(span, BLOCK)]).astype(jnp.bfloat16)
        for c in range(pairs):

            @pl.when(pair == c)
            def _(c=c):
                first(c)

        @pl.when(j == 0)
        def _():
            down_from(last, 2, 2)
            down_from(third, 4, 2)

        @pl.when(j == 1)
        def _():
            down_from(third, 6, 2)
            down_from(last, 4, 2)

    lax.fori_loop(0, pairs, pair_back, None)

    def tokens_out(t):
        return pltpu.make_async_copy(
            d_res.at[tile(t)], grad_tokens_hbm.at[tile(t)], tile_sem.at[1, t]
        )

    def share(t, _):
        part = mul(qkv[tile(t), :width], own1[:width], NT)
        part = part + mul(qkv[tile(t), width:], own1[width:, : at_out - width], NT)
        own2[tile(t)] = part.astype(jnp.bfloat16)
        swap(3, t).start()

    pl.semaphore_wait(free3, 1)
    lax.fori_loop(0, tiles, share, None)

    here_plane = y * NX + x

    def line_of(i):
        return jnp.sum(sums[i], axis=0, keepdims=True)

    for i in range(4):
        small_plane[here_plane, i : i + 1, :] = line_of(i)
    attn_line, ffn_line = line_of(4), line_of(5)
    small_plane[here_plane, 4:5, :] = ffn_line * gates_ref[1] + attn_line * gates_ref[0]
    unit_line = jnp.sum(unit_sum[...], axis=0, keepdims=True) / unit_row[...]
    for i in range(units // width):
        small_plane[here_plane, 5 + i : 6 + i, :] = unit_line[:, i * width : (i + 1) * width]
    lane = lax.broadcasted_iota(jnp.int32, (1, width), 1)
    layer0 = jnp.sum(attn_line * hidden_gate, axis=1, keepdims=True)
    layer1 = jnp.sum(ffn_line * hidden_gate, axis=1, keepdims=True)
    pair_line = jnp.where(lane == 128, layer0, jnp.where(lane == 129, layer1, 0.0))
    small_plane[here_plane, 7:8, :] = pair_line
    small_plane[here_plane, 7:8, :128] = heads[0:1]

    def spread(buffer, base, targets, at):
        copies = [
            pltpu.make_async_remote_copy(
                src_ref=buffer.at[at],
                dst_ref=buffer.at[at],
                send_sem=small_send.at[base + i],
                recv_sem=small_recv.at[base + i],
                device_id=to,
                device_id_type=MESH,
            )
            for i, to in enumerate(targets)
        ]
        for one in copies:
            one.start()
        return copies

    def added(buffer, copies):
        for one in copies:
            one.wait_recv()
        total = buffer[0]
        for at in range(1, buffer.shape[0]):
            total = total + buffer[at]
        return total

    sent1 = spread(small_plane, 0, [(p, core) for p in plane[1:]], here_plane)
    down_from(second, 9, 2)
    down_from(third, 8, 1)

    def finish(t, _):
        swap(3, t).wait()
        d_res[tile(t)] += summed(own2, got3, t)
        tokens_out(t).start()

    lax.fori_loop(0, tiles, finish, None)
    small_line[z] = added(small_plane, sent1)
    sent2 = spread(small_line, 3, line_peers, z)
    down_from(last, 6, 2)
    down_from(second, 11, 1)
    down_from(third, 9, 2)
    total = added(small_line, sent2)
    small_out[...] = total
    norm_grad = pltpu.roll(total, (width - me * rows) % width, 1)[:, :128]
    norm_out[...] = norm_grad
    down_from(third, 11, 1)

    row8 = lax.broadcasted_iota(jnp.int32, (8, 128), 0)
    lane8 = lax.broadcasted_iota(jnp.int32, (8, 128), 1)

    def put(tile8, row, weight, update):
        here = row8 == row
        return jnp.where(here & (lane8 == 0), weight, jnp.where(here & (lane8 == 1), update, tile8))

    def square(block):
        return jnp.sum(jnp.sum(block * block, axis=0, keepdims=True), axis=1, keepdims=True)

    tile8 = jnp.zeros((8, 128), jnp.float32)
    master, first_moment, second_moment = (ref[...] for ref in norms_refs)
    update = lamb_moments(master, first_moment, second_moment, norm_grad[:4, : master.shape[1]], 0.0)[2]
    for i in range(4):
        tile8 = put(tile8, 4 + i, 0.5 * square(master[i : i + 1]), 0.5 * square(update[i : i + 1]))

    def squares(p, n, lanes, start):
        master = masters[0][n, :, lanes] if p == 0 else masters[p][:, lanes]
        first_moment, second_moment = (
            moment(i, p, n)[...] if p else moment(i, p, n)[:, lanes] for i in range(2)
        )
        grad = sums_ref[:, start : start + master.shape[1]]
        update = lamb_moments(master, first_moment, second_moment, grad, WEIGHT_DECAY)[2]
        return square(master), square(update)

    def matrix(tile8, p, start):
        size = masters[p].shape[1]
        weights, updates = 0.0, 0.0
        for n in range(max(size // width, 1)):
            step = min(size, width)
            found = squares(p, n, slice(n * step, (n + 1) * step), start + n * step)
            weights, updates = weights + found[0], updates + found[1]
        return put(tile8, p, weights, updates)

    for one in moment_loads:
        one.wait()
    tile8 = matrix(matrix(tile8, 3, at_fo), 2, at_in)
    down_from(last, 8, 1)
    tile8 = matrix(tile8, 1, at_out)
    weights, updates = 0.0, 0.0
    for pair in range(pairs - 1, -1, -1):
        down_from(last, blocks - 1 - pair, 1)
        for part in range(3):
            lanes = slice(pair * PAIR, (pair + 1) * PAIR)
            found = squares(0, part, lanes, (3 * pair + part) * PAIR)
            weights, updates = weights + found[0], updates + found[1]
    tile8 = put(tile8, 0, weights, updates)
    here_cores = core * (NX * NY) + here_plane
    norm_plane[here_cores] = tile8
    targets = [(p, core) for p in plane[1:]] + [(p, 1 - core) for p in plane]
    sent3 = spread(norm_plane, 6, targets, here_cores)
    norm_line[z] = added(norm_plane, sent3)
    sent4 = spread(norm_line, 13, line_peers, z)
    total_out[...] = added(norm_line, sent4)
    for one in (*sent1, *sent2, *sent3, *sent4):
        one.wait_send()

    for c in range(blocks):
        leg1(c).wait_send()
        leg2(c).wait_send()
        for rz in (1, 2, 3):
            leg3(c, rz).wait_send()
    each(lambda t: tokens_out(t).wait(), 0, tiles)


def layer(lengths, layer_gates, head_gate, hidden_gate, unit_gate, norms, params, tokens, teacher):
    count, width = tokens.shape
    (rows, own_width), units = params[1].shape, unit_gate.shape[0]
    total = 4 * own_width + 2 * units
    tiles, tall, blocks = count // TILE, count // ROW, total // BLOCK
    vmem, smem = pl.BlockSpec(memory_space=pltpu.VMEM), pl.BlockSpec(memory_space=pltpu.SMEM)
    anywhere = pl.BlockSpec(memory_space=pl.ANY)
    low, full = jnp.bfloat16, jnp.float32
    return pl.pallas_call(
        layer_kernel,
        in_specs=[smem] * 3 + [vmem] * 9 + [anywhere] * 10,
        out_specs=[anywhere] * 2 + [vmem] * 4,
        out_shape=[
            jax.ShapeDtypeStruct((count, width), low),
            jax.ShapeDtypeStruct((count, width), full),
            jax.ShapeDtypeStruct((rows, total), full),
            jax.ShapeDtypeStruct((8, width), full),
            jax.ShapeDtypeStruct((8, 128), full),
            jax.ShapeDtypeStruct((8, 128), full),
        ],
        scratch_shapes=[
            pltpu.VMEM((width, total), low),
            pltpu.VMEM((width, 128), low),
            pltpu.VMEM((count, width), low),
            pltpu.VMEM((count, 3 * own_width), low),
            pltpu.VMEM((count, own_width), low),
            pltpu.VMEM((count, own_width), low),
            pltpu.VMEM((tall, own_width // PAIR, 8, ROW), full),
            pltpu.VMEM((width, count), low),
            pltpu.VMEM((width, count), low),
            *[pltpu.VMEM((count, width), low)] * 5,
            pltpu.VMEM((count, width), full),
            pltpu.VMEM((count, 1), full),
            pltpu.VMEM((count, units), low),
            pltpu.VMEM((count, units), low),
            pltpu.VMEM((count, width), full),
            pltpu.VMEM((8, NZ, rows, BLOCK), full),
            pltpu.VMEM((8, width), full),
            pltpu.VMEM((6, 8, width), full),
            pltpu.VMEM((8, units), full),
            pltpu.VMEM((8, 128), full),
            pltpu.VMEM((NX * NY, 8, width), full),
            pltpu.VMEM((NZ, 8, width), full),
            pltpu.VMEM((2 * NX * NY, 8, 128), full),
            pltpu.VMEM((NZ, 8, 128), full),
            pltpu.VMEM((1, own_width), full),
            pltpu.VMEM((1, units), full),
            pltpu.VMEM((128, 128), full),
            pltpu.VMEM((width, units), low),
            pltpu.SemaphoreType.DMA((3, tiles)),
            pltpu.SemaphoreType.DMA((2, tiles)),
            pltpu.SemaphoreType.DMA((blocks + 1, 15)),
            pltpu.SemaphoreType.DMA((blocks + 1, 16)),
            pltpu.SemaphoreType.DMA((4, tiles)),
            pltpu.SemaphoreType.DMA((4, tiles)),
            pltpu.SemaphoreType.DMA((blocks, 5)),
            pltpu.SemaphoreType.DMA((blocks, 5)),
            pltpu.SemaphoreType.DMA((16,)),
            pltpu.SemaphoreType.DMA((16,)),
            pltpu.SemaphoreType.DMA((3,)),
            pltpu.SemaphoreType.DMA((2, 8)),
            pltpu.SemaphoreType.REGULAR,
            pltpu.SemaphoreType.REGULAR,
            pltpu.SemaphoreType.REGULAR,
        ],
        compiler_params=pltpu.CompilerParams(
            collective_id=0, has_side_effects=True, vmem_limit_bytes=62 << 20
        ),
        name="layer",
    )(lengths, layer_gates, head_gate, hidden_gate, unit_gate, *params[:4], *norms, *params[4:], tokens, teacher)


PIECES = 4


def spans(shape):
    if len(shape) == 2:
        return [(slice(None), slice(None))]
    pairs = shape[2] // PAIR
    return [
        (part, slice(None), slice(pair * PAIR, (pair + 1) * PAIR))
        for pair in range(pairs)
        for part in range(3)
    ]


def update_kernel(count, small_ref, norm_ref, total_ref, *refs):
    norms_refs, refs = refs[:3], refs[3:]
    passed_in, sums_hbm, params_hbm, refs = refs[:count], refs[count], refs[count + 1 : count + 13], refs[count + 13 :]
    passed_out, made_hbm, refs = refs[:count], refs[count : count + 20], refs[count + 20 :]
    small_outs, refs = refs[:10], refs[10:]
    sums_ref, params, outs = refs[0], refs[1:13], refs[13:33]
    held, refs = refs[33 : 33 + count], refs[33 + count :]
    pass_in, pass_out, in_sem, out_sem = refs
    pieces = [
        (i, n, pl.ds(n * (a.shape[0] // PIECES), a.shape[0] // PIECES))
        for n in range(PIECES)
        for i, a in enumerate(held)
    ]
    passes_in = [
        pltpu.make_async_copy(passed_in[i].at[at], held[i].at[at], pass_in.at[i, n])
        for i, n, at in pieces
    ]
    passes_out = [
        pltpu.make_async_copy(held[i].at[at], passed_out[i].at[at], pass_out.at[i, n])
        for i, n, at in pieces
    ]
    loads = [
        pltpu.make_async_copy(source, target, in_sem.at[i])
        for i, (source, target) in enumerate(
            zip((*params_hbm, sums_hbm), (*params, sums_ref), strict=True)
        )
    ]
    stores = [
        pltpu.make_async_copy(source, target, out_sem.at[i])
        for i, (source, target) in enumerate(zip(outs, made_hbm, strict=True))
    ]
    loads[12].start()
    for p in range(4):
        for i in range(3):
            loads[4 * i + p].start()
    for one in passes_in:
        one.start()
    weight_norm = jnp.sqrt(total_ref[:, 0:1])
    update_norm = jnp.sqrt(total_ref[:, 1:2])
    trust = weight_norm / update_norm

    def step(row, targets, at, values, decay):
        master, first_moment, second_moment, grad = values
        new_first, new_second, update = lamb_moments(
            master, first_moment, second_moment, grad, decay
        )
        new_master = master - LEARN_RATE * trust[row] * update
        made = (grad, new_first, new_second, new_master, new_master.astype(jnp.bfloat16))
        for target, value in zip(targets, made, strict=True):
            target[at] = value

    loads[12].wait()
    start = 0
    for p in range(4):
        for i in range(3):
            loads[4 * i + p].wait()
        targets = outs[5 * p : 5 * p + 5]
        for at in spans(params[p].shape):
            width = params[p].shape[1] if len(at) == 2 else PAIR
            grad = sums_ref[:, start : start + width]
            values = (*(params[4 * i + p][at] for i in range(3)), grad)
            step(slice(p, p + 1), targets, at, values, WEIGHT_DECAY)
            start += width
        for one in stores[5 * p : 5 * p + 5]:
            one.start()
        if p == 0:
            for one, other in zip(passes_in, passes_out, strict=True):
                one.wait()
                other.start()
    norm_grad = norm_ref[:4, : norms_refs[0].shape[1]]
    values = (*(ref[...] for ref in norms_refs), norm_grad)
    step(slice(4, 8), small_outs[:5], (Ellipsis,), values, 0.0)
    stats_out, heads_out, units_out, hidden_out, layers_out = small_outs[5:]
    lane = lax.broadcasted_iota(jnp.int32, (8, 128), 1)
    stats = jnp.where(lane == 0, weight_norm, jnp.where(lane == 1, update_norm, trust))
    stats_out[...] = jnp.transpose(jnp.concatenate([stats] * 16, axis=0))[:3, :8]
    heads_out[...] = small_ref[7:8, : heads_out.shape[1]]
    width = small_ref.shape[1]
    for i in range(units_out.shape[0] // width):
        units_out[i * width : (i + 1) * width] = small_ref[5 + i : 6 + i, :].reshape(width)
    hidden_out[...] = small_ref[4:5, :].reshape(width)
    layers_out[...] = small_ref[7:8, 128:130]
    for one in (*stores, *passes_out):
        one.wait()


def update(passed, sums, small, norm_grad, totals, norms, params, sizes):
    vmem, anywhere = pl.BlockSpec(memory_space=pltpu.VMEM), pl.BlockSpec(memory_space=pltpu.HBM)
    big, little = [], []
    for master in params[:4]:
        big += [jax.ShapeDtypeStruct(master.shape, jnp.float32)] * 4
        big += [jax.ShapeDtypeStruct(master.shape, jnp.bfloat16)]
    little += [jax.ShapeDtypeStruct(norms[0].shape, jnp.float32)] * 4
    little += [jax.ShapeDtypeStruct(norms[0].shape, jnp.bfloat16)]
    little += [jax.ShapeDtypeStruct((3, 8), jnp.float32)]
    little += [jax.ShapeDtypeStruct(size, jnp.float32) for size in sizes]
    through = [jax.ShapeDtypeStruct(a.shape, a.dtype) for a in passed]
    made = pl.pallas_call(
        functools.partial(update_kernel, len(passed)),
        in_specs=[vmem] * 6 + [anywhere] * (len(passed) + 1 + len(params)),
        out_specs=[anywhere] * (len(passed) + len(big)) + [vmem] * len(little),
        out_shape=[*through, *big, *little],
        scratch_shapes=[
            pltpu.VMEM(sums.shape, jnp.float32),
            *[pltpu.VMEM(a.shape, a.dtype) for a in params],
            *[pltpu.VMEM(a.shape, a.dtype) for a in big],
            *[pltpu.VMEM(a.shape, a.dtype) for a in passed],
            pltpu.SemaphoreType.DMA((len(passed), PIECES)),
            pltpu.SemaphoreType.DMA((len(passed), PIECES)),
            pltpu.SemaphoreType.DMA((13,)),
            pltpu.SemaphoreType.DMA((20,)),
        ],
        compiler_params=pltpu.CompilerParams(vmem_limit_bytes=60 << 20),
        name="update",
    )(small, norm_grad, totals, *norms, *passed, sums, *params)
    return made[: len(passed)], made[len(passed) :]


def core_sum(part):
    part = part.astype(jnp.bfloat16)
    other = lax.ppermute(part, "head", [(0, 1), (1, 0)])
    return part.astype(jnp.float32) + other.astype(jnp.float32)


def plain_totals(sums, norm_grad, norms, params, head_count):
    found, start = [], 0
    for p in range(4):
        pair = jnp.zeros((2,), jnp.float32)
        for at in spans(params[p].shape):
            master, first_moment, second_moment = (params[4 * i + p][at] for i in range(3))
            grad = sums[:, start : start + master.shape[1]]
            update = lamb_moments(master, first_moment, second_moment, grad, WEIGHT_DECAY)[2]
            pair = pair + jnp.stack([jnp.sum(master * master), jnp.sum(update * update)])
            start += master.shape[1]
        found.append(pair)
    master, first_moment, second_moment = norms
    update = lamb_moments(master, first_moment, second_moment, norm_grad[:4, : master.shape[1]], 0.0)[2]
    rows = jnp.stack([jnp.sum(master * master, axis=1), jnp.sum(update * update, axis=1)], axis=1)
    found = jnp.concatenate([jnp.stack(found), rows / head_count])
    return jnp.pad(lax.psum(found, ("dp", "head")), ((0, 0), (0, 126)))


def rows_first(qkv):
    return jnp.transpose(qkv, (1, 0, 2))


def plain_layer(lengths, layer_gates, head_gate, hidden_gate, unit_gate, norms, params, tokens, teacher):
    heads_here, units = head_gate.shape[0], unit_gate.shape[0]
    rows, own_width = params[1].shape
    gate_lanes = jnp.repeat(head_gate, HEAD_DIM)[None, :]
    norm_shard = norms[0].T.astype(jnp.bfloat16)
    shards = [params[p][at] for p in range(4) for at in spans(params[p].shape)]
    shards = jnp.concatenate(shards, axis=1).astype(jnp.bfloat16)
    w, norm_t = (lax.all_gather(s, "dp", axis=0, tiled=True) for s in (shards, norm_shard))
    norm_p = norm_t.T.astype(jnp.float32)
    w_qkv, w_out_t, w_in, w_fo_t = jnp.split(
        w, (3 * own_width, 4 * own_width, 4 * own_width + units), axis=1
    )
    qkv = jnp.dot(tokens, w_qkv, preferred_element_type=jnp.float32).astype(jnp.bfloat16)
    context, stats = attention(qkv, lengths, gate_lanes)
    student, d_res1, d_context, grads, small = ffn(
        lengths,
        layer_gates,
        norm_p,
        hidden_gate,
        unit_gate,
        context,
        w_out_t,
        tokens,
        teacher,
        w_in,
        w_fo_t,
    )
    d_qkv, head_sums = attention_back(qkv, lengths, gate_lanes, stats, d_context)
    d_heads = jnp.sum(head_sums[:, :, 0, :2], axis=0).reshape(-1)
    grad_qkv = jnp.einsum("tc,tk->ck", tokens, d_qkv, preferred_element_type=jnp.float32)
    input_part = jnp.einsum("tk,ck->tc", d_qkv, w_qkv, preferred_element_type=jnp.float32)
    grad_tokens = d_res1 + core_sum(input_part)
    grad_fo, grad_in, grad_out = jnp.split(grads.astype(jnp.float32), (units, 2 * units), axis=1)
    grads = jnp.concatenate([grad_qkv, grad_out, grad_in, grad_fo], axis=1)
    sums = lax.psum_scatter(grads, "dp", scatter_dimension=0, tiled=True)
    small = lax.psum(small.at[7, :heads_here].set(d_heads), "dp")
    norm_grad = lax.dynamic_slice_in_dim(small, lax.axis_index("dp") * rows, rows, 1)
    norm_grad = jnp.pad(norm_grad, ((0, 0), (0, 128 - rows)))
    totals = plain_totals(sums, norm_grad, norms, params, lax.axis_size("head"))
    return student, grad_tokens, sums, small, norm_grad, totals


def local(
    tokens,
    teacher,
    lengths,
    head_gate,
    unit_gate,
    hidden_gate,
    layer_gates,
    master_qkv,
    first_qkv,
    second_qkv,
    master_attn_out,
    first_attn_out,
    second_attn_out,
    master_ffn_in,
    first_ffn_in,
    second_ffn_in,
    master_ffn_out,
    first_ffn_out,
    second_ffn_out,
    master_norms,
    first_norms,
    second_norms,
):
    ours = lax.axis_size("dp") == GRID and lax.axis_size("head") == 2
    params = [
        rows_first(master_qkv),
        master_attn_out.T,
        master_ffn_in,
        master_ffn_out.T,
        rows_first(first_qkv),
        first_attn_out.T,
        first_ffn_in,
        first_ffn_out.T,
        rows_first(second_qkv),
        second_attn_out.T,
        second_ffn_in,
        second_ffn_out.T,
    ]
    norms = [master_norms, first_norms, second_norms]
    run = layer if ours else plain_layer
    student, grad_tokens, sums, small, norm_grad, totals = run(
        lengths,
        layer_gates,
        head_gate,
        hidden_gate,
        unit_gate,
        norms,
        params,
        tokens,
        teacher,
    )
    sizes = ((1, head_gate.shape[0]), unit_gate.shape, hidden_gate.shape, (1, 2))
    (student, grad_tokens), made = update(
        (student, grad_tokens), sums, small, norm_grad, totals, norms, params, sizes
    )
    results = []
    for p in range(4):
        for value in made[5 * p : 5 * p + 5]:
            results.append(rows_first(value) if p == 0 else value if p == 2 else value.T)
    norm_results, (stats_rows, *gate_rows) = made[20:25], made[25:]
    gate_results = [row.reshape(-1) for row in gate_rows]
    return (
        student,
        grad_tokens,
        *gate_results,
        *results,
        *norm_results,
        stats_rows,
    )


def solution(mesh):
    return jax.shard_map(
        local,
        mesh=mesh,
        in_specs=(
            P("dp", None),
            P("dp", None),
            P("dp", None),
            P("head"),
            P("head"),
            P(),
            P(),
            P("dp", None, "head"),
            P("dp", None, "head"),
            P("dp", None, "head"),
            P("head", "dp"),
            P("head", "dp"),
            P("head", "dp"),
            P("dp", "head"),
            P("dp", "head"),
            P("dp", "head"),
            P("head", "dp"),
            P("head", "dp"),
            P("head", "dp"),
            P(None, "dp"),
            P(None, "dp"),
            P(None, "dp"),
        ),
        out_specs=(
            P("dp", None),
            P("dp", None),
            P("head"),
            P("head"),
            P(),
            P(),
            P("dp", None, "head"),
            P("dp", None, "head"),
            P("dp", None, "head"),
            P("dp", None, "head"),
            P("dp", None, "head"),
            P("head", "dp"),
            P("head", "dp"),
            P("head", "dp"),
            P("head", "dp"),
            P("head", "dp"),
            P("dp", "head"),
            P("dp", "head"),
            P("dp", "head"),
            P("dp", "head"),
            P("dp", "head"),
            P("head", "dp"),
            P("head", "dp"),
            P("head", "dp"),
            P("head", "dp"),
            P("head", "dp"),
            P(None, "dp"),
            P(None, "dp"),
            P(None, "dp"),
            P(None, "dp"),
            P(None, "dp"),
            P(),
        ),
        check_vma=False,
    )
```

```python
import functools

import jax
import jax.numpy as jnp
from jax import lax
from jax.experimental import pallas as pl
from jax.experimental.pallas import tpu as pltpu
from jax.sharding import PartitionSpec as P

D = 768
HEAD_DIM = 64
ROW = 512
STEP_COUNT = 5

LN_EPS = 1e-05
LAMB_EPS = 1e-06
WEIGHT_DECAY = 0.01
LEARN_RATE = 0.5
MOMENT_DECAY = 0.5
MASK_FILL = -1000000000.0


MESH = pl.DeviceIdType.MESH
NZ, NY, NX = 4, 2, 2
GRID = NZ * NY * NX


def place(me):
    return me // (NY * NX), (me // NX) % NY, me % NX


def index(z, y, x):
    return (z * NY + y) * NX + x


def slot(rz, ra, rb):
    return rz + NZ * (ra + 2 * rb)


def greet(peers):
    barrier = pltpu.get_barrier_semaphore()
    for peer in peers:
        pl.semaphore_signal(barrier, inc=1, device_id=peer, device_id_type=MESH)
    pl.semaphore_wait(barrier, len(peers))


NT = (((1,), (1,)), ((), ()))
NN = (((1,), (0,)), ((), ()))
PAIR = 2 * HEAD_DIM


def mul(a, b, dims=NN):
    return lax.dot_general(a, b, dims, preferred_element_type=jnp.float32)


def segments(lengths_ref, row, shape, axis):
    positions = lax.broadcasted_iota(jnp.int32, shape, axis)
    end = jnp.int32(0)
    found = jnp.zeros(shape, jnp.int32)
    for k in range(lengths_ref.shape[1]):
        end = end + lengths_ref[row, k]
        found = found + (positions >= end).astype(jnp.int32)
    return found


def flip(block):
    return jnp.transpose(block.astype(jnp.float32)).astype(block.dtype)


def head_lanes(block, head):
    lane = lax.broadcasted_iota(jnp.int32, block.shape, 1)
    inside = (lane < HEAD_DIM) if head == 0 else (lane >= HEAD_DIM)
    return jnp.where(inside, block, jnp.zeros_like(block))


def attend_pair(same, queries, keys, values):
    queries = queries * jnp.bfloat16(HEAD_DIM**-0.5)
    values_t = flip(values)
    mixes, totals = [], []
    for head in (0, 1):
        scores = mul(keys, head_lanes(queries, head), NT)
        scores = jnp.where(same, scores, MASK_FILL)
        top = jnp.max(scores, axis=0, keepdims=True)
        expo = jnp.exp(scores - top)
        total = jnp.sum(expo, axis=0, keepdims=True)
        probs = (expo * (1.0 / total)).astype(jnp.bfloat16)
        mixes.append(mul(values_t[head * HEAD_DIM : (head + 1) * HEAD_DIM], probs))
        totals.append(top + jnp.log(total))
    return jnp.transpose(jnp.concatenate(mixes, axis=0)), totals


def attend_back(same, queries, keys, values, stats, d_mix):
    queries = queries * jnp.bfloat16(HEAD_DIM**-0.5)
    keys_t = flip(keys)
    d_queries, d_keys, d_values, sums = [], None, None, []
    for head in (0, 1):
        q_one, d_one = head_lanes(queries, head), head_lanes(d_mix, head)
        scores = jnp.where(same, mul(keys, q_one, NT), MASK_FILL)
        probs = jnp.exp(scores - stats[head : head + 1, :])
        d_probs = mul(values, d_one, NT)
        weighed = jnp.sum(probs * d_probs, axis=0, keepdims=True)
        sums.append(jnp.sum(weighed, axis=1, keepdims=True))
        d_scores = (probs * (d_probs - weighed)).astype(jnp.bfloat16)
        dv = mul(probs.astype(jnp.bfloat16), d_one)
        dk = mul(d_scores, q_one)
        d_values = dv if head == 0 else d_values + dv
        d_keys = dk if head == 0 else d_keys + dk
        d_queries.append(mul(keys_t[head * HEAD_DIM : (head + 1) * HEAD_DIM], d_scores))
    dq = jnp.transpose(jnp.concatenate(d_queries, axis=0)) * HEAD_DIM**-0.5
    return (dq, d_keys, d_values), sums


def attention_kernel(lengths_ref, gate_ref, qkv_ref, context_ref, stats_ref):
    row = pl.program_id(0)
    same = segments(lengths_ref, row, (ROW, 1), 0) == segments(lengths_ref, row, (1, ROW), 1)
    mix, totals = attend_pair(same, *(qkv_ref[:, i * PAIR : (i + 1) * PAIR] for i in range(3)))
    for head in (0, 1):
        stats_ref[0, 0, head : head + 1, :] = totals[head]
    context_ref[...] = (mix * gate_ref[...]).astype(jnp.bfloat16)


def attention(qkv, lengths, gate_lanes):
    tokens, width = qkv.shape
    rows, pairs = lengths.shape[0], width // 3 // PAIR
    return pl.pallas_call(
        attention_kernel,
        grid=(rows, pairs),
        in_specs=[
            pl.BlockSpec(memory_space=pltpu.SMEM),
            pl.BlockSpec((1, PAIR), lambda r, h: (0, h)),
            pl.BlockSpec((ROW, 3 * PAIR), lambda r, h: (r, h)),
        ],
        out_specs=[
            pl.BlockSpec((ROW, PAIR), lambda r, h: (r, h)),
            pl.BlockSpec((1, 1, 8, ROW), lambda r, h: (r, h, 0, 0)),
        ],
        out_shape=[
            jax.ShapeDtypeStruct((tokens, width // 3), jnp.bfloat16),
            jax.ShapeDtypeStruct((rows, pairs, 8, ROW), jnp.float32),
        ],
        compiler_params=pltpu.CompilerParams(vmem_limit_bytes=32 << 20),
        name="attention",
    )(lengths, gate_lanes, qkv)


def attention_back_kernel(lengths_ref, gate_ref, qkv_ref, stats_ref, d_ref, out_ref, heads_ref):
    row = pl.program_id(0)
    same = segments(lengths_ref, row, (ROW, 1), 0) == segments(lengths_ref, row, (1, ROW), 1)
    gate = gate_ref[...]
    d_mix = (d_ref[...] * gate).astype(jnp.bfloat16)
    parts, weighed = attend_back(
        same, *(qkv_ref[:, i * PAIR : (i + 1) * PAIR] for i in range(3)), stats_ref[0, 0], d_mix
    )
    for i, value in enumerate(parts):
        out_ref[:, i * PAIR : (i + 1) * PAIR] = value.astype(jnp.bfloat16)
    lane = lax.broadcasted_iota(jnp.int32, (8, PAIR), 1)
    found = jnp.zeros((8, PAIR), jnp.float32)
    for head in (0, 1):
        value = weighed[head] / gate[:, head * HEAD_DIM : head * HEAD_DIM + 1]
        found = jnp.where(lane == head, value, found)
    heads_ref[0, 0] = found


def attention_back(qkv, lengths, gate_lanes, stats, d_context):
    tokens, width = qkv.shape
    rows, pairs = lengths.shape[0], width // 3 // PAIR
    wide = pl.BlockSpec((ROW, 3 * PAIR), lambda r, h: (r, h))
    return pl.pallas_call(
        attention_back_kernel,
        grid=(rows, pairs),
        in_specs=[
            pl.BlockSpec(memory_space=pltpu.SMEM),
            pl.BlockSpec((1, PAIR), lambda r, h: (0, h)),
            wide,
            pl.BlockSpec((1, 1, 8, ROW), lambda r, h: (r, h, 0, 0)),
            pl.BlockSpec((ROW, PAIR), lambda r, h: (r, h)),
        ],
        out_specs=[wide, pl.BlockSpec((1, 1, 8, PAIR), lambda r, h: (r, h, 0, 0))],
        out_shape=[
            jax.ShapeDtypeStruct((tokens, width), jnp.bfloat16),
            jax.ShapeDtypeStruct((rows, pairs, 8, PAIR), jnp.float32),
        ],
        compiler_params=pltpu.CompilerParams(vmem_limit_bytes=32 << 20),
        name="attention_back",
    )(lengths, gate_lanes, qkv, stats, d_context)


TILE = 256
PART = 256
TAIL_STEP = 0.3
TAIL = (
    0.11963200569152832,
    0.12071217596530914,
    0.10017567127943039,
    0.1276927888393402,
    -0.052036140114068985,
    0.2045592963695526,
    -0.15616002678871155,
    0.035424139350652695,
)


def normal_parts(u):
    bell = jnp.exp(-0.5 * u * u)
    t = 1.0 / (1.0 + TAIL_STEP * jnp.abs(u))
    series = TAIL[-1]
    for term in TAIL[-2::-1]:
        series = series * t + term
    tail = series * t * bell
    return jnp.where(u < 0, tail, 1.0 - tail), u * bell * 0.3989422804014327


def fold(block):
    return jnp.sum(block.reshape(-1, 8, block.shape[1]), axis=0)


def norm_back(d_out, normal, scale, gain):
    d_normal = d_out * gain
    d_normal = (
        d_normal
        - jnp.mean(d_normal, axis=-1, keepdims=True)
        - normal * jnp.mean(d_normal * normal, axis=-1, keepdims=True)
    )
    return d_normal * scale


def normalize(rows_in):
    center = rows_in - jnp.mean(rows_in, axis=-1, keepdims=True)
    scale = lax.rsqrt(jnp.mean(center * center, axis=-1, keepdims=True) + LN_EPS)
    return center * scale, scale


def ffn_kernel(
    lengths_ref,
    gates_ref,
    norm_ref,
    hidden_gate_ref,
    unit_gate_ref,
    context_ref,
    w_out_ref,
    tokens_hbm,
    teacher_hbm,
    w_in_hbm,
    w_fo_hbm,
    student_hbm,
    d_res1_hbm,
    d_context_hbm,
    grads_hbm,
    small_ref,
    w_in,
    w_fo,
    tokens,
    teacher,
    own1,
    own2,
    got1,
    got2,
    got3,
    normal1,
    scale1,
    gated,
    slope,
    d_res,
    d_context,
    hidden_t,
    d_ffn_t,
    d_attn_t,
    grad_wide,
    grad_out,
    sums,
    unit_sum,
    load_sem,
    tile_sem,
    grad_sem,
    send_sem,
    recv_sem,
):
    dp, core = lax.axis_index("dp"), lax.axis_index("head")
    loads = [
        pltpu.make_async_copy(source, target, load_sem.at[i])
        for i, (source, target) in enumerate(
            ((tokens_hbm, tokens), (w_in_hbm, w_in), (w_fo_hbm, w_fo), (teacher_hbm, teacher))
        )
    ]
    for one in loads:
        one.start()
    greet([(dp, 1 - core)])
    tiles = tokens.shape[0] // TILE
    units, width = w_in.shape[1], w_in.shape[0]
    sums[...] = jnp.zeros_like(sums)
    unit_sum[...] = jnp.zeros_like(unit_sum)
    hidden_gate = hidden_gate_ref[...]
    gate0, gate1 = hidden_gate * gates_ref[0], hidden_gate * gates_ref[1]
    gain1, bias1, gain2, bias2 = (norm_ref[i : i + 1, :] for i in range(4))

    def rows(t):
        return pl.ds(pl.multiple_of(t * TILE, TILE), TILE)

    def lanes(n):
        return pl.ds(n * PART, PART)

    def exchange(step, t):
        source, target = ((own1, got1), (own2, got2), (own2, got3))[step]
        return pltpu.make_async_remote_copy(
            src_ref=source.at[rows(t)],
            dst_ref=target.at[rows(t)],
            send_sem=send_sem.at[step, t],
            recv_sem=recv_sem.at[step, t],
            device_id=(dp, 1 - core),
            device_id_type=MESH,
        )

    def tile_copy(which, t):
        source, target = ((own1, student_hbm), (d_res, d_res1_hbm), (d_context, d_context_hbm))[
            which
        ]
        return pltpu.make_async_copy(
            source.at[rows(t)], target.at[rows(t)], tile_sem.at[which, t]
        )

    def phase1(t, _):
        part = mul(context_ref[rows(t)], w_out_ref[...], NT)
        own1[rows(t)] = part.astype(jnp.bfloat16)
        exchange(0, t).start()

    lax.fori_loop(0, tiles, phase1, None)
    loads[0].wait()
    loads[1].wait()
    loads[2].wait()

    def summed(source, target, t):
        return source[rows(t)].astype(jnp.float32) + target[rows(t)].astype(jnp.float32)

    def phase2(t, _):
        exchange(0, t).wait()
        rows_in = tokens[rows(t)].astype(jnp.float32) + summed(own1, got1, t) * gate0
        normal, scale = normalize(rows_in)
        normal1[rows(t)] = normal
        scale1[rows(t)] = scale
        hidden = normal * gain1 + bias1
        low = hidden.astype(jnp.bfloat16)
        hidden_t[:, rows(t)] = jnp.transpose(hidden).astype(jnp.bfloat16)
        for n in range(units // PART):
            up = mul(low, w_in[:, lanes(n)])
            below, density = normal_parts(up)
            gate = unit_gate_ref[:, lanes(n)]
            gated[rows(t), lanes(n)] = (up * below * gate).astype(jnp.bfloat16)
            slope[rows(t), lanes(n)] = ((below + density) * gate).astype(jnp.bfloat16)
        part = mul(gated[rows(t)], w_fo[...], NT)
        own2[rows(t)] = part.astype(jnp.bfloat16)
        exchange(1, t).start()

    lax.fori_loop(0, tiles, phase2, None)
    loads[3].wait()

    def phase3(t, _):
        exchange(1, t).wait()
        ffn = summed(own2, got2, t)
        hidden = normal1[rows(t)] * gain1 + bias1
        normal, scale = normalize(hidden + ffn * gate1)
        student = normal * gain2 + bias2
        student_tile = student.astype(jnp.bfloat16)
        got2[rows(t)] = student_tile
        row = t // (ROW // TILE)
        end = lengths_ref[row, 0]
        for k in range(1, lengths_ref.shape[1]):
            end = end + lengths_ref[row, k]
        position = lax.broadcasted_iota(jnp.int32, (TILE, 1), 0) + (t % (ROW // TILE)) * TILE
        valid = (position < end).astype(jnp.float32)
        d_out = valid * (student - teacher[rows(t)].astype(jnp.float32))
        d_res2 = norm_back(d_out, normal, scale, gain2)
        d_res[rows(t)] = d_res2
        sums[2] += fold(d_out * normal)
        sums[3] += fold(d_out)
        sums[5] += fold(d_res2 * ffn)
        d_ffn = d_res2 * gate1
        d_ffn_t[:, rows(t)] = jnp.transpose(d_ffn).astype(jnp.bfloat16)
        d_ffn = d_ffn.astype(jnp.bfloat16)
        for n in range(units // PART):
            d_gated = mul(d_ffn, w_fo[:, lanes(n)])
            unit_sum[:, lanes(n)] += fold(
                d_gated * gated[rows(t), lanes(n)].astype(jnp.float32)
            )
            d_up = d_gated * slope[rows(t), lanes(n)].astype(jnp.float32)
            slope[rows(t), lanes(n)] = d_up.astype(jnp.bfloat16)
        part = mul(slope[rows(t)], w_in[...], NT)
        own2[rows(t)] = part.astype(jnp.bfloat16)
        exchange(2, t).start()
        pltpu.make_async_copy(
            got2.at[rows(t)], student_hbm.at[rows(t)], tile_sem.at[0, t]
        ).start()

    lax.fori_loop(0, tiles, phase3, None)

    def wide(which, n):
        target = grads_hbm.at[:, pl.ds(which * units + n * PART, PART)]
        return pltpu.make_async_copy(
            grad_wide.at[which, :, lanes(n)], target, grad_sem.at[which, n]
        )

    for n in range(units // PART):
        grad_wide[0, :, lanes(n)] = mul(d_ffn_t[...], gated[:, lanes(n)]).astype(jnp.bfloat16)
        wide(0, n).start()

    def phase4(t, _):
        exchange(2, t).wait()
        normal = normal1[rows(t)]
        d_hidden = d_res[rows(t)] + summed(own2, got3, t)
        sums[0] += fold(d_hidden * normal)
        sums[1] += fold(d_hidden)
        d_res1 = norm_back(d_hidden, normal, scale1[rows(t)], gain1)
        d_res[rows(t)] = d_res1
        tile_copy(1, t).start()
        sums[4] += fold(d_res1 * summed(own1, got1, t))
        d_attn = d_res1 * gate0
        d_attn_t[:, rows(t)] = jnp.transpose(d_attn).astype(jnp.bfloat16)
        d_context[rows(t)] = mul(d_attn.astype(jnp.bfloat16), w_out_ref[...])
        tile_copy(2, t).start()

    lax.fori_loop(0, tiles, phase4, None)
    for n in range(units // PART):
        grad_wide[1, :, lanes(n)] = mul(hidden_t[...], slope[:, lanes(n)]).astype(jnp.bfloat16)
        wide(1, n).start()
    grad_out[...] = mul(d_attn_t[...], context_ref[...]).astype(jnp.bfloat16)
    last = pltpu.make_async_copy(
        grad_out, grads_hbm.at[:, pl.ds(2 * units, grad_out.shape[1])], grad_sem.at[2, 0]
    )
    last.start()

    def line(i):
        return jnp.sum(sums[i], axis=0, keepdims=True)

    for i in range(4):
        small_ref[i : i + 1, :] = line(i)
    attn_line, ffn_line = line(4), line(5)
    small_ref[4:5, :] = ffn_line * gates_ref[1] + attn_line * gates_ref[0]
    unit_line = jnp.sum(unit_sum[...], axis=0, keepdims=True) / unit_gate_ref[...]
    for i in range(units // width):
        small_ref[5 + i : 6 + i, :] = unit_line[:, i * width : (i + 1) * width]
    lane = lax.broadcasted_iota(jnp.int32, (1, width), 1)
    layer0 = jnp.sum(attn_line * hidden_gate, axis=1, keepdims=True)
    layer1 = jnp.sum(ffn_line * hidden_gate, axis=1, keepdims=True)
    small_ref[7:8, :] = jnp.where(lane == 128, layer0, jnp.where(lane == 129, layer1, 0.0))

    def finish(t, _):
        pltpu.make_async_copy(
            got2.at[rows(t)], student_hbm.at[rows(t)], tile_sem.at[0, t]
        ).wait()
        tile_copy(1, t).wait()
        tile_copy(2, t).wait()

    lax.fori_loop(0, tiles, finish, None)
    for n in range(units // PART):
        wide(0, n).wait()
        wide(1, n).wait()
    last.wait()


def ffn(lengths, layer_gates, norm_p, hidden_gate, unit_gate, context, w_out_t, tokens, teacher, w_in, w_fo_t):
    count, width = tokens.shape
    units, heads = w_in.shape[1], context.shape[1]
    tiles = count // TILE
    vmem, smem = pl.BlockSpec(memory_space=pltpu.VMEM), pl.BlockSpec(memory_space=pltpu.SMEM)
    anywhere = pl.BlockSpec(memory_space=pl.ANY)
    low, full = jnp.bfloat16, jnp.float32
    return pl.pallas_call(
        ffn_kernel,
        in_specs=[smem, smem] + [vmem] * 5 + [anywhere] * 4,
        out_specs=[anywhere] * 4 + [vmem],
        out_shape=[
            jax.ShapeDtypeStruct((count, width), low),
            jax.ShapeDtypeStruct((count, width), full),
            jax.ShapeDtypeStruct((count, heads), full),
            jax.ShapeDtypeStruct((width, 2 * units + heads), low),
            jax.ShapeDtypeStruct((8, width), full),
        ],
        scratch_shapes=[
            pltpu.VMEM((width, units), low),
            pltpu.VMEM((width, units), low),
            pltpu.VMEM((count, width), low),
            pltpu.VMEM((count, width), low),
            *[pltpu.VMEM((count, width), low)] * 5,
            pltpu.VMEM((count, width), full),
            pltpu.VMEM((count, 1), full),
            pltpu.VMEM((count, units), low),
            pltpu.VMEM((count, units), low),
            pltpu.VMEM((count, width), full),
            pltpu.VMEM((count, heads), full),
            *[pltpu.VMEM((width, count), low)] * 3,
            pltpu.VMEM((2, width, units), low),
            pltpu.VMEM((width, heads), low),
            pltpu.VMEM((6, 8, width), full),
            pltpu.VMEM((8, units), full),
            pltpu.SemaphoreType.DMA((4,)),
            pltpu.SemaphoreType.DMA((3, tiles)),
            pltpu.SemaphoreType.DMA((3, units // PART)),
            pltpu.SemaphoreType.DMA((3, tiles)),
            pltpu.SemaphoreType.DMA((3, tiles)),
        ],
        compiler_params=pltpu.CompilerParams(
            collective_id=4, has_side_effects=True, vmem_limit_bytes=60 << 20
        ),
        name="ffn",
    )(lengths, layer_gates, norm_p, hidden_gate[None, :], unit_gate[None, :], context, w_out_t, tokens, teacher, w_in, w_fo_t)


def lamb_moments(master, first, second, grad, decay):
    new_first = MOMENT_DECAY * first + (1.0 - MOMENT_DECAY) * grad
    new_second = MOMENT_DECAY * second + (1.0 - MOMENT_DECAY) * grad * grad
    correction = 1.0 - MOMENT_DECAY**STEP_COUNT
    update = (
        new_first / correction / (jnp.sqrt(new_second / correction) + LAMB_EPS) + decay * master
    )
    return (new_first, new_second, update)


BLOCK = 384
DEPTH = (1, 3, 2, 0)


def layer_kernel(
    lengths_ref,
    gates_ref,
    head_gate_ref,
    hidden_gate_ref,
    unit_gate_ref,
    *refs,
):
    masters, norms_refs, moments_hbm, refs = refs[:4], refs[4:7], refs[7:15], refs[15:]
    (
        tokens_hbm,
        teacher_hbm,
        student_hbm,
        grad_tokens_hbm,
        sums_ref,
        small_out,
        norm_out,
        total_out,
        w,
        w_norm,
        tokens,
        qkv,
        d_mix,
        context,
        stats,
        left_t,
        hidden_t,
        own1,
        got1,
        own2,
        got2,
        got3,
        normal1,
        scale1,
        gated,
        slope,
        d_res,
        keep,
        gains,
        sums,
        unit_sum,
        heads,
        small_plane,
        small_line,
        norm_plane,
        norm_line,
        gate_row,
        unit_row,
        norm_pad,
        fo_copy,
        load_sem,
        tile_sem,
        all_send,
        all_recv,
        swap_send,
        swap_recv,
        send_sem,
        recv_sem,
        small_send,
        small_recv,
        stash_sem,
        moment_sem,
        free1,
        free2,
        free3,
    ) = refs
    me, core = lax.axis_index("dp"), lax.axis_index("head")
    z, y, x = place(me)
    rows, blocks = sums_ref.shape[0], sums_ref.shape[1] // BLOCK
    count, width = tokens.shape
    tiles, tall = count // TILE, count // ROW
    units, own_width = unit_gate_ref.shape[0], masters[1].shape[1]
    lane = lax.broadcasted_iota(jnp.int32, (1, own_width), 1)
    gate_lanes = jnp.zeros((1, own_width), jnp.float32)
    for head in range(own_width // HEAD_DIM):
        gate_lanes = jnp.where(lane // HEAD_DIM == head, head_gate_ref[head], gate_lanes)
    gate_row[...] = gate_lanes
    unit_row[...] = unit_gate_ref[...].reshape(1, units)
    pairs = own_width // PAIR
    at_out, at_in = 3 * own_width, 4 * own_width
    at_fo = at_in + units

    def load(which, t):
        source = (tokens_hbm, teacher_hbm)[which % 2]
        return pltpu.make_async_copy(
            source.at[tile(t)], tokens.at[tile(t)], load_sem.at[which, t]
        )

    def tile(t):
        return pl.ds(pl.multiple_of(t * TILE, TILE), TILE)

    def tall_row(r):
        return pl.ds(pl.multiple_of(r * ROW, ROW), ROW)

    def each(action, begin, end):
        lax.fori_loop(begin, end, lambda i, _: action(i), None)

    each(lambda t: load(0, t).start(), 0, tiles)

    line_peers = [(index(lax.rem(z + d, NZ), y, x), core) for d in (1, 2, 3)]
    plane = [index(z, y + (1 - 2 * y) * (d // 2), x + (1 - 2 * x) * (d % 2)) for d in range(4)]
    ring = [(plane[1], core), (plane[2], core), *line_peers]
    sibling = (me, 1 - core)
    greet([(p, core) for p in plane[1:]] + [(p, 1 - core) for p in plane] + line_peers)

    def rows_of(device):
        return pl.ds(pl.multiple_of(device * rows, rows), rows)

    def columns(c):
        start = c * BLOCK
        return pl.ds(start if isinstance(c, int) else pl.multiple_of(start, BLOCK), BLOCK)

    def turned(odd, rz, ra, rb):
        flip_x = ra * (1 - odd) + rb * odd
        flip_y = rb * (1 - odd) + ra * odd
        return index(lax.rem(z + rz, NZ), y + (1 - 2 * y) * flip_y, x + (1 - 2 * x) * flip_x)

    def view(c, device):
        if isinstance(c, int) and c == blocks:
            return w_norm.at[rows_of(device)]
        return w.at[rows_of(device), columns(c)]

    def move(c, place_of, to, there, k):
        block = view(c, turned(c % 2, *place_of))
        return pltpu.make_async_remote_copy(
            src_ref=block,
            dst_ref=block,
            send_sem=all_send.at[c, k],
            recv_sem=all_recv.at[c, there],
            device_id=(to, core),
            device_id_type=MESH,
        )

    def near(c):
        return turned(c % 2, 0, 1, 0)

    def far(c):
        return turned(c % 2, 0, 0, 1)

    def arrived(c, rz, ra, rb):
        move(c, (rz, ra, rb), me, slot(rz, ra, rb), 0).wait_recv()

    def all_first(c):
        for i, dz in enumerate((1, 3, 2)):
            move(c, (0, 0, 0), line_peers[dz - 1][0], slot(NZ - dz, 0, 0), i).start()
        move(c, (0, 0, 0), near(c), slot(0, 1, 0), 3).start()
        move(c, (0, 0, 0), far(c), slot(0, 0, 1), 7).start()

    def all_second(c):
        for i, rz in enumerate((1, 3, 2)):
            arrived(c, rz, 0, 0)
            move(c, (rz, 0, 0), near(c), slot(rz, 1, 0), 4 + i).start()
            move(c, (rz, 0, 0), far(c), slot(rz, 0, 1), 8 + i).start()

    def all_third(c):
        for i, rz in enumerate((0, 1, 3, 2)):
            arrived(c, rz, 1, 0)
            move(c, (rz, 1, 0), far(c), slot(rz, 1, 1), 11 + i).start()

    def all_turn(c):
        arrived(c, 0, 1, 0)
        for i, dz in enumerate((1, 3, 2)):
            move(c, (0, 1, 0), line_peers[dz - 1][0], slot(NZ - dz, 1, 0), 4 + i).start()
        move(c, (0, 1, 0), far(c), slot(0, 1, 1), 11).start()

    def all_lined(c, ra):
        for i, rz in enumerate((1, 3, 2)):
            arrived(c, rz, ra, 0)
            move(c, (rz, ra, 0), far(c), slot(rz, ra, 1), 8 + 4 * ra + i).start()

    def all_own_line(c):
        all_lined(c, 0)

    def all_near_line(c):
        all_lined(c, 1)

    def all_last(c):
        for ra in (0, 1):
            for rz in range(NZ):
                arrived(c, rz, ra, 1)

    def all_sent(c):
        for k in range(15):
            move(c, (0, 0, 0), me, 0, k).wait_send()

    mine = rows_of(me)
    for pair in range(pairs):
        for part in range(3):
            lanes = slice((3 * pair + part) * PAIR, (3 * pair + part + 1) * PAIR)
            w[mine, lanes] = masters[0][part, :, pair * PAIR : (pair + 1) * PAIR].astype(jnp.bfloat16)
    norm_pad[...] = jnp.zeros_like(norm_pad)
    norm_pad[0:4, 0:rows] = norms_refs[0][...]
    w_norm[mine] = jnp.transpose(norm_pad[...])[:rows].astype(jnp.bfloat16)
    w[mine, at_out:at_in] = masters[1][...].astype(jnp.bfloat16)
    each(all_first, 0, 2)
    all_first(blocks)
    w[mine, at_in:at_fo] = masters[2][...].astype(jnp.bfloat16)
    w[mine, at_fo:] = masters[3][...].astype(jnp.bfloat16)
    each(all_first, 2, blocks)
    sums[...] = jnp.zeros_like(sums)
    heads[...] = jnp.zeros_like(heads)

    def two(action, p):
        each(action, 2 * p, 2 * p + 2)

    two(all_second, 0)
    all_second(blocks)
    two(all_second, 1)
    two(all_third, 0)
    all_third(blocks)
    two(all_turn, 4)
    two(all_turn, 5)
    each(lambda t: load(0, t).wait(), 0, tiles)

    def pair_lanes(pair):
        return pl.ds(pl.multiple_of(pair * PAIR, PAIR), PAIR)

    def attend(pair, _):
        all_last(pair)
        span = pl.multiple_of(pair * BLOCK, BLOCK)

        def row(r, _):
            here = tall_row(r)
            same = segments(lengths_ref, r, (ROW, 1), 0) == segments(lengths_ref, r, (1, ROW), 1)
            part = mul(tokens[here], w[:, pl.ds(span, BLOCK)]).astype(jnp.bfloat16)
            qkv[here, pl.ds(span, BLOCK)] = part
            mix, totals = attend_pair(
                same, *(part[:, i * PAIR : (i + 1) * PAIR] for i in range(3))
            )
            for head in (0, 1):
                stats[r, pair, head : head + 1, :] = totals[head]
            lanes = pair_lanes(pair)
            context[here, lanes] = (mix * gate_row[:, lanes]).astype(jnp.bfloat16)

            @pl.when((r == 1) & (pair < 2))
            def _():
                two(all_second, 2 + pair)
                two(all_third, 1 + pair)

            @pl.when((r == 1) & (pair == 2))
            def _():
                two(all_own_line, 4)
                two(all_third, 3)

        lax.fori_loop(0, tall, row, None)

    lax.fori_loop(0, pairs, attend, None)
    two(all_own_line, 5)
    all_last(3)

    def swap(step, t):
        source, target = ((own1, got1), (own2, got2), (own2, got3), (own2, got3))[step]
        return pltpu.make_async_remote_copy(
            src_ref=source.at[tile(t)],
            dst_ref=target.at[tile(t)],
            send_sem=swap_send.at[step, t],
            recv_sem=swap_recv.at[step, t],
            device_id=sibling,
            device_id_type=MESH,
        )

    def phase1(t, _):
        part = mul(context[tile(t)], w[:, at_out:at_in], NT)
        own1[tile(t)] = part.astype(jnp.bfloat16)
        swap(0, t).start()

    lax.fori_loop(0, tiles, phase1, None)
    all_last(blocks)
    gains[...] = jnp.transpose(w_norm[...].astype(jnp.float32))[:8]
    gain1, bias1, gain2, bias2 = (gains[i : i + 1, :] for i in range(4))
    hidden_gate = hidden_gate_ref[...].reshape(1, width)
    gate0, gate1 = hidden_gate * gates_ref[0], hidden_gate * gates_ref[1]
    each(all_last, 4, 8)

    def summed(source, target, t):
        return source[tile(t)].astype(jnp.float32) + target[tile(t)].astype(jnp.float32)

    def part_lanes(n):
        return slice(n * PART, (n + 1) * PART)

    def phase2(t, _):
        swap(0, t).wait()
        rows_in = tokens[tile(t)].astype(jnp.float32) + summed(own1, got1, t) * gate0
        load(1, t).start()
        normal, scale = normalize(rows_in)
        normal1[tile(t)] = normal
        scale1[tile(t)] = scale
        hidden = normal * gain1 + bias1
        low = hidden.astype(jnp.bfloat16)
        hidden_t[:, tile(t)] = jnp.transpose(hidden).astype(jnp.bfloat16)
        for n in range(units // PART):
            up = mul(low, w[:, at_in + n * PART : at_in + (n + 1) * PART])
            below, density = normal_parts(up)
            gate = unit_row[:, part_lanes(n)]
            gated[tile(t), part_lanes(n)] = (up * below * gate).astype(jnp.bfloat16)
            slope[tile(t), part_lanes(n)] = ((below + density) * gate).astype(jnp.bfloat16)

        @pl.when(t == 1)
        def _():
            two(all_near_line, 4)

        @pl.when(t == 3)
        def _():
            two(all_near_line, 5)

    lax.fori_loop(0, tiles, phase2, None)
    each(all_sent, 0, 8)
    all_sent(blocks)
    each(all_last, 8, blocks)
    stash_fo = pltpu.make_async_copy(w.at[:, at_fo:], fo_copy, stash_sem.at[2])
    stash_fo.start()

    def down(t, _):
        part = mul(gated[tile(t)], w[:, at_fo:], NT)
        own2[tile(t)] = part.astype(jnp.bfloat16)
        swap(1, t).start()

    lax.fori_loop(0, tiles, down, None)
    each(all_sent, 8, blocks)

    def student_out(t):
        return pltpu.make_async_copy(
            got2.at[tile(t)], student_hbm.at[tile(t)], tile_sem.at[0, t]
        )

    def phase3(t, _):
        swap(1, t).wait()
        load(1, t).wait()
        ffn = summed(own2, got2, t)
        hidden = normal1[tile(t)] * gain1 + bias1
        normal, scale = normalize(hidden + ffn * gate1)
        student = normal * gain2 + bias2
        got2[tile(t)] = student.astype(jnp.bfloat16)
        student_out(t).start()
        row = t // (ROW // TILE)
        end = lengths_ref[row, 0]
        for k in range(1, lengths_ref.shape[1]):
            end = end + lengths_ref[row, k]
        position = lax.broadcasted_iota(jnp.int32, (TILE, 1), 0) + (t % (ROW // TILE)) * TILE
        valid = (position < end).astype(jnp.float32)
        d_out = valid * (student - tokens[tile(t)].astype(jnp.float32))
        load(2, t).start()
        d_res2 = norm_back(d_out, normal, scale, gain2)
        d_res[tile(t)] = d_res2
        sums[2] += fold(d_out * normal)
        sums[3] += fold(d_out)
        sums[5] += fold(d_res2 * ffn)
        d_ffn = d_res2 * gate1
        left_t[:, tile(t)] = jnp.transpose(d_ffn).astype(jnp.bfloat16)

    lax.fori_loop(0, tiles, phase3, None)

    late_fo = at_fo // BLOCK
    grid_w = w.reshape(NZ, NY, NX, rows, w.shape[1])

    def landing(c, stage, i=0):
        buffer, n = (got2, c - late_fo) if c >= late_fo else (gated, c)
        across = buffer.shape[1] // BLOCK
        if stage == 1:
            view = buffer.reshape(4, NZ, 2, rows, buffer.shape[1])
            return view.at[n // across, :, :, :, pl.ds(n % across * BLOCK, BLOCK)]
        if stage == 2:
            view = buffer.reshape(8, NZ, rows, buffer.shape[1])
            return view.at[4 + n // across, :, :, pl.ds(n % across * BLOCK, BLOCK)]
        at = 24 * across + 3 * n + i
        view = buffer.reshape(32, rows, buffer.shape[1])
        return view.at[at // across, :, pl.ds(at % across * BLOCK, BLOCK)]

    def remote(source, target, c, k, to):
        return pltpu.make_async_remote_copy(
            src_ref=source,
            dst_ref=target,
            send_sem=send_sem.at[c, k],
            recv_sem=recv_sem.at[c, k],
            device_id=(to, core),
            device_id_type=MESH,
        )

    def half(c, other):
        if c % 2:
            return grid_w.at[:, :, 1 - x if other else x, :, columns(c)]
        return grid_w.at[:, 1 - y if other else y, :, :, columns(c)]

    def quarter(c, other):
        if c % 2:
            return grid_w.at[:, 1 - y if other else y, x, :, columns(c)]
        return grid_w.at[:, y, 1 - x if other else x, :, columns(c)]

    def side(c, other):
        mine_at = y if c % 2 else x
        return 1 - mine_at if other else mine_at

    def leg1(c):
        return remote(half(c, True), landing(c, 1), c, 0, far(c))

    def leg2(c):
        return remote(quarter(c, True), landing(c, 2), c, 1, near(c))

    def leg3(c, rz):
        source = grid_w.at[lax.rem(z + rz, NZ), y, x, :, columns(c)]
        there = NZ - rz
        return remote(source, landing(c, 3, there - 1), c, 1 + there, line_peers[rz - 1][0])

    def first(c):
        leg1(c).start()

    def second(c):
        leg1(c).wait_recv()
        came = landing(c, 1)
        block = quarter(c, True)
        total = block[...].astype(jnp.float32) + came[:, side(c, True)].astype(jnp.float32)
        block[...] = total.astype(jnp.bfloat16)
        leg2(c).start()
        block = quarter(c, False)
        total = block[...].astype(jnp.float32) + came[:, side(c, False)].astype(jnp.float32)
        keep[c % 8] = total

    def third(c):
        leg2(c).wait_recv()
        total = keep[c % 8] + landing(c, 2)[...].astype(jnp.float32)
        keep[c % 8] = total
        quarter(c, False)[...] = total.astype(jnp.bfloat16)
        for rz in (1, 3, 2):
            leg3(c, rz).start()

    def last(c):
        for rz in (1, 2, 3):
            leg3(c, rz).wait_recv()
        total = keep[c % 8, z]
        for i in range(3):
            total = total + landing(c, 3, i)[...].astype(jnp.float32)
        sums_ref[:, columns(c)] = total

    def down_from(action, i, n):
        for j in range(i, i + n):
            action(blocks - 1 - j)

    def weigh(left, right, start, size):
        for n in range(size // BLOCK):
            lanes = slice(start + n * BLOCK, start + (n + 1) * BLOCK)
            w[:, lanes] = mul(left[...], right[:, n * BLOCK : (n + 1) * BLOCK]).astype(jnp.bfloat16)

    def ready(semaphore, peers):
        for peer in peers:
            pl.semaphore_signal(semaphore, inc=1, device_id=peer, device_id_type=MESH)
        pl.semaphore_wait(semaphore, len(peers))

    each(lambda t: student_out(t).wait(), 0, tiles)
    stash_fo.wait()
    ready(free1, ring)
    for n in range(units // BLOCK - 1, -1, -1):
        lanes = slice(n * BLOCK, (n + 1) * BLOCK)
        grad = mul(left_t[...], gated[:, lanes])
        w[:, at_fo + n * BLOCK : at_fo + (n + 1) * BLOCK] = grad.astype(jnp.bfloat16)
        unit_sum[:, lanes] = fold(grad * fo_copy[:, lanes].astype(jnp.float32))
        first(late_fo + n)

    def phase3_units(t, _):
        d_ffn = (d_res[tile(t)] * gate1).astype(jnp.bfloat16)
        for n in range(units // PART):
            d_gated = mul(d_ffn, fo_copy[:, part_lanes(n)])
            d_up = d_gated * slope[tile(t), part_lanes(n)].astype(jnp.float32)
            slope[tile(t), part_lanes(n)] = d_up.astype(jnp.bfloat16)
        part = mul(slope[tile(t)], w[:, at_in:at_fo], NT)
        own2[tile(t)] = part.astype(jnp.bfloat16)
        swap(2, t).start()

        @pl.when(t == 3)
        def _():
            down_from(second, 0, 2)

    lax.fori_loop(0, tiles, phase3_units, None)
    down_from(second, 2, 2)
    ready(free2, ring)
    down_from(third, 0, 2)
    for n in range(units // BLOCK - 1, -1, -1):
        weigh(hidden_t, slope.at[:, n * BLOCK : (n + 1) * BLOCK], at_in + n * BLOCK, BLOCK)
        first(at_in // BLOCK + n)

    def moment(i, p, n):
        band = (8 * i + (0, 3, 4, 6)[p] + n) * rows
        return normal1.at[band : band + rows, : own_width if p < 2 else width]

    def moment_pieces(i):
        qkv_m, out_m, in_m, fo_m = moments_hbm[4 * i : 4 * i + 4]
        found = [(0, n, qkv_m.at[n]) for n in range(3)] + [(1, 0, out_m)]
        for p, array in ((2, in_m), (3, fo_m)):
            found += [(p, n, array.at[:, n * width : (n + 1) * width]) for n in range(2)]
        return found

    def phase4(t, _):
        swap(2, t).wait()
        normal = normal1[tile(t)]
        d_hidden = d_res[tile(t)] + summed(own2, got3, t)
        sums[0] += fold(d_hidden * normal)
        sums[1] += fold(d_hidden)
        d_res1 = norm_back(d_hidden, normal, scale1[tile(t)], gain1)
        d_res[tile(t)] = d_res1
        sums[4] += fold(d_res1 * summed(own1, got1, t))
        d_attn = d_res1 * gate0
        left_t[:, tile(t)] = jnp.transpose(d_attn).astype(jnp.bfloat16)
        d_context = mul(d_attn.astype(jnp.bfloat16), w[:, at_out:at_in])
        d_mix[tile(t)] = (d_context * gate_row[...]).astype(jnp.bfloat16)
        load(2, t).wait()
        hidden_t[:, tile(t)] = jnp.transpose(tokens[tile(t)].astype(jnp.float32)).astype(jnp.bfloat16)

    lax.fori_loop(0, tiles, phase4, None)
    pl.semaphore_signal(free3, inc=1, device_id=sibling, device_id_type=MESH)
    stash = [
        pltpu.make_async_copy(
            w.at[:, i * width : min((i + 1) * width, at_out)],
            own1.at[i * width : (i + 1) * width, : min((i + 1) * width, at_out) - i * width],
            stash_sem.at[i],
        )
        for i in range(2)
    ]
    for one in stash:
        one.start()
    moment_loads = [
        pltpu.make_async_copy(source, moment(i, p, n), moment_sem.at[i, at])
        for i in range(2)
        for at, (p, n, source) in enumerate(moment_pieces(i))
    ]
    for one in moment_loads:
        one.start()
    weigh(left_t, context, at_out, own_width)
    first(at_out // BLOCK)
    down_from(third, 2, 2)
    down_from(last, 0, 2)
    down_from(second, 4, 2)

    def pair_back(j, _):
        pair = pairs - 1 - j
        span = pl.multiple_of(pair * BLOCK, BLOCK)
        gate = gate_row[:, pl.ds(pl.multiple_of(pair * PAIR, PAIR), PAIR)]

        def row_back(r, _):
            here = tall_row(r)
            same = segments(lengths_ref, r, (ROW, 1), 0) == segments(lengths_ref, r, (1, ROW), 1)
            spans = [pl.ds(pl.multiple_of(span + i * PAIR, PAIR), PAIR) for i in range(3)]
            parts, weighed = attend_back(
                same,
                *(qkv[here, lanes] for lanes in spans),
                stats[r, pair],
                d_mix[here, pl.ds(pl.multiple_of(pair * PAIR, PAIR), PAIR)],
            )
            lane = lax.broadcasted_iota(jnp.int32, heads.shape, 1)
            for head in (0, 1):
                value = weighed[head] / gate[:, head * HEAD_DIM : head * HEAD_DIM + 1]
                heads[...] += jnp.where(lane == 2 * pair + head, value, 0.0)
            for lanes, value in zip(spans, parts, strict=True):
                qkv[here, lanes] = value.astype(jnp.bfloat16)

            @pl.when((r == 1) & (j == 1))
            def _():
                down_from(second, 6, 2)

            @pl.when((r == 1) & (j == 2))
            def _():
                down_from(second, 8, 1)

        lax.fori_loop(0, tall, row_back, None)

        @pl.when(j == 0)
        def _():
            for one in stash:
                one.wait()

        w[:, pl.ds(span, BLOCK)] = mul(hidden_t[...], qkv[:, pl.ds(span, BLOCK)]).astype(jnp.bfloat16)
        for c in range(pairs):

            @pl.when(pair == c)
            def _(c=c):
                first(c)

        @pl.when(j == 0)
        def _():
            down_from(last, 2, 2)
            down_from(third, 4, 2)

        @pl.when(j == 1)
        def _():
            down_from(third, 6, 2)
            down_from(last, 4, 2)

    lax.fori_loop(0, pairs, pair_back, None)

    def tokens_out(t):
        return pltpu.make_async_copy(
            d_res.at[tile(t)], grad_tokens_hbm.at[tile(t)], tile_sem.at[1, t]
        )

    def share(t, _):
        part = mul(qkv[tile(t), :width], own1[:width], NT)
        part = part + mul(qkv[tile(t), width:], own1[width:, : at_out - width], NT)
        own2[tile(t)] = part.astype(jnp.bfloat16)
        swap(3, t).start()

    pl.semaphore_wait(free3, 1)
    lax.fori_loop(0, tiles, share, None)

    here_plane = y * NX + x

    def line_of(i):
        return jnp.sum(sums[i], axis=0, keepdims=True)

    for i in range(4):
        small_plane[here_plane, i : i + 1, :] = line_of(i)
    attn_line, ffn_line = line_of(4), line_of(5)
    small_plane[here_plane, 4:5, :] = ffn_line * gates_ref[1] + attn_line * gates_ref[0]
    unit_line = jnp.sum(unit_sum[...], axis=0, keepdims=True) / unit_row[...]
    for i in range(units // width):
        small_plane[here_plane, 5 + i : 6 + i, :] = unit_line[:, i * width : (i + 1) * width]
    lane = lax.broadcasted_iota(jnp.int32, (1, width), 1)
    layer0 = jnp.sum(attn_line * hidden_gate, axis=1, keepdims=True)
    layer1 = jnp.sum(ffn_line * hidden_gate, axis=1, keepdims=True)
    pair_line = jnp.where(lane == 128, layer0, jnp.where(lane == 129, layer1, 0.0))
    small_plane[here_plane, 7:8, :] = pair_line
    small_plane[here_plane, 7:8, :128] = heads[0:1]

    def spread(buffer, base, targets, at):
        copies = [
            pltpu.make_async_remote_copy(
                src_ref=buffer.at[at],
                dst_ref=buffer.at[at],
                send_sem=small_send.at[base + i],
                recv_sem=small_recv.at[base + i],
                device_id=to,
                device_id_type=MESH,
            )
            for i, to in enumerate(targets)
        ]
        for one in copies:
            one.start()
        return copies

    def added(buffer, copies):
        for one in copies:
            one.wait_recv()
        total = buffer[0]
        for at in range(1, buffer.shape[0]):
            total = total + buffer[at]
        return total

    sent1 = spread(small_plane, 0, [(p, core) for p in plane[1:]], here_plane)
    down_from(second, 9, 2)
    down_from(third, 8, 1)

    def finish(t, _):
        swap(3, t).wait()
        d_res[tile(t)] += summed(own2, got3, t)
        tokens_out(t).start()

    lax.fori_loop(0, tiles, finish, None)
    small_line[z] = added(small_plane, sent1)
    sent2 = spread(small_line, 3, line_peers, z)
    down_from(last, 6, 2)
    down_from(second, 11, 1)
    down_from(third, 9, 2)
    total = added(small_line, sent2)
    small_out[...] = total
    norm_grad = pltpu.roll(total, (width - me * rows) % width, 1)[:, :128]
    norm_out[...] = norm_grad
    down_from(third, 11, 1)

    row8 = lax.broadcasted_iota(jnp.int32, (8, 128), 0)
    lane8 = lax.broadcasted_iota(jnp.int32, (8, 128), 1)

    def put(tile8, row, weight, update):
        here = row8 == row
        return jnp.where(here & (lane8 == 0), weight, jnp.where(here & (lane8 == 1), update, tile8))

    def square(block):
        return jnp.sum(jnp.sum(block * block, axis=0, keepdims=True), axis=1, keepdims=True)

    tile8 = jnp.zeros((8, 128), jnp.float32)
    master, first_moment, second_moment = (ref[...] for ref in norms_refs)
    update = lamb_moments(master, first_moment, second_moment, norm_grad[:4, : master.shape[1]], 0.0)[2]
    for i in range(4):
        tile8 = put(tile8, 4 + i, 0.5 * square(master[i : i + 1]), 0.5 * square(update[i : i + 1]))

    def squares(p, n, lanes, start):
        master = masters[0][n, :, lanes] if p == 0 else masters[p][:, lanes]
        first_moment, second_moment = (
            moment(i, p, n)[...] if p else moment(i, p, n)[:, lanes] for i in range(2)
        )
        grad = sums_ref[:, start : start + master.shape[1]]
        update = lamb_moments(master, first_moment, second_moment, grad, WEIGHT_DECAY)[2]
        return square(master), square(update)

    def matrix(tile8, p, start):
        size = masters[p].shape[1]
        weights, updates = 0.0, 0.0
        for n in range(max(size // width, 1)):
            step = min(size, width)
            found = squares(p, n, slice(n * step, (n + 1) * step), start + n * step)
            weights, updates = weights + found[0], updates + found[1]
        return put(tile8, p, weights, updates)

    for one in moment_loads:
        one.wait()
    tile8 = matrix(matrix(tile8, 3, at_fo), 2, at_in)
    down_from(last, 8, 1)
    tile8 = matrix(tile8, 1, at_out)
    weights, updates = 0.0, 0.0
    for pair in range(pairs - 1, -1, -1):
        down_from(last, blocks - 1 - pair, 1)
        for part in range(3):
            lanes = slice(pair * PAIR, (pair + 1) * PAIR)
            found = squares(0, part, lanes, (3 * pair + part) * PAIR)
            weights, updates = weights + found[0], updates + found[1]
    tile8 = put(tile8, 0, weights, updates)
    here_cores = core * (NX * NY) + here_plane
    norm_plane[here_cores] = tile8
    targets = [(p, core) for p in plane[1:]] + [(p, 1 - core) for p in plane]
    sent3 = spread(norm_plane, 6, targets, here_cores)
    for c in range(blocks):
        leg1(c).wait_send()
        leg2(c).wait_send()
        for rz in (1, 2, 3):
            leg3(c, rz).wait_send()
    each(lambda t: tokens_out(t).wait(), 0, tiles)
    norm_line[z] = added(norm_plane, sent3)
    sent4 = spread(norm_line, 13, line_peers, z)
    total_out[...] = added(norm_line, sent4)
    for one in (*sent1, *sent2, *sent3, *sent4):
        one.wait_send()


def layer(lengths, layer_gates, head_gate, hidden_gate, unit_gate, norms, params, tokens, teacher):
    count, width = tokens.shape
    (rows, own_width), units = params[1].shape, unit_gate.shape[0]
    total = 4 * own_width + 2 * units
    tiles, tall, blocks = count // TILE, count // ROW, total // BLOCK
    vmem, smem = pl.BlockSpec(memory_space=pltpu.VMEM), pl.BlockSpec(memory_space=pltpu.SMEM)
    anywhere = pl.BlockSpec(memory_space=pl.ANY)
    low, full = jnp.bfloat16, jnp.float32
    return pl.pallas_call(
        layer_kernel,
        in_specs=[smem] * 3 + [vmem] * 9 + [anywhere] * 10,
        out_specs=[anywhere] * 2 + [vmem] * 4,
        out_shape=[
            jax.ShapeDtypeStruct((count, width), low),
            jax.ShapeDtypeStruct((count, width), full),
            jax.ShapeDtypeStruct((rows, total), full),
            jax.ShapeDtypeStruct((8, width), full),
            jax.ShapeDtypeStruct((8, 128), full),
            jax.ShapeDtypeStruct((8, 128), full),
        ],
        scratch_shapes=[
            pltpu.VMEM((width, total), low),
            pltpu.VMEM((width, 128), low),
            pltpu.VMEM((count, width), low),
            pltpu.VMEM((count, 3 * own_width), low),
            pltpu.VMEM((count, own_width), low),
            pltpu.VMEM((count, own_width), low),
            pltpu.VMEM((tall, own_width // PAIR, 8, ROW), full),
            pltpu.VMEM((width, count), low),
            pltpu.VMEM((width, count), low),
            *[pltpu.VMEM((count, width), low)] * 5,
            pltpu.VMEM((count, width), full),
            pltpu.VMEM((count, 1), full),
            pltpu.VMEM((count, units), low),
            pltpu.VMEM((count, units), low),
            pltpu.VMEM((count, width), full),
            pltpu.VMEM((8, NZ, rows, BLOCK), full),
            pltpu.VMEM((8, width), full),
            pltpu.VMEM((6, 8, width), full),
            pltpu.VMEM((8, units), full),
            pltpu.VMEM((8, 128), full),
            pltpu.VMEM((NX * NY, 8, width), full),
            pltpu.VMEM((NZ, 8, width), full),
            pltpu.VMEM((2 * NX * NY, 8, 128), full),
            pltpu.VMEM((NZ, 8, 128), full),
            pltpu.VMEM((1, own_width), full),
            pltpu.VMEM((1, units), full),
            pltpu.VMEM((128, 128), full),
            pltpu.VMEM((width, units), low),
            pltpu.SemaphoreType.DMA((3, tiles)),
            pltpu.SemaphoreType.DMA((2, tiles)),
            pltpu.SemaphoreType.DMA((blocks + 1, 15)),
            pltpu.SemaphoreType.DMA((blocks + 1, 16)),
            pltpu.SemaphoreType.DMA((4, tiles)),
            pltpu.SemaphoreType.DMA((4, tiles)),
            pltpu.SemaphoreType.DMA((blocks, 5)),
            pltpu.SemaphoreType.DMA((blocks, 5)),
            pltpu.SemaphoreType.DMA((16,)),
            pltpu.SemaphoreType.DMA((16,)),
            pltpu.SemaphoreType.DMA((3,)),
            pltpu.SemaphoreType.DMA((2, 8)),
            pltpu.SemaphoreType.REGULAR,
            pltpu.SemaphoreType.REGULAR,
            pltpu.SemaphoreType.REGULAR,
        ],
        compiler_params=pltpu.CompilerParams(
            collective_id=0, has_side_effects=True, vmem_limit_bytes=62 << 20
        ),
        name="layer",
    )(lengths, layer_gates, head_gate, hidden_gate, unit_gate, *params[:4], *norms, *params[4:], tokens, teacher)


PIECES = 4


def spans(shape):
    if len(shape) == 2:
        return [(slice(None), slice(None))]
    pairs = shape[2] // PAIR
    return [
        (part, slice(None), slice(pair * PAIR, (pair + 1) * PAIR))
        for pair in range(pairs)
        for part in range(3)
    ]


def update_kernel(count, small_ref, norm_ref, total_ref, *refs):
    norms_refs, refs = refs[:3], refs[3:]
    passed_in, sums_hbm, params_hbm, refs = refs[:count], refs[count], refs[count + 1 : count + 13], refs[count + 13 :]
    passed_out, made_hbm, refs = refs[:count], refs[count : count + 20], refs[count + 20 :]
    small_outs, refs = refs[:10], refs[10:]
    sums_ref, params, outs = refs[0], refs[1:13], refs[13:33]
    held, refs = refs[33 : 33 + count], refs[33 + count :]
    pass_in, pass_out, in_sem, out_sem = refs
    pieces = [
        (i, n, pl.ds(n * (a.shape[0] // PIECES), a.shape[0] // PIECES))
        for n in range(PIECES)
        for i, a in enumerate(held)
    ]
    passes_in = [
        pltpu.make_async_copy(passed_in[i].at[at], held[i].at[at], pass_in.at[i, n])
        for i, n, at in pieces
    ]
    passes_out = [
        pltpu.make_async_copy(held[i].at[at], passed_out[i].at[at], pass_out.at[i, n])
        for i, n, at in pieces
    ]
    loads = [
        pltpu.make_async_copy(source, target, in_sem.at[i])
        for i, (source, target) in enumerate(
            zip((*params_hbm, sums_hbm), (*params, sums_ref), strict=True)
        )
    ]
    stores = [
        pltpu.make_async_copy(source, target, out_sem.at[i])
        for i, (source, target) in enumerate(zip(outs, made_hbm, strict=True))
    ]
    loads[12].start()
    for p in range(4):
        for i in range(3):
            loads[4 * i + p].start()
    for one in passes_in:
        one.start()
    weight_norm = jnp.sqrt(total_ref[:, 0:1])
    update_norm = jnp.sqrt(total_ref[:, 1:2])
    trust = weight_norm / update_norm

    def step(row, targets, at, values, decay):
        master, first_moment, second_moment, grad = values
        new_first, new_second, update = lamb_moments(
            master, first_moment, second_moment, grad, decay
        )
        new_master = master - LEARN_RATE * trust[row] * update
        made = (grad, new_first, new_second, new_master, new_master.astype(jnp.bfloat16))
        for target, value in zip(targets, made, strict=True):
            target[at] = value

    loads[12].wait()
    start = 0
    for p in range(4):
        for i in range(3):
            loads[4 * i + p].wait()
        targets = outs[5 * p : 5 * p + 5]
        for at in spans(params[p].shape):
            width = params[p].shape[1] if len(at) == 2 else PAIR
            grad = sums_ref[:, start : start + width]
            values = (*(params[4 * i + p][at] for i in range(3)), grad)
            step(slice(p, p + 1), targets, at, values, WEIGHT_DECAY)
            start += width
        for one in stores[5 * p : 5 * p + 5]:
            one.start()
        if p == 0:
            for one, other in zip(passes_in, passes_out, strict=True):
                one.wait()
                other.start()
    norm_grad = norm_ref[:4, : norms_refs[0].shape[1]]
    values = (*(ref[...] for ref in norms_refs), norm_grad)
    step(slice(4, 8), small_outs[:5], (Ellipsis,), values, 0.0)
    stats_out, heads_out, units_out, hidden_out, layers_out = small_outs[5:]
    lane = lax.broadcasted_iota(jnp.int32, (8, 128), 1)
    stats = jnp.where(lane == 0, weight_norm, jnp.where(lane == 1, update_norm, trust))
    stats_out[...] = jnp.transpose(jnp.concatenate([stats] * 16, axis=0))[:3, :8]
    heads_out[...] = small_ref[7:8, : heads_out.shape[1]]
    width = small_ref.shape[1]
    for i in range(units_out.shape[0] // width):
        units_out[i * width : (i + 1) * width] = small_ref[5 + i : 6 + i, :].reshape(width)
    hidden_out[...] = small_ref[4:5, :].reshape(width)
    layers_out[...] = small_ref[7:8, 128:130]
    for one in (*stores, *passes_out):
        one.wait()


def update(passed, sums, small, norm_grad, totals, norms, params, sizes):
    vmem, anywhere = pl.BlockSpec(memory_space=pltpu.VMEM), pl.BlockSpec(memory_space=pltpu.HBM)
    big, little = [], []
    for master in params[:4]:
        big += [jax.ShapeDtypeStruct(master.shape, jnp.float32)] * 4
        big += [jax.ShapeDtypeStruct(master.shape, jnp.bfloat16)]
    little += [jax.ShapeDtypeStruct(norms[0].shape, jnp.float32)] * 4
    little += [jax.ShapeDtypeStruct(norms[0].shape, jnp.bfloat16)]
    little += [jax.ShapeDtypeStruct((3, 8), jnp.float32)]
    little += [jax.ShapeDtypeStruct(size, jnp.float32) for size in sizes]
    through = [jax.ShapeDtypeStruct(a.shape, a.dtype) for a in passed]
    made = pl.pallas_call(
        functools.partial(update_kernel, len(passed)),
        in_specs=[vmem] * 6 + [anywhere] * (len(passed) + 1 + len(params)),
        out_specs=[anywhere] * (len(passed) + len(big)) + [vmem] * len(little),
        out_shape=[*through, *big, *little],
        scratch_shapes=[
            pltpu.VMEM(sums.shape, jnp.float32),
            *[pltpu.VMEM(a.shape, a.dtype) for a in params],
            *[pltpu.VMEM(a.shape, a.dtype) for a in big],
            *[pltpu.VMEM(a.shape, a.dtype) for a in passed],
            pltpu.SemaphoreType.DMA((len(passed), PIECES)),
            pltpu.SemaphoreType.DMA((len(passed), PIECES)),
            pltpu.SemaphoreType.DMA((13,)),
            pltpu.SemaphoreType.DMA((20,)),
        ],
        compiler_params=pltpu.CompilerParams(vmem_limit_bytes=60 << 20),
        name="update",
    )(small, norm_grad, totals, *norms, *passed, sums, *params)
    return made[: len(passed)], made[len(passed) :]


def core_sum(part):
    part = part.astype(jnp.bfloat16)
    other = lax.ppermute(part, "head", [(0, 1), (1, 0)])
    return part.astype(jnp.float32) + other.astype(jnp.float32)


def plain_totals(sums, norm_grad, norms, params, head_count):
    found, start = [], 0
    for p in range(4):
        pair = jnp.zeros((2,), jnp.float32)
        for at in spans(params[p].shape):
            master, first_moment, second_moment = (params[4 * i + p][at] for i in range(3))
            grad = sums[:, start : start + master.shape[1]]
            update = lamb_moments(master, first_moment, second_moment, grad, WEIGHT_DECAY)[2]
            pair = pair + jnp.stack([jnp.sum(master * master), jnp.sum(update * update)])
            start += master.shape[1]
        found.append(pair)
    master, first_moment, second_moment = norms
    update = lamb_moments(master, first_moment, second_moment, norm_grad[:4, : master.shape[1]], 0.0)[2]
    rows = jnp.stack([jnp.sum(master * master, axis=1), jnp.sum(update * update, axis=1)], axis=1)
    found = jnp.concatenate([jnp.stack(found), rows / head_count])
    return jnp.pad(lax.psum(found, ("dp", "head")), ((0, 0), (0, 126)))


def rows_first(qkv):
    return jnp.transpose(qkv, (1, 0, 2))


def plain_layer(lengths, layer_gates, head_gate, hidden_gate, unit_gate, norms, params, tokens, teacher):
    heads_here, units = head_gate.shape[0], unit_gate.shape[0]
    rows, own_width = params[1].shape
    gate_lanes = jnp.repeat(head_gate, HEAD_DIM)[None, :]
    norm_shard = norms[0].T.astype(jnp.bfloat16)
    shards = [params[p][at] for p in range(4) for at in spans(params[p].shape)]
    shards = jnp.concatenate(shards, axis=1).astype(jnp.bfloat16)
    w, norm_t = (lax.all_gather(s, "dp", axis=0, tiled=True) for s in (shards, norm_shard))
    norm_p = norm_t.T.astype(jnp.float32)
    w_qkv, w_out_t, w_in, w_fo_t = jnp.split(
        w, (3 * own_width, 4 * own_width, 4 * own_width + units), axis=1
    )
    qkv = jnp.dot(tokens, w_qkv, preferred_element_type=jnp.float32).astype(jnp.bfloat16)
    context, stats = attention(qkv, lengths, gate_lanes)
    student, d_res1, d_context, grads, small = ffn(
        lengths,
        layer_gates,
        norm_p,
        hidden_gate,
        unit_gate,
        context,
        w_out_t,
        tokens,
        teacher,
        w_in,
        w_fo_t,
    )
    d_qkv, head_sums = attention_back(qkv, lengths, gate_lanes, stats, d_context)
    d_heads = jnp.sum(head_sums[:, :, 0, :2], axis=0).reshape(-1)
    grad_qkv = jnp.einsum("tc,tk->ck", tokens, d_qkv, preferred_element_type=jnp.float32)
    input_part = jnp.einsum("tk,ck->tc", d_qkv, w_qkv, preferred_element_type=jnp.float32)
    grad_tokens = d_res1 + core_sum(input_part)
    grad_fo, grad_in, grad_out = jnp.split(grads.astype(jnp.float32), (units, 2 * units), axis=1)
    grads = jnp.concatenate([grad_qkv, grad_out, grad_in, grad_fo], axis=1)
    sums = lax.psum_scatter(grads, "dp", scatter_dimension=0, tiled=True)
    small = lax.psum(small.at[7, :heads_here].set(d_heads), "dp")
    norm_grad = lax.dynamic_slice_in_dim(small, lax.axis_index("dp") * rows, rows, 1)
    norm_grad = jnp.pad(norm_grad, ((0, 0), (0, 128 - rows)))
    totals = plain_totals(sums, norm_grad, norms, params, lax.axis_size("head"))
    return student, grad_tokens, sums, small, norm_grad, totals


def local(
    tokens,
    teacher,
    lengths,
    head_gate,
    unit_gate,
    hidden_gate,
    layer_gates,
    master_qkv,
    first_qkv,
    second_qkv,
    master_attn_out,
    first_attn_out,
    second_attn_out,
    master_ffn_in,
    first_ffn_in,
    second_ffn_in,
    master_ffn_out,
    first_ffn_out,
    second_ffn_out,
    master_norms,
    first_norms,
    second_norms,
):
    ours = lax.axis_size("dp") == GRID and lax.axis_size("head") == 2
    params = [
        rows_first(master_qkv),
        master_attn_out.T,
        master_ffn_in,
        master_ffn_out.T,
        rows_first(first_qkv),
        first_attn_out.T,
        first_ffn_in,
        first_ffn_out.T,
        rows_first(second_qkv),
        second_attn_out.T,
        second_ffn_in,
        second_ffn_out.T,
    ]
    norms = [master_norms, first_norms, second_norms]
    run = layer if ours else plain_layer
    student, grad_tokens, sums, small, norm_grad, totals = run(
        lengths,
        layer_gates,
        head_gate,
        hidden_gate,
        unit_gate,
        norms,
        params,
        tokens,
        teacher,
    )
    sizes = ((1, head_gate.shape[0]), unit_gate.shape, hidden_gate.shape, (1, 2))
    (student, grad_tokens), made = update(
        (student, grad_tokens), sums, small, norm_grad, totals, norms, params, sizes
    )
    results = []
    for p in range(4):
        for value in made[5 * p : 5 * p + 5]:
            results.append(rows_first(value) if p == 0 else value if p == 2 else value.T)
    norm_results, (stats_rows, *gate_rows) = made[20:25], made[25:]
    gate_results = [row.reshape(-1) for row in gate_rows]
    return (
        student,
        grad_tokens,
        *gate_results,
        *results,
        *norm_results,
        stats_rows,
    )


def solution(mesh):
    return jax.shard_map(
        local,
        mesh=mesh,
        in_specs=(
            P("dp", None),
            P("dp", None),
            P("dp", None),
            P("head"),
            P("head"),
            P(),
            P(),
            P("dp", None, "head"),
            P("dp", None, "head"),
            P("dp", None, "head"),
            P("head", "dp"),
            P("head", "dp"),
            P("head", "dp"),
            P("dp", "head"),
            P("dp", "head"),
            P("dp", "head"),
            P("head", "dp"),
            P("head", "dp"),
            P("head", "dp"),
            P(None, "dp"),
            P(None, "dp"),
            P(None, "dp"),
        ),
        out_specs=(
            P("dp", None),
            P("dp", None),
            P("head"),
            P("head"),
            P(),
            P(),
            P("dp", None, "head"),
            P("dp", None, "head"),
            P("dp", None, "head"),
            P("dp", None, "head"),
            P("dp", None, "head"),
            P("head", "dp"),
            P("head", "dp"),
            P("head", "dp"),
            P("head", "dp"),
            P("head", "dp"),
            P("dp", "head"),
            P("dp", "head"),
            P("dp", "head"),
            P("dp", "head"),
            P("dp", "head"),
            P("head", "dp"),
            P("head", "dp"),
            P("head", "dp"),
            P("head", "dp"),
            P("head", "dp"),
            P(None, "dp"),
            P(None, "dp"),
            P(None, "dp"),
            P(None, "dp"),
            P(None, "dp"),
            P(),
        ),
        check_vma=False,
    )
```
